32 devices in a mesh: seq: 8 (over z, y), head: 4 (over x, core).
Axes of the slice: x: 2, y: 2, z: 4, core: 2. Of those that a mesh axis runs over, the one named last changes fastest.
Arguments:
- tokens: bfloat16 [64, 512, 1024], P('seq', 'head'), may hold values from -6 to 6
- cotangent: bfloat16 [64, 512, 1024], P('seq', 'head'), may hold values from -6 to 6
- lengths: int32 [64], replicated, may hold values from 64 to 512, as said below
- seq_order: int32 [64], replicated, may hold values from 0 to 63, as said below
- w_qkv: bfloat16 [1024, 3072], P('head'), may hold values from -0.1875 to 0.1875
- w_out: bfloat16 [1024, 1024], P('head'), may hold values from -1.5 to 1.5
- w_up: bfloat16 [1024, 4096], P('head'), may hold values from -0.1875 to 0.1875
- w_down: bfloat16 [4096, 1024], P('head'), may hold values from -0.09375 to 0.09375
- bias_q: bfloat16 [1024], P('head'), may hold values from -3 to 3
- bias_v: bfloat16 [1024], P('head'), may hold values from -3 to 3
- bias_out: bfloat16 [1024], P('head'), may hold values from -3 to 3
- bias_up: bfloat16 [4096], P('head'), may hold values from -3 to 3
- bias_down: bfloat16 [1024], P('head'), may hold values from -3 to 3
- gain_attn: bfloat16 [1024], P('head'), may hold values from 0.25 to 1.75
- shift_attn: bfloat16 [1024], P('head'), may hold values from -3 to 3
- gain_mlp: bfloat16 [1024], P('head'), may hold values from 0.25 to 1.75
- shift_mlp: bfloat16 [1024], P('head'), may hold values from -3 to 3
Outputs:
- activations: bfloat16 [64, 512, 1024], P('seq', 'head')
- input_grad: bfloat16 [64, 512, 1024], P('seq', 'head')
- grad_qkv: float32 [1024, 3072], P('head')
- grad_out: float32 [1024, 1024], P('head')
- grad_up: float32 [1024, 4096], P('head')
- grad_down: float32 [4096, 1024], P('head')
- grad_bias_q: float32 [1024], P('head')
- grad_bias_v: float32 [1024], P('head')
- grad_bias_out: float32 [1024], P('head')
- grad_bias_up: float32 [4096], P('head')
- grad_bias_down: float32 [1024], P('head')
- grad_gain_attn: float32 [1024], P('head')
- grad_shift_attn: float32 [1024], P('head')
- grad_gain_mlp: float32 [1024], P('head')
- grad_shift_mlp: float32 [1024], P('head')
The draws below stay inside these ranges and needn't reach their ends.
Inputs may be any that keep to these rules, and one draw needn't show every extreme that they name: In the placed order each group of 8 consecutive sequences has lengths summing to 2304, one of them 512 long. `seq_order`: A permutation of the sequences. Placed slot c of a group comes from the given group o_c further along (counted round), with o_0 = 0, o_1 = 1, o_c = c * 1 for 1 < c < 7 and o_c = 7 for the last slot; the 8 sequences of one given group go to 8 different groups, one to each slot number, in an order drawn from the seed.
All inputs are finite; a program needn't handle non-finite values.
Results may differ from the reference program's by a relative error of at most 0.017.
Values may be sent and summed in bfloat16 or wider, within the bound.
No kernel may reach another device: no remote copies, remote signals or barrier semaphores. Data moves between devices by JAX's collectives and lax.ppermute only.
A program may use at most 256 MiB of HBM per device.

```python
import jax
import jax.numpy as jnp
from jax import lax

D = 1024
HEADS = 16
FF = 4096
HEAD_SIZE = 64
SEQ_LEN = 512
PAIRS = 3
SLOTS = 8
GROUPS = 8
SEQS = 64


def slot_offsets():
    column = jnp.arange(SLOTS, dtype=jnp.int32)
    spaced = column * GROUPS // SLOTS
    spaced = jnp.where(column == 1, 1, spaced)
    return jnp.where(column == SLOTS - 1, GROUPS - 1, spaced).astype(jnp.int32)


def placed_layout(key):
    base = jax.random.fold_in(key, 11)
    key_local, key_pair, key_mix = jax.random.split(base, 3)
    shifts = slot_offsets()
    local = jax.vmap(lambda subkey: jax.random.permutation(subkey, SLOTS))(jax.random.split(key_local, GROUPS)).astype(jnp.int32)
    pair_lengths = jax.random.randint(key_pair, (GROUPS, PAIRS), SEQ_LEN // 8, SEQ_LEN + 1).astype(jnp.int32)
    pattern = jnp.concatenate([jnp.full((GROUPS, 1), SEQ_LEN, jnp.int32), jnp.full((GROUPS, 1), SEQ_LEN // 8, jnp.int32), pair_lengths, SEQ_LEN + SEQ_LEN // 8 - pair_lengths], axis=1)
    mixing = jax.vmap(lambda subkey: jax.random.permutation(subkey, SLOTS))(jax.random.split(key_mix, GROUPS)).astype(jnp.int32)
    pattern = jnp.take_along_axis(pattern, mixing, axis=1)
    source = jnp.arange(GROUPS, dtype=jnp.int32)[:, None]
    column = jnp.arange(SLOTS, dtype=jnp.int32)[None, :]
    target = (source - shifts[None, :]) % GROUPS
    given = (source * SLOTS + local).reshape(-1)
    placed = (target * SLOTS + column).reshape(-1)
    chosen = pattern[target, column].reshape(-1)
    seq_order = jnp.zeros((SEQS,), jnp.int32).at[given].set(placed)
    lengths = jnp.zeros((SEQS,), jnp.int32).at[given].set(chosen)
    return (seq_order, lengths)


def draw_lengths(key, part):
    return placed_layout(key)[1]


def draw_seq_order(key, part):
    return placed_layout(key)[0]


def steps_of(own_key, extent, pieces, low, top_value):
    level = 1.0
    for position, shards_of in pieces:
        draws = jax.random.uniform(jax.random.fold_in(jax.random.fold_in(own_key, 6), position), (shards_of,), jnp.float32, low / len(pieces), top_value / len(pieces))
        level = level * jnp.repeat(jnp.exp(draws), extent[position] // shards_of).reshape((-1,) + (1,) * (len(extent) - 1 - position))
    return level


def gaussian(own_key, dims, width, most, shards=(), kind=jnp.bfloat16):
    array = jax.random.normal(own_key, dims, jnp.float32) * width
    if len(shards) > 0:
        array = steps_of(own_key, dims, shards, -0.22, 0.18) * array
    return jnp.clip(array, min=-most, max=most).astype(kind)


def setup_inputs(seed: int = 0) -> dict:
    seeds = jax.random.split(jax.random.key(seed), 18)
    return {
        "tokens": gaussian(seeds[0], (SEQS, SEQ_LEN, D), 1.0, 6.0, ((0, 8), (1, 4))),
        "cotangent": gaussian(seeds[1], (SEQS, SEQ_LEN, D), 1.0, 6.0, ((0, 8), (1, 4))),
        "lengths": draw_lengths(jax.random.fold_in(seeds[17], 71), 0),
        "seq_order": draw_seq_order(jax.random.fold_in(seeds[17], 71), 0),
        "w_qkv": gaussian(seeds[4], (D, 3 * D), D ** -0.5, 0.1875, ((0, 4),)),
        "w_out": gaussian(seeds[5], (D, D), (D // 64) ** -0.5, 1.5, ((0, 4),)),
        "w_up": gaussian(seeds[6], (D, FF), D ** -0.5, 0.1875, ((0, 4),)),
        "w_down": gaussian(seeds[7], (FF, D), FF ** -0.5, 0.09375, ((0, 4),)),
        "bias_q": gaussian(seeds[8], (D,), 0.5, 3.0, ((0, 4),)),
        "bias_v": gaussian(seeds[9], (D,), 0.5, 3.0, ((0, 4),)),
        "bias_out": gaussian(seeds[10], (D,), 0.5, 3.0, ((0, 4),)),
        "bias_up": gaussian(seeds[11], (FF,), 0.5, 3.0, ((0, 4),)),
        "bias_down": gaussian(seeds[12], (D,), 0.5, 3.0, ((0, 4),)),
        "gain_attn": jnp.clip(1.0 + 0.15 * jax.random.normal(seeds[13], (D,), jnp.float32), 0.25, 1.75).astype(jnp.bfloat16),
        "shift_attn": gaussian(seeds[14], (D,), 0.5, 3.0, ((0, 4),)),
        "gain_mlp": jnp.clip(1.0 + 0.15 * jax.random.normal(seeds[15], (D,), jnp.float32), 0.25, 1.75).astype(jnp.bfloat16),
        "shift_mlp": gaussian(seeds[16], (D,), 0.5, 3.0, ((0, 4),)),
    }


@jax.custom_vjp
def low(v):
    return lax.optimization_barrier(v.astype(jnp.bfloat16)).astype(jnp.float32)

@jax.custom_vjp
def low_back(v):
    return v

def low_keep(v):
    return (low(v), None)

def low_pass(kept, grad):
    return (grad,)

def back_keep(v):
    return (v, None)

def back_low(kept, grad):
    return (low(grad),)
low.defvjp(low_keep, low_pass)
low_back.defvjp(back_keep, back_low)

def layer_norm(inputs, gain, shift):
    average = lax.optimization_barrier(jnp.mean(inputs, axis=-1, keepdims=True))
    centered = inputs - average
    variance = lax.optimization_barrier(jnp.mean(centered * centered, axis=-1, keepdims=True))
    return centered * lax.rsqrt(variance + 1e-12) * gain + shift

def matmul(left, right):
    return jnp.dot(left, right, precision=lax.Precision.HIGHEST, preferred_element_type=jnp.float32)

def sequence_attention(packed):
    queries, keys_in, values_in, keep_row = packed
    raw = jnp.einsum('qhe,khe->hqk', queries, keys_in, precision=lax.Precision.HIGHEST) * HEAD_SIZE ** (-0.5)
    scores = jnp.where(keep_row[None, None, :], low_back(raw), -1e+30)
    probs = jax.nn.softmax(scores, axis=-1)
    mixed = jnp.einsum('hqk,khe->qhe', low(probs), values_in, precision=lax.Precision.HIGHEST)
    return low(low_back(mixed))

def block_forward(params, inputs, lens):
    w_qkv, w_out, w_up, w_down, bias_q, bias_v, bias_out, bias_up, bias_down, gain_attn, shift_attn, gain_mlp, shift_mlp = params
    count_here = inputs.shape[0]
    rows_in = inputs.reshape(-1, D)
    joint_bias = jnp.concatenate([bias_q, jnp.zeros_like(bias_q), bias_v])
    qkv = low(low_back(matmul(rows_in, w_qkv) + joint_bias))
    qkv = qkv.reshape(count_here, SEQ_LEN, 3, HEADS, HEAD_SIZE)
    keep = jnp.arange(SEQ_LEN, dtype=jnp.int32)[None, :] < lens[:, None]
    context = lax.map(sequence_attention, (qkv[:, :, 0], qkv[:, :, 1], qkv[:, :, 2], keep))
    ctx_rows = context.reshape(-1, D)
    resid_attn = rows_in + low_back(matmul(ctx_rows, w_out) + bias_out)
    hidden = layer_norm(resid_attn, gain_attn, shift_attn)
    pre_act = low_back(matmul(low(hidden), w_up) + bias_up)
    act_low = low(jax.nn.gelu(pre_act, approximate=False))
    resid_mlp = hidden + low_back(matmul(act_low, w_down) + bias_down)
    final = layer_norm(resid_mlp, gain_mlp, shift_mlp)
    final = jnp.where(keep.reshape(-1, 1), final, 0.0)
    return final.reshape(count_here, SEQ_LEN, D)

def reference(tokens, cotangent, lengths, seq_order, w_qkv, w_out, w_up, w_down, bias_q, bias_v, bias_out, bias_up, bias_down, gain_attn, shift_attn, gain_mlp, shift_mlp):
    params = tuple((weight.astype(jnp.float32) for weight in (w_qkv, w_out, w_up, w_down, bias_q, bias_v, bias_out, bias_up, bias_down, gain_attn, shift_attn, gain_mlp, shift_mlp)))
    inputs = tokens.astype(jnp.float32)
    block_count = inputs.shape[0] // SLOTS
    placed_inputs = jnp.zeros_like(inputs).at[seq_order].set(inputs)
    placed_lengths = jnp.zeros_like(lengths).at[seq_order].set(lengths)

    def forward_placed(weights, values_in):
        shaped = values_in.reshape(block_count, SLOTS, SEQ_LEN, D)
        lens = placed_lengths.reshape(block_count, SLOTS)
        runner = jax.checkpoint(block_forward)
        result = lax.map(lambda paired: runner(weights, paired[0], paired[1]), (shaped, lens))
        return result.reshape(values_in.shape)
    final, pullback = jax.vjp(forward_placed, params, placed_inputs)
    grad_params, grad_placed = pullback(cotangent.astype(jnp.float32))
    grad_inputs = jnp.take(grad_placed, seq_order, axis=0)
    g_qkv, g_out, g_up, g_down, g_bq, g_bv, g_bo, g_bu, g_bd, g_ga, g_sa, g_gm, g_sm = grad_params
    return (final.astype(jnp.bfloat16), grad_inputs.astype(jnp.bfloat16), g_qkv, g_out, g_up, g_down, g_bq, g_bv, g_bo, g_bu, g_bd, g_ga, g_sa, g_gm, g_sm)
```

```python
import functools
import itertools

import jax
import jax.numpy as jnp
import numpy as np
from jax import lax
from jax.experimental import pallas as pl
from jax.experimental.pallas import tpu as pltpu
from jax.sharding import PartitionSpec as P

HEAD_SIZE = 64
CAP = 1472
HALF = CAP // 2
EPS = 1e-12
BF = jnp.bfloat16
F32 = jnp.float32
VMEM_SPEC = pl.BlockSpec(memory_space=pltpu.VMEM)
SMEM_SPEC = pl.BlockSpec(memory_space=pltpu.SMEM)
ANY_SPEC = pl.BlockSpec(memory_space=pl.ANY)


def mm(left, right):
    return jnp.dot(left, right, preferred_element_type=F32)


def mm_rows(left, right):
    return lax.dot_general(left, right, (((0,), (0,)), ((), ())), preferred_element_type=F32)


def mm_cols(left, right):
    return lax.dot_general(left, right, (((1,), (1,)), ((), ())), preferred_element_type=F32)


def _route_kernel(count, single, dst_ref, *refs):
    if single:
        src_ref, out_ref, sems = refs
        sources = [src_ref.at[k] for k in range(count)]
    else:
        sources = list(refs[:count])
        out_ref, sems = refs[count:]
    copies = []
    for k in range(count):
        copy = pltpu.make_async_copy(sources[k], out_ref.at[dst_ref[k]], sems.at[k])
        copy.start()
        copies.append(copy)
    for copy in copies:
        copy.wait()


def route(blocks, dst):
    single = not isinstance(blocks, (list, tuple))
    args = [blocks] if single else list(blocks)
    count = args[0].shape[0] if single else len(args)
    shape = args[0].shape[1:] if single else args[0].shape
    return pl.pallas_call(
        functools.partial(_route_kernel, count, single),
        out_shape=jax.ShapeDtypeStruct((count,) + shape, args[0].dtype),
        in_specs=[SMEM_SPEC] + [ANY_SPEC] * len(args),
        out_specs=ANY_SPEC,
        scratch_shapes=[pltpu.SemaphoreType.DMA((count,))],
        cost_estimate=pl.CostEstimate(flops=0, bytes_accessed=4 << 20, transcendentals=0),
        name="route",
    )(dst, *args)


def _pack_kernel(meta_ref, a0, a1, a2, a3, out_ref):
    here = meta_ref[12]
    out_ref[...] = jnp.zeros_like(out_ref)
    for slot in range(4):
        offset, length = meta_ref[slot], meta_ref[4 + slot]
        for src, flip in ((a0, 0), (a1, 2), (a2, 1), (a3, 3)):
            start = (here ^ flip) * 128
            pieces = jnp.clip((length - start + 15) // 16, 0, 8)

            @pl.loop(0, pieces)
            def _(i):
                row = pl.multiple_of(offset + start + i * 16, 16)
                out_ref[pl.ds(row, 16), :] = src[slot, pl.ds(pl.multiple_of(i * 16, 16), 16), :]


def pack(meta, own, from_x, from_core, from_both):
    return pl.pallas_call(
        _pack_kernel,
        out_shape=jax.ShapeDtypeStruct((CAP, own.shape[-1]), own.dtype),
        in_specs=[SMEM_SPEC] + [VMEM_SPEC] * 4,
        out_specs=VMEM_SPEC,
        compiler_params=pltpu.CompilerParams(vmem_limit_bytes=40 << 20),
        cost_estimate=pl.CostEstimate(flops=0, bytes_accessed=8 << 20, transcendentals=0),
        name="pack",
    )(meta, own, from_x, from_core, from_both)


def _unpack_kernel(meta_ref, mine_ref, other_ref, own_ref, far_ref, rows_ref, sems):
    here, core = meta_ref[12], meta_ref[13]
    first = pltpu.make_async_copy(
        mine_ref, rows_ref.at[pl.ds(pl.multiple_of(core * HALF, 16), HALF)], sems.at[0]
    )
    second = pltpu.make_async_copy(
        other_ref, rows_ref.at[pl.ds(pl.multiple_of((1 - core) * HALF, 16), HALF)], sems.at[1]
    )
    first.start()
    second.start()
    first.wait()
    second.wait()
    width = rows_ref.shape[1]
    for slot in range(4):
        offset, length = meta_ref[slot], meta_ref[4 + slot]
        for dst, flip in ((own_ref, 0), (far_ref, 2)):
            start = (here ^ flip) * 128

            @pl.loop(0, 8)
            def _(i):
                position = start + i * 16
                row = pl.multiple_of(jnp.minimum(offset + position, CAP - 16), 16)
                keep = lax.broadcasted_iota(jnp.int32, (16, width), 0) + position < length
                part = rows_ref[pl.ds(row, 16), :].astype(F32)
                dst[slot, pl.ds(pl.multiple_of(i * 16, 16), 16), :] = jnp.where(
                    keep, part, 0.0
                ).astype(BF)


def unpack(meta, mine, other):
    width = mine.shape[1]
    shape = jax.ShapeDtypeStruct((4, 128, width), BF)
    return pl.pallas_call(
        _unpack_kernel,
        out_shape=(shape, shape),
        in_specs=[SMEM_SPEC, ANY_SPEC, ANY_SPEC],
        out_specs=(VMEM_SPEC, VMEM_SPEC),
        scratch_shapes=[pltpu.VMEM((CAP, width), BF), pltpu.SemaphoreType.DMA((2,))],
        compiler_params=pltpu.CompilerParams(vmem_limit_bytes=40 << 20),
        cost_estimate=pl.CostEstimate(flops=0, bytes_accessed=5 << 20, transcendentals=0),
        name="unpack",
    )(meta, mine, other)


def _attend_kernel(meta_ref, qkv_ref, ctx_ref, lse_ref):
    ctx_ref[...] = jnp.zeros_like(ctx_ref)
    width = ctx_ref.shape[1]

    def one(slot, blocks):
        span = blocks * 128
        offset = pl.multiple_of(meta_ref[slot], 16)
        length = meta_ref[4 + slot]
        rows = pl.ds(offset, span)

        @pl.loop(0, width // 128)
        def _(pair):
            lane0 = pl.multiple_of(pair * 128, 128)
            keys = qkv_ref[rows, pl.ds(pl.multiple_of(width + lane0, 128), 128)]
            values = qkv_ref[rows, pl.ds(pl.multiple_of(2 * width + lane0, 128), 128)]
            values_t = values.astype(F32).T.astype(BF)
            for first in range(0, span, 256):
                step = min(span - first, 256)
                queries = qkv_ref[
                    pl.ds(pl.multiple_of(offset + first, 16), step), pl.ds(lane0, 128)
                ]
                queries = queries * jnp.asarray(HEAD_SIZE**-0.5, BF)
                lane = lax.broadcasted_iota(jnp.int32, (step, 128), 1)
                parts = []
                for half in range(2):
                    picked = jnp.where((lane >= 64) == (half == 1), queries, jnp.zeros_like(queries))
                    scores = mm_cols(keys, picked)
                    key_id = lax.broadcasted_iota(jnp.int32, scores.shape, 0)
                    scores = jnp.where(key_id < length, scores, -1e30)
                    highest = jnp.max(scores, axis=0, keepdims=True)
                    expo = jnp.exp(scores - highest)
                    total = jnp.sum(expo, axis=0, keepdims=True)
                    probs = (expo * (1.0 / total)).astype(BF)
                    parts.append(mm(values_t[64 * half : 64 * half + 64], probs))
                    lse_ref[slot, pair * 2 + half, :, first : first + step] = highest + jnp.log(total)
                mixed = jnp.concatenate(parts, axis=0).T
                ctx_ref[pl.ds(pl.multiple_of(offset + first, 16), step), pl.ds(lane0, 128)] = (
                    mixed.astype(BF)
                )

    @pl.loop(0, 4)
    def _(slot):
        for blocks in range(1, 5):
            pl.when(meta_ref[8 + slot] == blocks)(functools.partial(one, slot, blocks))


def attend(meta, qkv):
    width = qkv.shape[1] // 3
    return pl.pallas_call(
        _attend_kernel,
        out_shape=(
            jax.ShapeDtypeStruct((CAP, width), BF),
            jax.ShapeDtypeStruct((4, width // HEAD_SIZE, 1, 512), F32),
        ),
        in_specs=[SMEM_SPEC, VMEM_SPEC],
        out_specs=(VMEM_SPEC, VMEM_SPEC),
        compiler_params=pltpu.CompilerParams(vmem_limit_bytes=40 << 20),
        cost_estimate=pl.CostEstimate(
            flops=8 << 30, bytes_accessed=6 << 20, transcendentals=4 << 20
        ),
        name="attend",
    )(meta, qkv)


def _attend_back_kernel(meta_ref, qkv_ref, lse_ref, gctx_ref, out_ref):
    out_ref[...] = jnp.zeros_like(out_ref)
    width = gctx_ref.shape[1]

    def one(slot, blocks):
        span = blocks * 128
        offset = pl.multiple_of(meta_ref[slot], 16)
        length = meta_ref[4 + slot]
        rows = pl.ds(offset, span)

        @pl.loop(0, width // 128)
        def _(pair):
            lane0 = pl.multiple_of(pair * 128, 128)
            key_lanes = pl.ds(pl.multiple_of(width + lane0, 128), 128)
            value_lanes = pl.ds(pl.multiple_of(2 * width + lane0, 128), 128)
            keys = qkv_ref[rows, key_lanes]
            values = qkv_ref[rows, value_lanes]
            keys_t = keys.astype(F32).T.astype(BF)
            grad_keys = jnp.zeros((span, 128), F32)
            grad_values = jnp.zeros((span, 128), F32)
            for first in range(0, span, 256):
                step = min(span - first, 256)
                here = pl.ds(pl.multiple_of(offset + first, 16), step)
                queries = qkv_ref[here, pl.ds(lane0, 128)] * jnp.asarray(HEAD_SIZE**-0.5, BF)
                grad_ctx = gctx_ref[here, pl.ds(lane0, 128)]
                lane = lax.broadcasted_iota(jnp.int32, (step, 128), 1)
                row = lax.broadcasted_iota(jnp.int32, (step, 128), 0) + first
                grad_ctx = jnp.where(row < length, grad_ctx, jnp.zeros_like(grad_ctx))
                parts = []
                for half in range(2):
                    side = (lane >= 64) == (half == 1)
                    picked = jnp.where(side, queries, jnp.zeros_like(queries))
                    picked_grad = jnp.where(side, grad_ctx, jnp.zeros_like(grad_ctx))
                    scores = mm_cols(keys, picked)
                    log_total = lse_ref[slot, pair * 2 + half, :, first : first + step]
                    key_id = lax.broadcasted_iota(jnp.int32, scores.shape, 0)
                    probs = jnp.where(key_id < length, jnp.exp(scores - log_total), 0.0)
                    grad_values = grad_values + mm(probs.astype(BF), picked_grad)
                    grad_probs = mm_cols(values, picked_grad)
                    inner = jnp.sum(probs * grad_probs, axis=0, keepdims=True)
                    grad_scores = (probs * (grad_probs - inner)).astype(BF)
                    grad_keys = grad_keys + mm(grad_scores, picked)
                    parts.append(mm(keys_t[64 * half : 64 * half + 64], grad_scores))
                grad_queries = jnp.concatenate(parts, axis=0).T * HEAD_SIZE**-0.5
                out_ref[here, pl.ds(lane0, 128)] = grad_queries.astype(BF)
            out_ref[rows, key_lanes] = grad_keys.astype(BF)
            out_ref[rows, value_lanes] = grad_values.astype(BF)

    @pl.loop(0, 4)
    def _(slot):
        for blocks in range(1, 5):
            pl.when(meta_ref[8 + slot] == blocks)(functools.partial(one, slot, blocks))


def attend_back(meta, qkv, lse, grad_ctx):
    return pl.pallas_call(
        _attend_back_kernel,
        out_shape=jax.ShapeDtypeStruct(qkv.shape, BF),
        in_specs=[SMEM_SPEC] + [VMEM_SPEC] * 3,
        out_specs=VMEM_SPEC,
        compiler_params=pltpu.CompilerParams(vmem_limit_bytes=48 << 20),
        cost_estimate=pl.CostEstimate(
            flops=20 << 30, bytes_accessed=12 << 20, transcendentals=4 << 20
        ),
        name="attend_back",
    )(meta, qkv, lse, grad_ctx)


def normed(inputs):
    average = jnp.mean(inputs, axis=-1, keepdims=True)
    centered = inputs - average
    variance = jnp.mean(centered * centered, axis=-1, keepdims=True)
    rstd = lax.rsqrt(variance + EPS)
    return centered * rstd, rstd


def norm_back(unit, rstd, grad, gain):
    scaled = grad * gain
    return (
        scaled
        - jnp.mean(scaled, axis=-1, keepdims=True)
        - unit * jnp.mean(scaled * unit, axis=-1, keepdims=True)
    ) * rstd


def total_over_seq(part, group_count):
    if group_count != 8:
        return lax.psum(part, "seq")
    count, width = part.shape
    index = lax.axis_index("seq")
    here_y, here_z = index % 2, index // 2
    swap_y = [(i, i ^ 1) for i in range(8)]
    halves = part.reshape(2, count // 2, width)
    send = lax.dynamic_index_in_dim(halves, 1 - here_y, 0, keepdims=False).astype(BF)
    keep = lax.dynamic_index_in_dim(halves, here_y, 0, keepdims=False)
    keep = keep + lax.ppermute(send, "seq", swap_y).astype(F32)
    keep = keep.reshape(4, count // 8, width)
    right = left = None
    for step in (1, 2, 3):
        to_right = lax.dynamic_index_in_dim(
            keep, jnp.clip(here_z + 4 - step, 0, 3), 0, keepdims=False
        )
        to_left = lax.dynamic_index_in_dim(
            keep, jnp.clip(here_z - 4 + step, 0, 3), 0, keepdims=False
        )
        if right is not None:
            to_right = to_right + right.astype(F32)
            to_left = to_left + left.astype(F32)
        right = lax.ppermute(
            to_right.astype(BF),
            "seq",
            [(2 * z + y, 2 * z + 2 + y) for z in range(step) for y in range(2) if z < 3],
        )
        left = lax.ppermute(
            to_left.astype(BF),
            "seq",
            [(2 * z + y, 2 * z - 2 + y) for z in range(4 - step, 4) for y in range(2) if z > 0],
        )
    own = lax.dynamic_index_in_dim(keep, here_z, 0, keepdims=False)
    own = (own + right.astype(F32) + left.astype(F32)).astype(BF)
    pieces = [own] * 4
    right = left = own
    found = [[own, here_z]]
    for step in (1, 2, 3):
        right = lax.ppermute(
            right,
            "seq",
            [(2 * z + y, 2 * z + 2 + y) for z in range(step - 1, 3) for y in range(2)],
        )
        left = lax.ppermute(
            left,
            "seq",
            [(2 * z + y, 2 * z - 2 + y) for z in range(1, 5 - step) for y in range(2)],
        )
        found += [[right, here_z - step], [left, here_z + step]]
    for spot in range(4):
        for piece, where in found[1:]:
            pieces[spot] = jnp.where(where == spot, piece, pieces[spot])
    mine = jnp.concatenate(pieces, axis=0)
    other = lax.ppermute(mine, "seq", swap_y)
    lower = jnp.where(here_y == 0, mine, other)
    upper = jnp.where(here_y == 0, other, mine)
    return jnp.concatenate([lower, upper], axis=0).astype(F32)


def on_device(
    tokens,
    cotangent,
    lengths,
    seq_order,
    w_qkv,
    w_out,
    w_up,
    w_down,
    bias_q,
    bias_v,
    bias_out,
    bias_up,
    bias_down,
    gain_attn,
    shift_attn,
    gain_mlp,
    shift_mlp,
):
    group_count = lax.axis_size("seq")
    group_id = lax.axis_index("seq")
    here = lax.axis_index("head").astype(jnp.int32)
    core, chip = here % 2, here // 2
    slots, span_rows, width = tokens.shape
    part = width // 4
    ff_part = w_up.shape[1] // 4
    offsets = [k * group_count // slots for k in range(slots)]
    offsets[1], offsets[-1] = 1, group_count - 1
    swap_x = [(i, i ^ 2) for i in range(4)]
    swap_core = [(i, i ^ 1) for i in range(4)]

    def over_x(value):
        return lax.ppermute(value, "head", swap_x)

    def over_core(value):
        return lax.ppermute(value, "head", swap_core)

    def column_halves(weight, kinds):
        blocks = weight.reshape(weight.shape[0], kinds, 4, -1)

        def pick(flip):
            return lax.dynamic_slice_in_dim(blocks, here ^ flip, 1, axis=2)

        kept = jnp.concatenate([pick(0), pick(2)], axis=2).reshape(weight.shape[0], -1)
        sent = jnp.concatenate([pick(1), pick(3)], axis=2).reshape(weight.shape[0], -1)
        return kept, sent

    def gathered_columns(weight, kinds):
        kept, sent = column_halves(weight, kinds)
        far_kept, far_sent = column_halves(over_x(weight), kinds)
        full = jnp.zeros((4 * weight.shape[0], kept.shape[1]), BF)
        for flip, block in (
            (0, kept),
            (1, over_core(sent)),
            (2, far_kept),
            (3, over_core(far_sent)),
        ):
            full = lax.dynamic_update_slice_in_dim(full, block, (here ^ flip) * part, axis=0)
        return full

    full_qkv = gathered_columns(w_qkv, 3)
    full_out = jnp.concatenate([w_out, over_x(w_out)], axis=0)
    full_up = gathered_columns(w_up, 1)
    full_down = jnp.concatenate([w_down, over_x(w_down)], axis=0)
    small = lax.all_gather(
        jnp.concatenate(
            [
                bias_q,
                bias_v,
                bias_out,
                bias_down,
                gain_attn,
                shift_attn,
                gain_mlp,
                shift_mlp,
                bias_up,
            ]
        ),
        "head",
        axis=0,
        tiled=False,
    ).astype(F32)

    def vector(place):
        return small[:, place * part : (place + 1) * part].reshape(1, width)

    def local_columns(rows):
        return jnp.concatenate(
            [
                lax.dynamic_index_in_dim(rows, here, 0, keepdims=False),
                lax.dynamic_index_in_dim(rows, here ^ 2, 0, keepdims=False),
            ]
        )

    query_bias = local_columns(small[:, 0:part])
    value_bias = local_columns(small[:, part : 2 * part])
    up_bias = local_columns(small[:, 8 * part :])[None, :]
    out_bias, down_bias = vector(2), vector(3)
    attn_gain, attn_shift, mlp_gain, mlp_shift = vector(4), vector(5), vector(6), vector(7)
    joint_bias = jnp.concatenate([query_bias, jnp.zeros_like(query_bias), value_bias])[None, :]

    slot_ids = jnp.arange(slots, dtype=jnp.int32)
    local_ids = group_id * slots + slot_ids
    given_slot = lax.dynamic_slice_in_dim(seq_order, group_id * slots, slots) % slots
    given_of_slot = jnp.sum(
        jnp.where(given_slot[None, :] == slot_ids[:, None], slot_ids[None, :], 0), axis=1
    )
    matches = seq_order[None, :] == local_ids[:, None]
    slot_lens = jnp.sum(jnp.where(matches, lengths[None, :], 0), axis=1)
    aligned = (slot_lens + 15) // 16 * 16
    choices = np.zeros((35, slots), np.int32)
    for row, picks in enumerate(itertools.combinations(range(1, slots), 3)):
        choices[row, [0, *picks]] = 1
    sides = jnp.sum(choices * aligned[None, :], axis=1)
    larger = jnp.maximum(sides, jnp.sum(aligned) - sides)
    squares = jnp.sum(choices * (slot_lens * slot_lens)[None, :], axis=1)
    heavier = jnp.maximum(squares, jnp.sum(slot_lens * slot_lens) - squares)
    score = larger * 1024 + heavier // 4096
    best = jnp.min(score)
    chosen = jnp.argmax(score == best)
    in_first = jnp.sum(
        jnp.where(jnp.arange(35)[:, None] == chosen, choices, 0), axis=0, dtype=jnp.int32
    )
    is_own = jnp.where(chip == 0, in_first, 1 - in_first)
    before = np.tril(np.ones((slots, slots), np.int32), -1)
    rank_own = jnp.sum(before * is_own[None, :], axis=1)
    rank_far = jnp.sum(before * (1 - is_own)[None, :], axis=1)
    list_pos = jnp.where(is_own == 1, rank_own, 4 + rank_far).astype(jnp.int32)
    at_place = list_pos[None, :] == slot_ids[:, None]
    slot_at = jnp.sum(jnp.where(at_place, slot_ids[None, :], 0), axis=1)
    own_lens = jnp.sum(jnp.where(at_place, slot_lens[None, :], 0), axis=1)[:4]
    own_aligned = (own_lens + 15) // 16 * 16
    own_offsets = jnp.sum(np.tril(np.ones((4, 4), np.int32), -1) * own_aligned[None, :], axis=1)
    meta = jnp.concatenate(
        [
            own_offsets,
            own_lens,
            (own_lens + 127) // 128,
            here[None],
            core[None],
            jnp.zeros((2,), jnp.int32),
        ]
    ).astype(jnp.int32)
    row_ids = core * HALF + jnp.arange(HALF, dtype=jnp.int32)
    row_keep = jnp.any(
        (row_ids[:, None] >= own_offsets[None, :])
        & (row_ids[:, None] < (own_offsets + own_lens)[None, :]),
        axis=1,
        keepdims=True,
    )

    def to_chip(lists):
        own, far = lists[:4], over_x(lists[4:])
        return pack(meta, own, far, over_core(own), over_core(far))

    outgoing = route(tokens, given_slot.astype(jnp.int32))
    arrived = [outgoing[0]]
    for k in range(1, slots):
        arrived.append(
            lax.ppermute(
                outgoing[k],
                "seq",
                [(i, (i - offsets[k]) % group_count) for i in range(group_count)],
            )
        )
    rows_in = to_chip(route(arrived, list_pos))
    cot_rows = to_chip(route(cotangent, list_pos))

    def halves(value):
        return (
            lax.dynamic_slice_in_dim(value, core * HALF, HALF, axis=0),
            lax.dynamic_slice_in_dim(value, (1 - core) * HALF, HALF, axis=0),
        )

    def in_order(mine, other):
        lower = jnp.where(core == 0, mine, other)
        upper = jnp.where(core == 0, other, mine)
        return jnp.concatenate([lower, upper], axis=0)

    def core_sum(mine_left, other_left, right, product):
        arriving = over_core(product(other_left, right).astype(BF))
        return product(mine_left, right) + arriving.astype(F32)

    qkv = (mm(rows_in, full_qkv) + joint_bias).astype(BF)
    context, lse = attend(meta, qkv)
    ctx_mine, ctx_other = halves(context)
    rows_mine, _ = halves(rows_in)
    resid_attn = (
        core_sum(ctx_mine, ctx_other, full_out, mm) + rows_mine.astype(F32) + out_bias
    )
    unit_attn, rstd_attn = normed(resid_attn)
    hidden = unit_attn * attn_gain + attn_shift
    low_mine = hidden.astype(BF)
    low_other = over_core(low_mine)

    def up(low):
        pre = mm(low, full_up) + up_bias
        cdf = 0.5 * (1.0 + lax.erf(pre * np.float32(0.5**0.5)))
        slope = cdf + pre * jnp.exp(-0.5 * pre * pre) * np.float32((2 * np.pi) ** -0.5)
        return (pre * cdf).astype(BF), slope.astype(BF)

    act_mine, slope_mine = up(low_mine)
    act_other, slope_other = up(low_other)
    resid_mlp = core_sum(act_mine, act_other, full_down, mm) + hidden + down_bias
    unit_mlp, rstd_mlp = normed(resid_mlp)
    final_mine = (unit_mlp * mlp_gain + mlp_shift).astype(BF)

    cot_mine, _ = halves(cot_rows)
    grad_y = jnp.where(row_keep, cot_mine.astype(F32), 0.0)
    grad_mlp2 = norm_back(unit_mlp, rstd_mlp, grad_y, mlp_gain)
    sum_gain_mlp = jnp.sum(grad_y * unit_mlp, axis=0)
    sum_shift_mlp = jnp.sum(grad_y, axis=0)
    branch_mine = grad_mlp2.astype(BF)
    branch_other = over_core(branch_mine)
    sum_bias_down = jnp.sum(branch_mine, axis=0, dtype=F32)
    pre_mine = (mm_cols(branch_mine, full_down) * slope_mine.astype(F32)).astype(BF)
    pre_other = (mm_cols(branch_other, full_down) * slope_other.astype(F32)).astype(BF)
    sum_bias_up = jnp.sum(pre_mine, axis=0, dtype=F32) + jnp.sum(pre_other, axis=0, dtype=F32)
    branch = jnp.concatenate([branch_mine, branch_other], axis=0)
    act = jnp.concatenate([act_mine, act_other], axis=0)
    low = jnp.concatenate([low_mine, low_other], axis=0)
    grad_pre = jnp.concatenate([pre_mine, pre_other], axis=0)

    def chip_sum(far_product, own_product):
        arriving = over_x(far_product.astype(BF))
        return own_product + arriving.astype(F32)

    down_part = chip_sum(mm_rows(act[:, ff_part:], branch), mm_rows(act[:, :ff_part], branch))
    grad_hidden = core_sum(pre_mine, pre_other, full_up, mm_cols) + grad_mlp2

    def feature_block(value, flip):
        return lax.dynamic_slice_in_dim(value, (here ^ flip) * part, part, axis=1)

    def column_grads(left, right, kinds):
        blocks = right.shape[1] // (2 * kinds)

        def merged(mine, other):
            mine = mine.reshape(part, kinds, 2, blocks)
            other = other.reshape(part, kinds, 2, blocks)
            low_core = jnp.where(core == 0, mine, other)
            high_core = jnp.where(core == 0, other, mine)
            near = jnp.stack([low_core[:, :, 0], high_core[:, :, 0]], axis=2)
            far = jnp.stack([low_core[:, :, 1], high_core[:, :, 1]], axis=2)
            first = jnp.where(chip == 0, near, far)
            last = jnp.where(chip == 0, far, near)
            return jnp.concatenate([first, last], axis=2).reshape(part, -1)

        both = mm_rows(feature_block(left, 3), right).astype(BF)
        near = mm_rows(feature_block(left, 1), right).astype(BF)
        got_far = over_core(both)
        got_near = over_core(near)
        far_mine = mm_rows(feature_block(left, 2), right).astype(BF)
        arriving = over_x(merged(far_mine, got_far))
        own_mine = mm_rows(feature_block(left, 0), right)
        return merged(own_mine, got_near.astype(F32)) + arriving.astype(F32)

    up_part = column_grads(low, grad_pre, 1)

    grad_attn2 = norm_back(unit_attn, rstd_attn, grad_hidden, attn_gain)
    sum_gain_attn = jnp.sum(grad_hidden * unit_attn, axis=0)
    sum_shift_attn = jnp.sum(grad_hidden, axis=0)
    attn_mine = grad_attn2.astype(BF)
    attn_other = over_core(attn_mine)
    sum_bias_out = jnp.sum(attn_mine, axis=0, dtype=F32)
    grad_ctx = in_order(
        mm_cols(attn_mine, full_out).astype(BF), mm_cols(attn_other, full_out).astype(BF)
    )
    ctx_local = jnp.concatenate([ctx_mine, ctx_other], axis=0)
    attn_local = jnp.concatenate([attn_mine, attn_other], axis=0)
    out_part = chip_sum(
        mm_rows(ctx_local[:, part:], attn_local), mm_rows(ctx_local[:, :part], attn_local)
    )
    grad_qkv = attend_back(meta, qkv, lse, grad_ctx)
    gqkv_mine, gqkv_other = halves(grad_qkv)
    gx_mine = (core_sum(gqkv_mine, gqkv_other, full_qkv, mm_cols) + grad_attn2).astype(BF)
    qkv_part = column_grads(rows_in, grad_qkv, 3)
    qkv_sums = jnp.sum(grad_qkv, axis=0, dtype=F32)
    sum_bias_q, sum_bias_v = qkv_sums[: 2 * part], qkv_sums[4 * part :]

    def to_slots(mine):
        own, far = unpack(meta, mine, over_core(mine))
        arriving = over_x(far)
        parts = [own[k] for k in range(4)] + [arriving[k] for k in range(4)]
        return route(parts, slot_at.astype(jnp.int32))

    activations = to_slots(final_mine)
    back = to_slots(gx_mine)
    returned = [back[0]]
    for k in range(1, slots):
        returned.append(
            lax.ppermute(
                back[k],
                "seq",
                [(i, (i + offsets[k]) % group_count) for i in range(group_count)],
            )
        )
    input_grad = route(returned, given_of_slot.astype(jnp.int32))

    def whole_row(value):
        return value.reshape(4, part)

    def spread(value, size):
        result = jnp.zeros((4, size), F32)
        result = lax.dynamic_update_slice(result, value[None, :size], (here, 0))
        return lax.dynamic_update_slice(result, value[None, size:], (here ^ 2, 0))

    terms = jnp.concatenate(
        [
            spread(sum_bias_q, part),
            spread(sum_bias_v, part),
            whole_row(sum_bias_out),
            whole_row(sum_bias_down),
            whole_row(sum_gain_attn),
            whole_row(sum_shift_attn),
            whole_row(sum_gain_mlp),
            whole_row(sum_shift_mlp),
            spread(sum_bias_up, ff_part),
        ],
        axis=1,
    )

    def shard(value, flip):
        return lax.dynamic_index_in_dim(value, here ^ flip, 0, keepdims=True)

    from_core = over_core(jnp.concatenate([shard(terms, 1), shard(terms, 3)]).astype(BF))
    near_term = shard(terms, 0) + from_core[:1].astype(F32)
    far_term = shard(terms, 2) + from_core[1:].astype(F32)
    term = (near_term + over_x(far_term.astype(BF)).astype(F32))[0]
    lanes = term.shape[0] // part
    term = jnp.pad(term.reshape(lanes, part).T, ((0, 0), (0, 128 - lanes)))

    grad_down = total_over_seq(down_part, group_count)
    grad_up = total_over_seq(up_part, group_count)
    last = total_over_seq(jnp.concatenate([qkv_part, out_part, term], axis=1), group_count)
    grad_w_qkv = last[:, : 3 * width]
    grad_w_out = last[:, 3 * width : 4 * width]
    sums = last[:, 4 * width : 4 * width + lanes].T.reshape(-1)

    def piece(place):
        return sums[place * part : (place + 1) * part]

    return (
        activations,
        input_grad,
        grad_w_qkv,
        grad_w_out,
        grad_up,
        grad_down,
        piece(0),
        piece(1),
        piece(2),
        sums[8 * part :],
        piece(3),
        piece(4),
        piece(5),
        piece(6),
        piece(7),
    )


def solution(mesh):
    rows = P("seq", "head", None)
    weight, vector = P("head", None), P("head")
    in_specs = (rows, rows, P(), P()) + (weight,) * 4 + (vector,) * 9
    out_specs = (rows, rows) + (weight,) * 4 + (vector,) * 9
    return jax.shard_map(
        on_device, mesh=mesh, in_specs=in_specs, out_specs=out_specs, check_vma=False
    )
```

```python
import functools
import itertools

import jax
import jax.numpy as jnp
import numpy as np
from jax import lax
from jax.experimental import pallas as pl
from jax.experimental.pallas import tpu as pltpu
from jax.sharding import PartitionSpec as P

HEAD_SIZE = 64
CAP = 1536
HALF = CAP // 2
EPS = 1e-12
BF = jnp.bfloat16
F32 = jnp.float32
VMEM_SPEC = pl.BlockSpec(memory_space=pltpu.VMEM)
SMEM_SPEC = pl.BlockSpec(memory_space=pltpu.SMEM)
ANY_SPEC = pl.BlockSpec(memory_space=pl.ANY)
LIGHT = pl.CostEstimate(flops=0, bytes_accessed=1024, transcendentals=0)


def after(value, *others):
    return lax.optimization_barrier((value, *others))[0]


def mm(left, right):
    return jnp.dot(left, right, preferred_element_type=F32)


def mm_rows(left, right):
    return lax.dot_general(left, right, (((0,), (0,)), ((), ())), preferred_element_type=F32)


def mm_cols(left, right):
    return lax.dot_general(left, right, (((1,), (1,)), ((), ())), preferred_element_type=F32)


def _route_kernel(count, single, dst_ref, *refs):
    out_ref = refs[-1]
    for k in range(count):
        out_ref[dst_ref[k]] = refs[0][k] if single else refs[k][...]


def route(blocks, dst):
    single = not isinstance(blocks, (list, tuple))
    args = [blocks] if single else list(blocks)
    count = args[0].shape[0] if single else len(args)
    shape = args[0].shape[1:] if single else args[0].shape
    return pl.pallas_call(
        functools.partial(_route_kernel, count, single),
        out_shape=jax.ShapeDtypeStruct((count,) + shape, args[0].dtype),
        in_specs=[SMEM_SPEC] + [VMEM_SPEC] * len(args),
        out_specs=VMEM_SPEC,
        compiler_params=pltpu.CompilerParams(vmem_limit_bytes=24 << 20),
        cost_estimate=LIGHT,
        name="route",
    )(dst, *args)


def _pack_kernel(meta_ref, a0, a1, a2, a3, out_ref):
    here = meta_ref[12]
    out_ref[...] = jnp.zeros_like(out_ref)
    for slot in range(4):
        offset, length = meta_ref[slot], meta_ref[4 + slot]
        for src, flip in ((a0, 0), (a1, 2), (a2, 1), (a3, 3)):
            start = (here ^ flip) * 128
            pieces = jnp.clip((length - start + 15) // 16, 0, 8)

            @pl.loop(0, pieces)
            def _(i):
                row = pl.multiple_of(offset + start + i * 16, 16)
                out_ref[pl.ds(row, 16), :] = src[slot, pl.ds(pl.multiple_of(i * 16, 16), 16), :]


def pack(meta, own, from_x, from_core, from_both):
    return pl.pallas_call(
        _pack_kernel,
        out_shape=jax.ShapeDtypeStruct((CAP, own.shape[-1]), own.dtype),
        in_specs=[SMEM_SPEC] + [VMEM_SPEC] * 4,
        out_specs=VMEM_SPEC,
        compiler_params=pltpu.CompilerParams(vmem_limit_bytes=24 << 20),
        cost_estimate=LIGHT,
        name="pack",
    )(meta, own, from_x, from_core, from_both)


def _unpack_kernel(meta_ref, mine_ref, other_ref, own_ref, far_ref, rows_ref, sems):
    here, core = meta_ref[12], meta_ref[13]
    first = pltpu.make_async_copy(
        mine_ref, rows_ref.at[pl.ds(pl.multiple_of(core * HALF, 16), HALF)], sems.at[0]
    )
    second = pltpu.make_async_copy(
        other_ref, rows_ref.at[pl.ds(pl.multiple_of((1 - core) * HALF, 16), HALF)], sems.at[1]
    )
    first.start()
    second.start()
    first.wait()
    second.wait()
    width = rows_ref.shape[1]
    for slot in range(4):
        offset, length = meta_ref[slot], meta_ref[4 + slot]
        for dst, flip in ((own_ref, 0), (far_ref, 2)):
            start = (here ^ flip) * 128

            @pl.loop(0, 8)
            def _(i):
                position = start + i * 16
                row = pl.multiple_of(jnp.minimum(offset + position, CAP - 16), 16)
                keep = lax.broadcasted_iota(jnp.int32, (16, width), 0) + position < length
                part = rows_ref[pl.ds(row, 16), :].astype(F32)
                dst[slot, pl.ds(pl.multiple_of(i * 16, 16), 16), :] = jnp.where(
                    keep, part, 0.0
                ).astype(BF)


def unpack(meta, mine, other):
    width = mine.shape[1]
    shape = jax.ShapeDtypeStruct((4, 128, width), BF)
    return pl.pallas_call(
        _unpack_kernel,
        out_shape=(shape, shape),
        in_specs=[SMEM_SPEC, ANY_SPEC, ANY_SPEC],
        out_specs=(VMEM_SPEC, VMEM_SPEC),
        scratch_shapes=[pltpu.VMEM((CAP, width), BF), pltpu.SemaphoreType.DMA((2,))],
        compiler_params=pltpu.CompilerParams(vmem_limit_bytes=24 << 20),
        cost_estimate=LIGHT,
        name="unpack",
    )(meta, mine, other)


def _attend_kernel(meta_ref, qkv_ref, ctx_ref, lse_ref):
    ctx_ref[...] = jnp.zeros_like(ctx_ref)
    width = ctx_ref.shape[1]
    part = width // 2

    def one(slot, blocks):
        span = blocks * 128
        offset = pl.multiple_of(meta_ref[slot], 16)
        length = meta_ref[4 + slot]
        rows = pl.ds(offset, span)
        key_id = lax.broadcasted_iota(jnp.int32, (span, 1), 0)
        key_bias = jnp.where(key_id < length, 0.0, -1e30)

        @pl.loop(0, width // 128)
        def _(pair):
            lane0 = pl.multiple_of((pair // 2) * (3 * part) + (pair % 2) * 128, 128)
            keys = qkv_ref[rows, pl.ds(pl.multiple_of(part + lane0, 128), 128)]
            values = qkv_ref[rows, pl.ds(pl.multiple_of(2 * part + lane0, 128), 128)]
            values_t = values.astype(F32).T.astype(BF)
            for first in range(0, span, 256):
                step = min(span - first, 256)
                queries = qkv_ref[
                    pl.ds(pl.multiple_of(offset + first, 16), step), pl.ds(lane0, 128)
                ]
                queries = queries * jnp.asarray(HEAD_SIZE**-0.5, BF)
                lane = lax.broadcasted_iota(jnp.int32, (step, 128), 1)
                parts = []
                for half in range(2):
                    picked = jnp.where((lane >= 64) == (half == 1), queries, jnp.zeros_like(queries))
                    scores = mm_cols(keys, picked)
                    scores = scores + key_bias
                    highest = jnp.max(scores, axis=0, keepdims=True)
                    expo = jnp.exp(scores - highest)
                    total = jnp.sum(expo, axis=0, keepdims=True)
                    weighted = mm(values_t[64 * half : 64 * half + 64], expo.astype(BF))
                    parts.append(weighted * (1.0 / total))
                    lse_ref[slot, pair * 2 + half, :, first : first + step] = highest + jnp.log(total)
                mixed = jnp.concatenate(parts, axis=0).T
                out_lane = pl.multiple_of(pair * 128, 128)
                ctx_ref[pl.ds(pl.multiple_of(offset + first, 16), step), pl.ds(out_lane, 128)] = (
                    mixed.astype(BF)
                )

    @pl.loop(0, 4)
    def _(slot):
        for blocks in range(1, 5):
            pl.when(meta_ref[8 + slot] == blocks)(functools.partial(one, slot, blocks))


def attend(meta, qkv):
    width = qkv.shape[1] // 3
    return pl.pallas_call(
        _attend_kernel,
        out_shape=(
            jax.ShapeDtypeStruct((CAP, width), BF),
            jax.ShapeDtypeStruct((4, width // HEAD_SIZE, 1, 512), F32),
        ),
        in_specs=[SMEM_SPEC, VMEM_SPEC],
        out_specs=(VMEM_SPEC, VMEM_SPEC),
        compiler_params=pltpu.CompilerParams(vmem_limit_bytes=24 << 20),
        cost_estimate=LIGHT,
        name="attend",
    )(meta, qkv)


def _attend_back_kernel(block, meta_ref, qkv_ref, lse_ref, gctx_ref, out_ref):
    out_ref[...] = jnp.zeros_like(out_ref)
    part = out_ref.shape[1] // 3

    def one(slot, blocks):
        span = blocks * 128
        offset = pl.multiple_of(meta_ref[slot], 16)
        length = meta_ref[4 + slot]
        rows = pl.ds(offset, span)
        key_id = lax.broadcasted_iota(jnp.int32, (span, 1), 0)
        key_bias = jnp.where(key_id < length, 0.0, -1e30)

        @pl.loop(0, part // 128)
        def _(turn):
            pair = block * (part // 128) + turn
            out_lane = pl.multiple_of(turn * 128, 128)
            base = block * 3 * part
            lane0 = pl.multiple_of(base + turn * 128, 128)
            ctx_lane = pl.multiple_of(block * part + turn * 128, 128)
            keys = qkv_ref[rows, pl.ds(pl.multiple_of(part + lane0, 128), 128)]
            values = qkv_ref[rows, pl.ds(pl.multiple_of(2 * part + lane0, 128), 128)]
            keys_t = keys.astype(F32).T.astype(BF)
            grad_keys = jnp.zeros((span, 128), F32)
            grad_values = jnp.zeros((span, 128), F32)
            for first in range(0, span, 256):
                step = min(span - first, 256)
                here = pl.ds(pl.multiple_of(offset + first, 16), step)
                queries = qkv_ref[here, pl.ds(lane0, 128)] * jnp.asarray(HEAD_SIZE**-0.5, BF)
                grad_ctx = gctx_ref[here, pl.ds(ctx_lane, 128)]
                lane = lax.broadcasted_iota(jnp.int32, (step, 128), 1)
                row = lax.broadcasted_iota(jnp.int32, (step, 128), 0) + first
                grad_ctx = jnp.where(row < length, grad_ctx, jnp.zeros_like(grad_ctx))
                parts = []
                for half in range(2):
                    side = (lane >= 64) == (half == 1)
                    picked = jnp.where(side, queries, jnp.zeros_like(queries))
                    picked_grad = jnp.where(side, grad_ctx, jnp.zeros_like(grad_ctx))
                    scores = mm_cols(keys, picked)
                    log_total = lse_ref[slot, pair * 2 + half, :, first : first + step]
                    probs = jnp.exp(scores - log_total + key_bias)
                    grad_values = grad_values + mm(probs.astype(BF), picked_grad)
                    grad_probs = mm_cols(values, picked_grad)
                    inner = jnp.sum(probs * grad_probs, axis=0, keepdims=True)
                    grad_scores = (probs * (grad_probs - inner)).astype(BF)
                    grad_keys = grad_keys + mm(grad_scores, picked)
                    parts.append(mm(keys_t[64 * half : 64 * half + 64], grad_scores))
                grad_queries = jnp.concatenate(parts, axis=0).T * HEAD_SIZE**-0.5
                out_ref[here, pl.ds(out_lane, 128)] = grad_queries.astype(BF)
            key_lane = pl.multiple_of(part + out_lane, 128)
            value_lane = pl.multiple_of(2 * part + out_lane, 128)
            out_ref[rows, pl.ds(key_lane, 128)] = grad_keys.astype(BF)
            out_ref[rows, pl.ds(value_lane, 128)] = grad_values.astype(BF)

    @pl.loop(0, 4)
    def _(slot):
        for blocks in range(1, 5):
            pl.when(meta_ref[8 + slot] == blocks)(functools.partial(one, slot, blocks))


def attend_back(meta, qkv, lse, grad_ctx, block):
    return pl.pallas_call(
        functools.partial(_attend_back_kernel, block),
        out_shape=jax.ShapeDtypeStruct((qkv.shape[0], qkv.shape[1] // 2), BF),
        in_specs=[SMEM_SPEC] + [VMEM_SPEC] * 3,
        out_specs=VMEM_SPEC,
        compiler_params=pltpu.CompilerParams(vmem_limit_bytes=24 << 20),
        cost_estimate=LIGHT,
        name="attend_back",
    )(meta, qkv, lse, grad_ctx)


def _assemble_kernel(kinds, meta_ref, *refs):
    out_ref = refs[-1]
    here, core = meta_ref[12], meta_ref[13]
    rows, columns = refs[0].shape
    block = columns // (4 * kinds)
    for flip, src in zip((0, 2, 1, 3), refs[:4]):
        place = pl.ds(pl.multiple_of((here ^ flip) * rows, 16), rows)
        for kind in range(kinds):
            for side in range(2):
                lane = pl.multiple_of((kind * 4 + core + 2 * side) * block, 128)
                spot = (side * kinds + kind) * block
                out_ref[place, spot : spot + block] = src[:, pl.ds(lane, block)]


def assemble(meta, kinds, own, from_x, from_core, from_both):
    rows, columns = own.shape
    return pl.pallas_call(
        functools.partial(_assemble_kernel, kinds),
        out_shape=jax.ShapeDtypeStruct((4 * rows, columns // 2), BF),
        in_specs=[SMEM_SPEC] + [VMEM_SPEC] * 4,
        out_specs=VMEM_SPEC,
        compiler_params=pltpu.CompilerParams(vmem_limit_bytes=24 << 20),
        cost_estimate=LIGHT,
        name="assemble",
    )(meta, own, from_x, from_core, from_both)


def _spread_kernel(kinds, sides, meta_ref, *refs):
    out_ref = refs[-1]
    core = meta_ref[13]
    block = out_ref.shape[1] // (4 * kinds)
    for flip in range(2):
        for kind in range(kinds):
            for side in range(2):
                lane = pl.multiple_of((kind * 4 + (core ^ flip) + 2 * side) * block, 128)
                if sides:
                    src, spot = refs[2 * side + flip], kind * block
                else:
                    src, spot = refs[flip], (side * kinds + kind) * block
                out_ref[:, pl.ds(lane, block)] = src[:, spot : spot + block].astype(F32)


def spread_columns(meta, kinds, columns, *blocks):
    return pl.pallas_call(
        functools.partial(_spread_kernel, kinds, len(blocks) == 4),
        out_shape=jax.ShapeDtypeStruct((blocks[0].shape[0], columns), F32),
        in_specs=[SMEM_SPEC] + [VMEM_SPEC] * len(blocks),
        out_specs=VMEM_SPEC,
        compiler_params=pltpu.CompilerParams(vmem_limit_bytes=24 << 20),
        cost_estimate=LIGHT,
        name="spread_columns",
    )(meta, *blocks)


def _stack_kernel(place, meta_ref, mine_ref, other_ref, out_ref):
    spot = meta_ref[place]
    rows = mine_ref.shape[0]
    mine_at = pl.multiple_of(spot * rows, 16)
    other_at = pl.multiple_of((1 - spot) * rows, 16)
    out_ref[pl.ds(mine_at, rows), :] = mine_ref[...].astype(out_ref.dtype)
    out_ref[pl.ds(other_at, rows), :] = other_ref[...].astype(out_ref.dtype)


def stack_rows(meta, place, mine, other, kind=F32):
    return pl.pallas_call(
        functools.partial(_stack_kernel, place),
        out_shape=jax.ShapeDtypeStruct((2 * mine.shape[0], mine.shape[1]), kind),
        in_specs=[SMEM_SPEC] + [VMEM_SPEC] * 2,
        out_specs=VMEM_SPEC,
        compiler_params=pltpu.CompilerParams(vmem_limit_bytes=24 << 20),
        cost_estimate=LIGHT,
        name="stack_rows",
    )(meta, mine, other)


def _merge_kernel(meta_ref, own_ref, up_ref, mine_ref, other_ref, down_out, up_out):
    here_y, chip = meta_ref[14], meta_ref[18]
    rows, share = own_ref.shape[0], own_ref.shape[0] // 8
    lines = up_ref.shape[0] // 4
    width = own_ref.shape[1]
    size = mine_ref.shape[0] // 4
    down_out[pl.ds(pl.multiple_of(chip * rows, 16), rows), :] = own_ref[...]
    up_out[4 * lines :, :] = up_ref[...]
    for src, y in ((mine_ref, here_y), (other_ref, 1 - here_y)):
        for turn in range(4):
            at = (1 - chip) * rows + (y * 4 + turn) * share
            down_out[pl.ds(pl.multiple_of(at, 16), share), :] = src[
                turn * size : turn * size + share, :
            ]
            line = pl.multiple_of((y * 4 + turn) * (lines // 2), 16)
            for column in range(4):
                first = turn * size + share + column * (lines // 2)
                up_out[pl.ds(line, lines // 2), column * width : (column + 1) * width] = src[
                    first : first + lines // 2, :
                ]


def merge_shares(meta, w_down, far_up_high, mine, other):
    rows, width = w_down.shape
    return pl.pallas_call(
        _merge_kernel,
        out_shape=(
            jax.ShapeDtypeStruct((2 * rows, width), BF),
            jax.ShapeDtypeStruct((2 * far_up_high.shape[0], far_up_high.shape[1]), BF),
        ),
        in_specs=[SMEM_SPEC] + [VMEM_SPEC] * 4,
        out_specs=(VMEM_SPEC, VMEM_SPEC),
        compiler_params=pltpu.CompilerParams(vmem_limit_bytes=24 << 20),
        cost_estimate=LIGHT,
        name="merge_shares",
    )(meta, w_down, far_up_high, mine, other)


TILE = 256


def _tiles(meta_ref, count_at, out_refs, body):
    rows = out_refs[0].shape[0]
    used = jnp.minimum((meta_ref[count_at] + TILE - 1) // TILE, rows // TILE)

    @pl.loop(0, used)
    def _(tile):
        body(pl.ds(pl.multiple_of(tile * TILE, TILE), TILE))

    @pl.loop(used, rows // TILE)
    def _(tile):
        for out_ref in out_refs:
            place = pl.ds(pl.multiple_of(tile * TILE, TILE), TILE)
            out_ref[place, :] = jnp.zeros((TILE, out_ref.shape[1]), out_ref.dtype)


def _up_kernel(count_at, meta_ref, low_ref, weight_ref, bias_ref, act_ref, slope_ref):
    width = act_ref.shape[1]
    step = 512

    def body(place):
        @pl.loop(0, width // step)
        def _(turn):
            lanes = pl.ds(pl.multiple_of(turn * step, step), step)
            pre = mm(low_ref[place, :], weight_ref[:, lanes]) + bias_ref[:, lanes]
            cdf = 0.5 * (1.0 + lax.erf(pre * np.float32(0.5**0.5)))
            slope = cdf + pre * jnp.exp(-0.5 * pre * pre) * np.float32((2 * np.pi) ** -0.5)
            act_ref[place, lanes] = (pre * cdf).astype(BF)
            slope_ref[place, lanes] = slope.astype(BF)

    _tiles(meta_ref, count_at, (act_ref, slope_ref), body)


def up_product(meta, count_at, low, weight, bias):
    shape = jax.ShapeDtypeStruct((low.shape[0], weight.shape[1]), BF)
    return pl.pallas_call(
        functools.partial(_up_kernel, count_at),
        out_shape=(shape, shape),
        in_specs=[SMEM_SPEC] + [VMEM_SPEC] * 3,
        out_specs=(VMEM_SPEC, VMEM_SPEC),
        compiler_params=pltpu.CompilerParams(vmem_limit_bytes=24 << 20),
        cost_estimate=LIGHT,
        name="up_product",
    )(meta, low, weight, bias)


def _rows_kernel(count_at, turned, terms, scaled, meta_ref, *refs):
    lefts, rights = refs[:terms], refs[terms : 2 * terms]
    out_ref = refs[2 * terms + scaled]
    width = out_ref.shape[1]
    step = min(512, width)

    def body(place):
        @pl.loop(0, width // step)
        def _(turn):
            lanes = pl.ds(pl.multiple_of(turn * step, step), step)
            total = None
            for left_ref, right_ref in zip(lefts, rights):
                left = left_ref[place, :]
                if turned:
                    term = mm_cols(left, right_ref[lanes, :])
                else:
                    term = mm(left, right_ref[:, lanes])
                total = term if total is None else total + term
            if scaled:
                total = total * refs[2 * terms][place, lanes].astype(F32)
            out_ref[place, lanes] = total.astype(out_ref.dtype)

    _tiles(meta_ref, count_at, (out_ref,), body)


def rows_product(meta, count_at, lefts, rights, turned, kind, scale=None):
    width = rights[0].shape[0] if turned else rights[0].shape[1]
    args = [*lefts, *rights] + ([] if scale is None else [scale])
    return pl.pallas_call(
        functools.partial(_rows_kernel, count_at, turned, len(lefts), int(scale is not None)),
        out_shape=jax.ShapeDtypeStruct((lefts[0].shape[0], width), kind),
        in_specs=[SMEM_SPEC] + [VMEM_SPEC] * len(args),
        out_specs=VMEM_SPEC,
        compiler_params=pltpu.CompilerParams(vmem_limit_bytes=24 << 20),
        cost_estimate=LIGHT,
        name="rows_product",
    )(meta, *args)


def _grad_kernel(terms, meta_ref, at_ref, *refs):
    lefts, rights = refs[:terms], refs[terms : 2 * terms]
    out_ref, turned_ref = refs[2 * terms :]
    count, width = out_ref.shape
    first = 0
    for left_ref in lefts:
        rows = left_ref.shape[0]
        piece = left_ref[:, pl.ds(pl.multiple_of(at_ref[0], 128), count)]
        turned_ref[:, first : first + rows] = piece.astype(F32).T.astype(BF)
        first += rows
    step = 256

    @pl.loop(0, width // step)
    def _(turn):
        lanes = pl.ds(pl.multiple_of(turn * step, step), step)
        total, start = None, 0
        for right_ref in rights:
            rows = right_ref.shape[0]
            term = mm(turned_ref[:, start : start + rows], right_ref[:, lanes])
            total = term if total is None else total + term
            start += rows
        out_ref[:, lanes] = total.astype(out_ref.dtype)


def grad_product(meta, lefts, rights, start, count, kind):
    rows = sum(left.shape[0] for left in lefts)
    args = [*lefts, *rights]
    return pl.pallas_call(
        functools.partial(_grad_kernel, len(lefts)),
        out_shape=jax.ShapeDtypeStruct((count, rights[0].shape[1]), kind),
        in_specs=[SMEM_SPEC, SMEM_SPEC] + [VMEM_SPEC] * len(args),
        out_specs=VMEM_SPEC,
        scratch_shapes=[pltpu.VMEM((count, rows), BF)],
        compiler_params=pltpu.CompilerParams(vmem_limit_bytes=24 << 20),
        cost_estimate=LIGHT,
        name="grad_product",
    )(meta, jnp.asarray(start, jnp.int32)[None], *args)


def normed(inputs):
    average = jnp.mean(inputs, axis=-1, keepdims=True)
    centered = inputs - average
    variance = jnp.mean(centered * centered, axis=-1, keepdims=True)
    rstd = lax.rsqrt(variance + EPS)
    return centered * rstd, rstd


def norm_back(unit, rstd, grad, gain):
    scaled = grad * gain
    return (
        scaled
        - jnp.mean(scaled, axis=-1, keepdims=True)
        - unit * jnp.mean(scaled * unit, axis=-1, keepdims=True)
    ) * rstd


SWAP_X = [(i, i ^ 2) for i in range(4)]
SWAP_Y = [(i, i ^ 1) for i in range(8)]
SWAP_Z1 = [(i, i ^ 2) for i in range(8)]
SWAP_Z2 = [(i, i ^ 4) for i in range(8)]
AT_Y, AT_Z1, AT_Z2 = 14, 16, 17
MINE, OTHER = 19, 20


def moved(name, value, axis, pairs):
    with jax.named_scope(name):
        return lax.ppermute(value, axis, pairs)


class SeqSum:
    def __init__(self, name, meta, group_count):
        self.name, self.meta, self.whole = name, meta, group_count == 8
        index = lax.axis_index("seq")
        self.bits = {AT_Y: index % 2, AT_Z1: index // 2 % 2, AT_Z2: index // 4 % 2}

    def send(self, step, value, axis, pairs):
        self.token = value
        self.arrived = moved(f"{self.name}_{step}", value, axis, pairs)

    def start_x(self, far, own):
        self.kept = own[None]
        self.send("x", far.astype(BF), "head", SWAP_X)

    def start_y(self, far, kept):
        self.kept = kept
        self.send("y", far.astype(BF), "seq", SWAP_Y)

    def added(self, gates):
        arrived = after(self.arrived, *gates).astype(F32)
        self.kept = self.kept + arrived.reshape(self.kept.shape)

    def split(self, step, place, pairs):
        blocks, rows, columns = self.kept.shape
        halves = self.kept.reshape(blocks, 2, rows // 2, columns)
        bit = self.bits[place]
        self.kept = lax.dynamic_index_in_dim(halves, bit, 1, keepdims=False)
        sent = lax.dynamic_index_in_dim(halves, 1 - bit, 1, keepdims=False)
        self.send(step, sent.astype(BF).reshape(-1, columns), "seq", pairs)

    def step_y(self, *gates):
        self.added(gates)
        if self.whole:
            self.split("y", AT_Y, SWAP_Y)
            return
        count = self.kept.shape[1] // 2
        halves = lax.psum(self.kept[0], "seq").astype(BF).reshape(2, count, -1)
        bit = self.bits[AT_Y]
        self.mine = self.token = lax.dynamic_index_in_dim(halves, bit, 0, keepdims=False)
        self.arrived = lax.dynamic_index_in_dim(halves, 1 - bit, 0, keepdims=False)

    def step_z1(self, *gates):
        if self.whole:
            self.added(gates)
            self.split("z1", AT_Z1, SWAP_Z1)

    def step_z2(self, *gates):
        if self.whole:
            self.added(gates)
            self.split("z2", AT_Z2, SWAP_Z2)

    def step_x(self, *gates):
        if self.whole:
            self.added(gates)
            far = self.kept[1]
            self.kept = self.kept[:1]
            self.send("x", far.astype(BF), "head", SWAP_X)

    def back_z2(self, *gates):
        if self.whole:
            self.added(gates)
            self.mine = self.kept[0].astype(BF)
            self.send("back_z2", self.mine, "seq", SWAP_Z2)

    def joined(self, place, gates):
        arrived = after(self.arrived, *gates)
        self.mine = stack_rows(self.meta, place, self.mine, arrived, BF)

    def back_z1(self, *gates):
        if self.whole:
            self.joined(AT_Z2, gates)
            self.send("back_z1", self.mine, "seq", SWAP_Z1)

    def back_y(self, *gates):
        if self.whole:
            self.joined(AT_Z1, gates)
            self.send("back_y", self.mine, "seq", SWAP_Y)

    def halves(self, *gates):
        return self.mine, after(self.arrived, *gates)


def on_device(
    tokens,
    cotangent,
    lengths,
    seq_order,
    w_qkv,
    w_out,
    w_up,
    w_down,
    bias_q,
    bias_v,
    bias_out,
    bias_up,
    bias_down,
    gain_attn,
    shift_attn,
    gain_mlp,
    shift_mlp,
):
    group_count = lax.axis_size("seq")
    group_id = lax.axis_index("seq")
    here = lax.axis_index("head").astype(jnp.int32)
    core, chip = here % 2, here // 2
    slots, span_rows, width = tokens.shape
    part = width // 4
    ff_part = w_up.shape[1] // 4
    offsets = [k * group_count // slots for k in range(slots)]
    offsets[1], offsets[-1] = 1, group_count - 1
    swap_x = [(i, i ^ 2) for i in range(4)]
    swap_core = [(i, i ^ 1) for i in range(4)]

    def over_x(value, name="x"):
        with jax.named_scope(name):
            return lax.ppermute(value, "head", swap_x)

    def over_core(value, name="core"):
        with jax.named_scope(name):
            return lax.ppermute(value, "head", swap_core)

    slot_ids = jnp.arange(slots, dtype=jnp.int32)
    local_ids = group_id * slots + slot_ids
    given_slot = lax.dynamic_slice_in_dim(seq_order, group_id * slots, slots) % slots
    given_of_slot = jnp.sum(
        jnp.where(given_slot[None, :] == slot_ids[:, None], slot_ids[None, :], 0), axis=1
    )
    matches = seq_order[None, :] == local_ids[:, None]
    slot_lens = jnp.sum(jnp.where(matches, lengths[None, :], 0), axis=1)
    aligned = (slot_lens + 15) // 16 * 16
    choices = np.zeros((35, slots), np.int32)
    for row, picks in enumerate(itertools.combinations(range(1, slots), 3)):
        choices[row, [0, *picks]] = 1
    sides = jnp.sum(choices * aligned[None, :], axis=1)
    larger = jnp.maximum(sides, jnp.sum(aligned) - sides)
    squares = jnp.sum(choices * (slot_lens * slot_lens)[None, :], axis=1)
    heavier = jnp.maximum(squares, jnp.sum(slot_lens * slot_lens) - squares)
    score = larger * 1024 + heavier // 4096
    best = jnp.min(score)
    chosen = jnp.argmax(score == best)
    in_first = jnp.sum(
        jnp.where(jnp.arange(35)[:, None] == chosen, choices, 0), axis=0, dtype=jnp.int32
    )
    is_own = jnp.where(chip == 0, in_first, 1 - in_first)
    before = np.tril(np.ones((slots, slots), np.int32), -1)
    rank_own = jnp.sum(before * is_own[None, :], axis=1)
    rank_far = jnp.sum(before * (1 - is_own)[None, :], axis=1)
    list_pos = jnp.where(is_own == 1, rank_own, 4 + rank_far).astype(jnp.int32)
    at_place = list_pos[None, :] == slot_ids[:, None]
    slot_at = jnp.sum(jnp.where(at_place, slot_ids[None, :], 0), axis=1)
    own_lens = jnp.sum(jnp.where(at_place, slot_lens[None, :], 0), axis=1)[:4]
    own_aligned = (own_lens + 15) // 16 * 16
    own_offsets = jnp.sum(np.tril(np.ones((4, 4), np.int32), -1) * own_aligned[None, :], axis=1)
    total_rows = jnp.sum(own_aligned)
    meta = jnp.concatenate(
        [
            own_offsets,
            own_lens,
            (own_lens + 127) // 128,
            here[None],
            core[None],
            (group_id % 2)[None],
            (group_id // 2)[None],
            (group_id // 2 % 2)[None],
            (group_id // 4 % 2)[None],
            chip[None],
            jnp.clip(total_rows - core * HALF, 0, HALF)[None],
            jnp.clip(total_rows - (1 - core) * HALF, 0, HALF)[None],
            jnp.zeros((3,), jnp.int32),
        ]
    ).astype(jnp.int32)
    row_ids = core * HALF + jnp.arange(HALF, dtype=jnp.int32)
    row_keep = jnp.any(
        (row_ids[:, None] >= own_offsets[None, :])
        & (row_ids[:, None] < (own_offsets + own_lens)[None, :]),
        axis=1,
        keepdims=True,
    )

    def swapped(own, far):
        return own, far, over_core(own), over_core(far)

    if group_count == slots:
        spots = (group_id - given_slot) % slots
        sent_tokens = route(tokens, spots)
    else:
        sent_tokens = route(tokens, given_slot.astype(jnp.int32))
    small_here = jnp.concatenate(
        [
            bias_q,
            bias_v,
            bias_out,
            bias_down,
            gain_attn,
            shift_attn,
            gain_mlp,
            shift_mlp,
            bias_up,
        ]
    )[None, :]
    small_here = after(small_here, sent_tokens)
    small_core = over_core(small_here)

    def ordered(first, second, is_low):
        return jnp.concatenate(
            [jnp.where(is_low, first, second), jnp.where(is_low, second, first)], axis=0
        )

    small_pair = ordered(small_here, small_core, core == 0)
    small = ordered(small_pair, over_x(small_pair), chip == 0).astype(F32)

    def vector(place):
        return small[:, place * part : (place + 1) * part].reshape(1, width)

    def local_columns(rows):
        return jnp.concatenate(
            [
                lax.dynamic_index_in_dim(rows, core, 0, keepdims=False),
                lax.dynamic_index_in_dim(rows, core + 2, 0, keepdims=False),
            ]
        )

    query_bias = local_columns(small[:, 0:part])
    value_bias = local_columns(small[:, part : 2 * part])
    up_bias = local_columns(small[:, 8 * part :])[None, :]
    out_bias, down_bias = vector(2), vector(3)
    attn_gain, attn_shift, mlp_gain, mlp_shift = vector(4), vector(5), vector(6), vector(7)
    no_bias = jnp.zeros((part,), F32)
    joint_bias = jnp.concatenate(
        [query_bias[:part], no_bias, value_bias[:part], query_bias[part:], no_bias, value_bias[part:]]
    )[None, :]


    if group_count == 8:
        share = w_down.shape[0] // 8
        turn = (group_id % 2) * 4 + group_id // 4 + 2 * (group_id // 2 % 2)
        lines = w_up.shape[0] // 16
        up_lines = lax.dynamic_slice_in_dim(w_up, turn * lines, lines, axis=0)
        mixed = jnp.concatenate(
            [lax.dynamic_slice_in_dim(w_down, turn * share, share, axis=0)]
            + jnp.split(up_lines, 4, axis=1),
            axis=0,
        )
        mixed = over_x(after(mixed, small), "x_shares")
    else:
        mixed = small
    if group_count == slots:
        got = lax.all_to_all(sent_tokens, "seq", split_axis=0, concat_axis=0, tiled=True)
        came = (slot_ids - group_id) % slots
        placed = jnp.sum(
            jnp.where(came[:, None] == slot_ids[None, :], list_pos[None, :], 0), axis=1
        )
        lists = route(after(got, small, mixed), placed.astype(jnp.int32))
    else:
        arrived = [sent_tokens[0]]
        for k in range(1, slots):
            arrived.append(
                lax.ppermute(
                    sent_tokens[k],
                    "seq",
                    [(i, (i - offsets[k]) % group_count) for i in range(group_count)],
                )
            )
        lists = route(arrived, list_pos)

    def by_chip(own, far):
        return jnp.concatenate(
            [jnp.where(chip == 0, own, far), jnp.where(chip == 0, far, own)], axis=0
        )

    first_weights = over_x(
        after(jnp.concatenate([w_qkv, w_out], axis=1), mixed), "x_first_weights"
    )
    far_qkv, far_out = first_weights[:, : 3 * width], first_weights[:, 3 * width :]
    full_qkv = assemble(meta, 3, *swapped(w_qkv, far_qkv))
    full_out = by_chip(w_out, far_out)

    far_tokens = over_x(lists[4:], "x_tokens")
    if group_count == 8:
        pair = stack_rows(meta, AT_Z2, mixed, moved("share_z2", mixed, "seq", SWAP_Z2), BF)
        gate = four = stack_rows(meta, AT_Z1, pair, moved("share_z1", pair, "seq", SWAP_Z1), BF)
    else:
        gate = far_tokens
    rows_in = pack(meta, *swapped(lists[:4], after(far_tokens, gate)))
    w_up_later, _ = lax.optimization_barrier((w_up, far_tokens))
    if group_count == 8:
        far_up_high = over_x(w_up_later[part // 2 :], "x_up_weight")
        other_four = moved("share_y", four, "seq", SWAP_Y)
    else:
        far_up = over_x(w_up_later, "x_up_weight")
        full_down = by_chip(w_down, over_x(w_down))
    cot_lists = route(cotangent, list_pos)
    cot_far_in, _ = lax.optimization_barrier((cot_lists[4:], far_tokens))
    cot_rows = pack(meta, *swapped(cot_lists[:4], over_x(cot_far_in, "x_cotangent")))

    def halves(value):
        return (
            lax.dynamic_slice_in_dim(value, core * HALF, HALF, axis=0),
            lax.dynamic_slice_in_dim(value, (1 - core) * HALF, HALF, axis=0),
        )

    def in_order(mine, other):
        lower = jnp.where(core == 0, mine, other)
        upper = jnp.where(core == 0, other, mine)
        return jnp.concatenate([lower, upper], axis=0)

    def core_sum(lefts_mine, lefts_other, rights, turned):
        arriving = over_core(rows_product(meta, OTHER, lefts_other, rights, turned, BF))
        return rows_product(meta, MINE, lefts_mine, rights, turned, F32) + arriving.astype(F32)

    qkv = (mm(rows_in, full_qkv) + joint_bias).astype(BF)
    context, lse = attend(meta, qkv)
    if group_count == 8:
        context, other_four, far_up_high = lax.optimization_barrier(
            (context, other_four, far_up_high)
        )
        full_down, far_up = merge_shares(meta, w_down, far_up_high, four, other_four)
    full_up = assemble(meta, 1, *swapped(w_up, far_up))
    ctx_mine, ctx_other = halves(context)
    rows_mine, _ = halves(rows_in)
    resid_attn = (
        core_sum([ctx_mine], [ctx_other], [full_out], False) + rows_mine.astype(F32) + out_bias
    )
    unit_attn, rstd_attn = normed(resid_attn)
    hidden = unit_attn * attn_gain + attn_shift
    low_mine = hidden.astype(BF)
    low_other = over_core(low_mine)

    low_mine = after(low_mine, cot_rows)
    act_mine, slope_mine = up_product(meta, MINE, low_mine, full_up, up_bias)
    act_other, slope_other = up_product(meta, OTHER, low_other, full_up, up_bias)
    resid_mlp = core_sum([act_mine], [act_other], [full_down], False) + hidden + down_bias
    unit_mlp, rstd_mlp = normed(resid_mlp)
    final_mine = (unit_mlp * mlp_gain + mlp_shift).astype(BF)

    cot_mine, _ = halves(cot_rows)
    grad_y = jnp.where(row_keep, cot_mine.astype(F32), 0.0)
    grad_mlp2 = norm_back(unit_mlp, rstd_mlp, grad_y, mlp_gain)
    sum_gain_mlp = jnp.sum(grad_y * unit_mlp, axis=0)
    sum_shift_mlp = jnp.sum(grad_y, axis=0)
    branch_mine = grad_mlp2.astype(BF)
    branch_other = over_core(branch_mine)
    sum_bias_down = jnp.sum(branch_mine, axis=0, dtype=F32)
    def grads(lefts, rights, start, count, kind=F32):
        return grad_product(meta, lefts, rights, start, count, kind)

    down_sum = SeqSum("down", meta, group_count)
    acts, branches = [act_mine, act_other], [branch_mine, branch_other]
    if group_count == 8:
        here_y = group_id % 2
        count = ff_part // 2

        def down_term(half, kind):
            return jnp.stack(
                [
                    grads(acts, branches, side * ff_part + half * count, count, kind)
                    for side in (chip, 1 - chip)
                ]
            )

        down_sum.start_y(down_term(1 - here_y, BF).reshape(-1, width), down_term(here_y, F32))
    else:
        down_sum.start_x(
            *(grads(acts, branches, side * ff_part, ff_part) for side in (1 - chip, chip))
        )
    branch_mine, branch_other, _ = lax.optimization_barrier(
        (branch_mine, branch_other, down_sum.token)
    )
    pre_mine = rows_product(meta, MINE, [branch_mine], [full_down], True, BF, slope_mine)
    pre_other = rows_product(meta, OTHER, [branch_other], [full_down], True, BF, slope_other)
    sum_bias_up = jnp.sum(pre_mine, axis=0, dtype=F32) + jnp.sum(pre_other, axis=0, dtype=F32)

    lows, pres = [low_mine, low_other], [pre_mine, pre_other]
    up_far, up_own = (
        grads(lows, pres, side * 2 * part, 2 * part, kind)
        for side, kind in ((1 - chip, BF), (chip, F32))
    )
    up_sum = SeqSum("up", meta, group_count)
    up_sum.start_x(up_far, up_own)
    pre_mine, pre_other, _ = lax.optimization_barrier((pre_mine, pre_other, up_sum.token))
    gh_other = rows_product(meta, OTHER, [pre_other], [full_up], True, BF)
    gh_arrived = over_core(gh_other)
    if group_count == 8:
        down_sum.step_z1(gh_other)
    else:
        down_sum.step_y(gh_other)
    pre_mine = after(pre_mine, down_sum.token)
    grad_hidden = rows_product(meta, MINE, [pre_mine], [full_up], True, F32)
    grad_hidden = grad_hidden + gh_arrived.astype(F32) + grad_mlp2

    grad_attn2 = norm_back(unit_attn, rstd_attn, grad_hidden, attn_gain)
    sum_gain_attn = jnp.sum(grad_hidden * unit_attn, axis=0)
    sum_shift_attn = jnp.sum(grad_hidden, axis=0)
    attn_mine = grad_attn2.astype(BF)
    attn_other = over_core(attn_mine)
    sum_bias_out = jnp.sum(attn_mine, axis=0, dtype=F32)
    half_width = width // 2

    def out_term(side, kind):
        term = grads([ctx_mine, ctx_other], [attn_mine, attn_other], side * part, part, kind)
        return jnp.concatenate([term[:, :half_width], term[:, half_width:]], axis=0)

    out_far, out_own = out_term(1 - chip, BF), out_term(chip, F32)
    down_sum.step_z2(out_own, out_far)
    up_sum.step_y(down_sum.token)
    attn_mine, attn_other, _ = lax.optimization_barrier((attn_mine, attn_other, up_sum.token))
    grad_ctx = in_order(
        rows_product(meta, MINE, [attn_mine], [full_out], True, BF),
        rows_product(meta, OTHER, [attn_other], [full_out], True, BF),
    )
    grad_first = attend_back(meta, qkv, lse, grad_ctx, 0)
    down_sum.step_x(grad_first)
    up_sum.step_z1(down_sum.token)
    grad_first = after(grad_first, up_sum.token)
    first_far, first_own = (
        jnp.concatenate(
            [grads([rows_in], [grad_first], side * 2 * part, 2 * part, out.dtype), out], axis=1
        )
        for side, out in ((1 - chip, out_far), (chip, out_own))
    )
    first_sum = SeqSum("first", meta, group_count)
    first_sum.start_x(first_far, first_own)
    down_sum.back_z2(first_sum.token, first_own)
    grad_last = attend_back(meta, qkv, lse, after(grad_ctx, down_sum.token), 1)
    up_sum.step_z2(grad_last)
    down_sum.back_z1(up_sum.token)
    grad_last = after(grad_last, down_sum.token)
    last_far, last_own = (
        grads([rows_in], [grad_last], side * 2 * part, 2 * part, kind)
        for side, kind in ((1 - chip, BF), (chip, F32))
    )
    first_sums = jnp.sum(grad_first, axis=0, dtype=F32)
    last_sums = jnp.sum(grad_last, axis=0, dtype=F32)
    sum_bias_q = jnp.concatenate([first_sums[:part], last_sums[:part]])
    sum_bias_v = jnp.concatenate([first_sums[2 * part :], last_sums[2 * part :]])

    def whole_row(value):
        return value.reshape(4, part)

    def spread(value, size):
        result = jnp.zeros((4, size), F32)
        result = lax.dynamic_update_slice(result, value[None, :size], (core, 0))
        return lax.dynamic_update_slice(result, value[None, size:], (core + 2, 0))

    terms = jnp.concatenate(
        [
            spread(sum_bias_q, part),
            spread(sum_bias_v, part),
            whole_row(sum_bias_out),
            whole_row(sum_bias_down),
            whole_row(sum_gain_attn),
            whole_row(sum_shift_attn),
            whole_row(sum_gain_mlp),
            whole_row(sum_shift_mlp),
            spread(sum_bias_up, ff_part),
        ],
        axis=1,
    )

    def shard(value, flip):
        return lax.dynamic_index_in_dim(value, here ^ flip, 0, keepdims=True)

    from_core = over_core(jnp.concatenate([shard(terms, 1), shard(terms, 3)]).astype(BF))
    near_term = shard(terms, 0)[0] + from_core[0].astype(F32)
    far_term = shard(terms, 2)[0] + from_core[1].astype(F32)
    lanes = near_term.shape[0] // (2 * part)

    def as_columns(term):
        return jnp.pad(term.reshape(lanes, 2 * part).T, ((0, 0), (0, 128 - lanes)))

    last_far = jnp.concatenate([last_far, as_columns(far_term).astype(BF)], axis=1)
    last_own = jnp.concatenate([last_own, as_columns(near_term)], axis=1)
    last_sum = SeqSum("last", meta, group_count)
    last_sum.start_x(last_far, last_own)
    first_sum.step_y(last_sum.token)
    up_sum.back_z2(first_sum.token)
    grad_last = after(grad_last, up_sum.token)

    qkv_blocks = [full_qkv[:, : 3 * part], full_qkv[:, 3 * part :]]
    first_mine, first_other = halves(grad_first)
    last_mine, last_other = halves(grad_last)
    gx_other = rows_product(meta, OTHER, [first_other, last_other], qkv_blocks, True, BF)
    gx_arrived = over_core(gx_other)
    down_sum.back_y(gx_other)
    first_sum.step_z1(down_sum.token)
    last_mine = after(last_mine, first_sum.token)
    gx_mine = rows_product(meta, MINE, [first_mine, last_mine], qkv_blocks, True, F32)
    gx_mine = (gx_mine + gx_arrived.astype(F32) + grad_attn2).astype(BF)

    def listed(own, arriving):
        parts = [own[k] for k in range(4)] + [arriving[k] for k in range(4)]
        return route(parts, slot_at.astype(jnp.int32))

    up_sum.back_z1(gx_mine)
    gx_own, gx_far = unpack(meta, gx_mine, over_core(after(gx_mine, up_sum.token)))
    last_sum.step_y(gx_far)
    gx_arrived = over_x(after(gx_far, last_sum.token), "x_grad")
    first_sum.step_z2(last_sum.token)
    up_sum.back_y(first_sum.token)
    last_sum.step_z1(up_sum.token)
    first_sum.back_z2(last_sum.token)
    last_sum.step_z2(first_sum.token)
    back = listed(gx_own, after(gx_arrived, last_sum.token))
    y_own, y_far = unpack(meta, final_mine, over_core(after(final_mine, gx_far)))
    activations = listed(y_own, over_x(after(y_far, gx_arrived), "x_activations"))
    if group_count == slots:
        spots = (group_id + slot_ids) % slots
        got = lax.all_to_all(
            route(back, spots.astype(jnp.int32)), "seq", split_axis=0, concat_axis=0, tiled=True
        )
        came = (group_id - slot_ids) % slots
        home = jnp.sum(
            jnp.where(came[:, None] == slot_ids[None, :], given_of_slot[None, :], 0), axis=1
        )
        input_grad = route(got, home.astype(jnp.int32))
    else:
        returned = [back[0]]
        for k in range(1, slots):
            returned.append(
                lax.ppermute(
                    back[k],
                    "seq",
                    [(i, (i + offsets[k]) % group_count) for i in range(group_count)],
                )
            )
        input_grad = route(returned, given_of_slot.astype(jnp.int32))

    def my_block(mine, other):
        aligned_here = (group_id % 2) == core
        return jnp.where(aligned_here, mine, other), jnp.where(aligned_here, other, mine)

    first_sum.back_z1(back)
    grad_down = stack_rows(meta, AT_Y, *down_sum.halves(first_sum.token))
    last_sum.back_z2(grad_down)
    first_sum.back_y(last_sum.token)
    last_sum.back_z1(first_sum.token)
    kept, sent = my_block(*up_sum.halves(last_sum.token))
    grad_w_up = spread_columns(meta, 1, 4 * ff_part, kept, over_core(sent))
    last_sum.back_y(kept)
    first_halves = first_sum.halves(last_sum.token)
    last_halves = last_sum.halves()
    blocks = []
    for mine, other in (first_halves, last_halves):
        kept, sent = my_block(mine[:, : 3 * part], other[:, : 3 * part])
        blocks += [kept, over_core(sent)]
    grad_w_qkv = spread_columns(meta, 3, 3 * width, *blocks)

    def by_y(mine, other, axis):
        lower = jnp.where(group_id % 2 == 0, mine, other)
        upper = jnp.where(group_id % 2 == 0, other, mine)
        return jnp.concatenate([lower, upper], axis=axis).astype(F32)

    grad_w_out = by_y(*(half[:, 3 * part :] for half in first_halves), 1)
    sums = by_y(*(half[:, 3 * part :] for half in last_halves), 0)[:, :lanes].T.reshape(-1)

    def piece(place):
        return sums[place * part : (place + 1) * part]

    return (
        activations,
        input_grad,
        grad_w_qkv,
        grad_w_out,
        grad_w_up,
        grad_down,
        piece(0),
        piece(1),
        piece(2),
        sums[8 * part :],
        piece(3),
        piece(4),
        piece(5),
        piece(6),
        piece(7),
    )


def solution(mesh):
    rows = P("seq", "head", None)
    weight, vector = P("head", None), P("head")
    in_specs = (rows, rows, P(), P()) + (weight,) * 4 + (vector,) * 9
    out_specs = (rows, rows) + (weight,) * 4 + (vector,) * 9
    return jax.shard_map(
        on_device, mesh=mesh, in_specs=in_specs, out_specs=out_specs, check_vma=False
    )
```

```python
import functools
import itertools

import jax
import jax.numpy as jnp
import numpy as np
from jax import lax
from jax.experimental import pallas as pl
from jax.experimental.pallas import tpu as pltpu
from jax.sharding import PartitionSpec as P

HEAD_SIZE = 64
CAP = 1536
HALF = CAP // 2
EPS = 1e-12
BF = jnp.bfloat16
F32 = jnp.float32
VMEM_SPEC = pl.BlockSpec(memory_space=pltpu.VMEM)
SMEM_SPEC = pl.BlockSpec(memory_space=pltpu.SMEM)
ANY_SPEC = pl.BlockSpec(memory_space=pl.ANY)
LIGHT = pl.CostEstimate(flops=0, bytes_accessed=1024, transcendentals=0)


def after(value, *others):
    return lax.optimization_barrier((value, *others))[0]


def mm(left, right):
    return jnp.dot(left, right, preferred_element_type=F32)


def mm_rows(left, right):
    return lax.dot_general(left, right, (((0,), (0,)), ((), ())), preferred_element_type=F32)


def mm_cols(left, right):
    return lax.dot_general(left, right, (((1,), (1,)), ((), ())), preferred_element_type=F32)


def _route_kernel(count, single, dst_ref, *refs):
    out_ref = refs[-1]
    for k in range(count):
        out_ref[dst_ref[k]] = refs[0][k] if single else refs[k][...]


def route(blocks, dst):
    single = not isinstance(blocks, (list, tuple))
    args = [blocks] if single else list(blocks)
    count = args[0].shape[0] if single else len(args)
    shape = args[0].shape[1:] if single else args[0].shape
    return pl.pallas_call(
        functools.partial(_route_kernel, count, single),
        out_shape=jax.ShapeDtypeStruct((count,) + shape, args[0].dtype),
        in_specs=[SMEM_SPEC] + [VMEM_SPEC] * len(args),
        out_specs=VMEM_SPEC,
        compiler_params=pltpu.CompilerParams(vmem_limit_bytes=12 << 20),
        cost_estimate=LIGHT,
        name="route",
    )(dst, *args)


def _pack_kernel(meta_ref, a0, a1, a2, a3, out_ref):
    here = meta_ref[12]
    out_ref[...] = jnp.zeros_like(out_ref)
    for slot in range(4):
        offset, length = meta_ref[slot], meta_ref[4 + slot]
        for src, flip in ((a0, 0), (a1, 2), (a2, 1), (a3, 3)):
            start = (here ^ flip) * 128
            pieces = jnp.clip((length - start + 15) // 16, 0, 8)

            @pl.loop(0, pieces)
            def _(i):
                row = pl.multiple_of(offset + start + i * 16, 16)
                out_ref[pl.ds(row, 16), :] = src[slot, pl.ds(pl.multiple_of(i * 16, 16), 16), :]


def pack(meta, own, from_x, from_core, from_both):
    return pl.pallas_call(
        _pack_kernel,
        out_shape=jax.ShapeDtypeStruct((CAP, own.shape[-1]), own.dtype),
        in_specs=[SMEM_SPEC] + [VMEM_SPEC] * 4,
        out_specs=VMEM_SPEC,
        compiler_params=pltpu.CompilerParams(vmem_limit_bytes=12 << 20),
        cost_estimate=LIGHT,
        name="pack",
    )(meta, own, from_x, from_core, from_both)


def _unpack_kernel(meta_ref, mine_ref, other_ref, own_ref, far_ref, rows_ref, sems):
    here, core = meta_ref[12], meta_ref[13]
    first = pltpu.make_async_copy(
        mine_ref, rows_ref.at[pl.ds(pl.multiple_of(core * HALF, 16), HALF)], sems.at[0]
    )
    second = pltpu.make_async_copy(
        other_ref, rows_ref.at[pl.ds(pl.multiple_of((1 - core) * HALF, 16), HALF)], sems.at[1]
    )
    first.start()
    second.start()
    first.wait()
    second.wait()
    width = rows_ref.shape[1]
    for slot in range(4):
        offset, length = meta_ref[slot], meta_ref[4 + slot]
        for dst, flip in ((own_ref, 0), (far_ref, 2)):
            start = (here ^ flip) * 128

            @pl.loop(0, 8)
            def _(i):
                position = start + i * 16
                row = pl.multiple_of(jnp.minimum(offset + position, CAP - 16), 16)
                keep = lax.broadcasted_iota(jnp.int32, (16, width), 0) + position < length
                part = rows_ref[pl.ds(row, 16), :].astype(F32)
                dst[slot, pl.ds(pl.multiple_of(i * 16, 16), 16), :] = jnp.where(
                    keep, part, 0.0
                ).astype(BF)


def unpack(meta, mine, other):
    width = mine.shape[1]
    shape = jax.ShapeDtypeStruct((4, 128, width), BF)
    return pl.pallas_call(
        _unpack_kernel,
        out_shape=(shape, shape),
        in_specs=[SMEM_SPEC, ANY_SPEC, ANY_SPEC],
        out_specs=(VMEM_SPEC, VMEM_SPEC),
        scratch_shapes=[pltpu.VMEM((CAP, width), BF), pltpu.SemaphoreType.DMA((2,))],
        compiler_params=pltpu.CompilerParams(vmem_limit_bytes=12 << 20),
        cost_estimate=LIGHT,
        name="unpack",
    )(meta, mine, other)


def _attend_kernel(meta_ref, qkv_ref, ctx_ref, lse_ref):
    ctx_ref[...] = jnp.zeros_like(ctx_ref)
    width = ctx_ref.shape[1]
    part = width // 2

    def one(slot, blocks):
        span = blocks * 128
        offset = pl.multiple_of(meta_ref[slot], 16)
        length = meta_ref[4 + slot]
        rows = pl.ds(offset, span)
        key_id = lax.broadcasted_iota(jnp.int32, (span, 1), 0)
        key_bias = jnp.where(key_id < length, 0.0, -1e30)

        @pl.loop(0, width // 128)
        def _(pair):
            lane0 = pl.multiple_of((pair // 2) * (3 * part) + (pair % 2) * 128, 128)
            keys = qkv_ref[rows, pl.ds(pl.multiple_of(part + lane0, 128), 128)]
            values = qkv_ref[rows, pl.ds(pl.multiple_of(2 * part + lane0, 128), 128)]
            values_t = values.astype(F32).T.astype(BF)
            for first in range(0, span, 256):
                step = min(span - first, 256)
                queries = qkv_ref[
                    pl.ds(pl.multiple_of(offset + first, 16), step), pl.ds(lane0, 128)
                ]
                queries = queries * jnp.asarray(HEAD_SIZE**-0.5, BF)
                lane = lax.broadcasted_iota(jnp.int32, (step, 128), 1)
                parts = []
                for half in range(2):
                    picked = jnp.where((lane >= 64) == (half == 1), queries, jnp.zeros_like(queries))
                    scores = mm_cols(keys, picked)
                    scores = scores + key_bias
                    highest = jnp.max(scores, axis=0, keepdims=True)
                    expo = jnp.exp(scores - highest)
                    total = jnp.sum(expo, axis=0, keepdims=True)
                    weighted = mm(values_t[64 * half : 64 * half + 64], expo.astype(BF))
                    parts.append(weighted * (1.0 / total))
                    lse_ref[slot, pair * 2 + half, :, first : first + step] = highest + jnp.log(total)
                mixed = jnp.concatenate(parts, axis=0).T
                out_lane = pl.multiple_of(pair * 128, 128)
                ctx_ref[pl.ds(pl.multiple_of(offset + first, 16), step), pl.ds(out_lane, 128)] = (
                    mixed.astype(BF)
                )

    @pl.loop(0, 4)
    def _(slot):
        for blocks in range(1, 5):
            pl.when(meta_ref[8 + slot] == blocks)(functools.partial(one, slot, blocks))


def attend(meta, qkv):
    width = qkv.shape[1] // 3
    return pl.pallas_call(
        _attend_kernel,
        out_shape=(
            jax.ShapeDtypeStruct((CAP, width), BF),
            jax.ShapeDtypeStruct((4, width // HEAD_SIZE, 1, 512), F32),
        ),
        in_specs=[SMEM_SPEC, VMEM_SPEC],
        out_specs=(VMEM_SPEC, VMEM_SPEC),
        compiler_params=pltpu.CompilerParams(vmem_limit_bytes=12 << 20),
        cost_estimate=LIGHT,
        name="attend",
    )(meta, qkv)


def _attend_back_kernel(block, meta_ref, qkv_ref, lse_ref, gctx_ref, out_ref):
    out_ref[...] = jnp.zeros_like(out_ref)
    part = out_ref.shape[1] // 3

    def one(slot, blocks):
        span = blocks * 128
        offset = pl.multiple_of(meta_ref[slot], 16)
        length = meta_ref[4 + slot]
        rows = pl.ds(offset, span)
        key_id = lax.broadcasted_iota(jnp.int32, (span, 1), 0)
        key_bias = jnp.where(key_id < length, 0.0, -1e30)

        @pl.loop(0, part // 128)
        def _(turn):
            pair = block * (part // 128) + turn
            out_lane = pl.multiple_of(turn * 128, 128)
            base = block * 3 * part
            lane0 = pl.multiple_of(base + turn * 128, 128)
            ctx_lane = pl.multiple_of(block * part + turn * 128, 128)
            keys = qkv_ref[rows, pl.ds(pl.multiple_of(part + lane0, 128), 128)]
            values = qkv_ref[rows, pl.ds(pl.multiple_of(2 * part + lane0, 128), 128)]
            keys_t = keys.astype(F32).T.astype(BF)
            grad_keys = jnp.zeros((span, 128), F32)
            grad_values = jnp.zeros((span, 128), F32)
            for first in range(0, span, 256):
                step = min(span - first, 256)
                here = pl.ds(pl.multiple_of(offset + first, 16), step)
                queries = qkv_ref[here, pl.ds(lane0, 128)] * jnp.asarray(HEAD_SIZE**-0.5, BF)
                grad_ctx = gctx_ref[here, pl.ds(ctx_lane, 128)]
                lane = lax.broadcasted_iota(jnp.int32, (step, 128), 1)
                row = lax.broadcasted_iota(jnp.int32, (step, 128), 0) + first
                grad_ctx = jnp.where(row < length, grad_ctx, jnp.zeros_like(grad_ctx))
                parts = []
                for half in range(2):
                    side = (lane >= 64) == (half == 1)
                    picked = jnp.where(side, queries, jnp.zeros_like(queries))
                    picked_grad = jnp.where(side, grad_ctx, jnp.zeros_like(grad_ctx))
                    scores = mm_cols(keys, picked)
                    log_total = lse_ref[slot, pair * 2 + half, :, first : first + step]
                    probs = jnp.exp(scores - log_total + key_bias)
                    grad_values = grad_values + mm(probs.astype(BF), picked_grad)
                    grad_probs = mm_cols(values, picked_grad)
                    inner = jnp.sum(probs * grad_probs, axis=0, keepdims=True)
                    grad_scores = (probs * (grad_probs - inner)).astype(BF)
                    grad_keys = grad_keys + mm(grad_scores, picked)
                    parts.append(mm(keys_t[64 * half : 64 * half + 64], grad_scores))
                grad_queries = jnp.concatenate(parts, axis=0).T * HEAD_SIZE**-0.5
                out_ref[here, pl.ds(out_lane, 128)] = grad_queries.astype(BF)
            key_lane = pl.multiple_of(part + out_lane, 128)
            value_lane = pl.multiple_of(2 * part + out_lane, 128)
            out_ref[rows, pl.ds(key_lane, 128)] = grad_keys.astype(BF)
            out_ref[rows, pl.ds(value_lane, 128)] = grad_values.astype(BF)

    @pl.loop(0, 4)
    def _(slot):
        for blocks in range(1, 5):
            pl.when(meta_ref[8 + slot] == blocks)(functools.partial(one, slot, blocks))


def attend_back(meta, qkv, lse, grad_ctx, block):
    return pl.pallas_call(
        functools.partial(_attend_back_kernel, block),
        out_shape=jax.ShapeDtypeStruct((qkv.shape[0], qkv.shape[1] // 2), BF),
        in_specs=[SMEM_SPEC] + [VMEM_SPEC] * 3,
        out_specs=VMEM_SPEC,
        compiler_params=pltpu.CompilerParams(vmem_limit_bytes=12 << 20),
        cost_estimate=LIGHT,
        name="attend_back",
    )(meta, qkv, lse, grad_ctx)


def _assemble_kernel(kinds, meta_ref, *refs):
    out_ref = refs[-1]
    here, core = meta_ref[12], meta_ref[13]
    rows, columns = refs[0].shape
    block = columns // (4 * kinds)
    for flip, src in zip((0, 2, 1, 3), refs[:4]):
        place = pl.ds(pl.multiple_of((here ^ flip) * rows, 16), rows)
        for kind in range(kinds):
            for side in range(2):
                lane = pl.multiple_of((kind * 4 + core + 2 * side) * block, 128)
                spot = (side * kinds + kind) * block
                out_ref[place, spot : spot + block] = src[:, pl.ds(lane, block)]


def assemble(meta, kinds, own, from_x, from_core, from_both):
    rows, columns = own.shape
    return pl.pallas_call(
        functools.partial(_assemble_kernel, kinds),
        out_shape=jax.ShapeDtypeStruct((4 * rows, columns // 2), BF),
        in_specs=[SMEM_SPEC] + [VMEM_SPEC] * 4,
        out_specs=VMEM_SPEC,
        compiler_params=pltpu.CompilerParams(vmem_limit_bytes=12 << 20),
        cost_estimate=LIGHT,
        name="assemble",
    )(meta, own, from_x, from_core, from_both)


def _spread_kernel(kinds, sides, meta_ref, *refs):
    out_ref = refs[-1]
    core = meta_ref[13]
    block = out_ref.shape[1] // (4 * kinds)
    for flip in range(2):
        for kind in range(kinds):
            for side in range(2):
                lane = pl.multiple_of((kind * 4 + (core ^ flip) + 2 * side) * block, 128)
                if sides:
                    src, spot = refs[2 * side + flip], kind * block
                else:
                    src, spot = refs[flip], (side * kinds + kind) * block
                out_ref[:, pl.ds(lane, block)] = src[:, spot : spot + block].astype(F32)


def spread_columns(meta, kinds, columns, *blocks):
    return pl.pallas_call(
        functools.partial(_spread_kernel, kinds, len(blocks) == 4),
        out_shape=jax.ShapeDtypeStruct((blocks[0].shape[0], columns), F32),
        in_specs=[SMEM_SPEC] + [VMEM_SPEC] * len(blocks),
        out_specs=VMEM_SPEC,
        compiler_params=pltpu.CompilerParams(vmem_limit_bytes=12 << 20),
        cost_estimate=LIGHT,
        name="spread_columns",
    )(meta, *blocks)


def _stack_kernel(place, meta_ref, mine_ref, other_ref, out_ref):
    spot = meta_ref[place]
    rows = mine_ref.shape[0]
    mine_at = pl.multiple_of(spot * rows, 16)
    other_at = pl.multiple_of((1 - spot) * rows, 16)
    out_ref[pl.ds(mine_at, rows), :] = mine_ref[...].astype(out_ref.dtype)
    out_ref[pl.ds(other_at, rows), :] = other_ref[...].astype(out_ref.dtype)


def stack_rows(meta, place, mine, other, kind=F32):
    return pl.pallas_call(
        functools.partial(_stack_kernel, place),
        out_shape=jax.ShapeDtypeStruct((2 * mine.shape[0], mine.shape[1]), kind),
        in_specs=[SMEM_SPEC] + [VMEM_SPEC] * 2,
        out_specs=VMEM_SPEC,
        compiler_params=pltpu.CompilerParams(vmem_limit_bytes=12 << 20),
        cost_estimate=LIGHT,
        name="stack_rows",
    )(meta, mine, other)


def _merge_kernel(meta_ref, own_ref, up_ref, mine_ref, other_ref, down_out, up_out):
    here_y, chip = meta_ref[14], meta_ref[18]
    rows, share = own_ref.shape[0], own_ref.shape[0] // 8
    lines = up_ref.shape[0] // 4
    width = own_ref.shape[1]
    size = mine_ref.shape[0] // 4
    down_out[pl.ds(pl.multiple_of(chip * rows, 16), rows), :] = own_ref[...]
    up_out[4 * lines :, :] = up_ref[...]
    for src, y in ((mine_ref, here_y), (other_ref, 1 - here_y)):
        for turn in range(4):
            at = (1 - chip) * rows + (y * 4 + turn) * share
            down_out[pl.ds(pl.multiple_of(at, 16), share), :] = src[
                turn * size : turn * size + share, :
            ]
            line = pl.multiple_of((y * 4 + turn) * (lines // 2), 16)
            for column in range(4):
                first = turn * size + share + column * (lines // 2)
                up_out[pl.ds(line, lines // 2), column * width : (column + 1) * width] = src[
                    first : first + lines // 2, :
                ]


def merge_shares(meta, w_down, far_up_high, mine, other):
    rows, width = w_down.shape
    return pl.pallas_call(
        _merge_kernel,
        out_shape=(
            jax.ShapeDtypeStruct((2 * rows, width), BF),
            jax.ShapeDtypeStruct((2 * far_up_high.shape[0], far_up_high.shape[1]), BF),
        ),
        in_specs=[SMEM_SPEC] + [VMEM_SPEC] * 4,
        out_specs=(VMEM_SPEC, VMEM_SPEC),
        compiler_params=pltpu.CompilerParams(vmem_limit_bytes=12 << 20),
        cost_estimate=LIGHT,
        name="merge_shares",
    )(meta, w_down, far_up_high, mine, other)


TILE = 256


def _tiles(meta_ref, count_at, out_refs, body):
    rows = out_refs[0].shape[0]
    used = jnp.minimum((meta_ref[count_at] + TILE - 1) // TILE, rows // TILE)

    @pl.loop(0, used)
    def _(tile):
        body(pl.ds(pl.multiple_of(tile * TILE, TILE), TILE))

    @pl.loop(used, rows // TILE)
    def _(tile):
        for out_ref in out_refs:
            place = pl.ds(pl.multiple_of(tile * TILE, TILE), TILE)
            out_ref[place, :] = jnp.zeros((TILE, out_ref.shape[1]), out_ref.dtype)


def _up_kernel(count_at, meta_ref, low_ref, weight_ref, bias_ref, act_ref, slope_ref):
    width = act_ref.shape[1]
    step = 512

    def body(place):
        @pl.loop(0, width // step)
        def _(turn):
            lanes = pl.ds(pl.multiple_of(turn * step, step), step)
            pre = mm(low_ref[place, :], weight_ref[:, lanes]) + bias_ref[:, lanes]
            cdf = 0.5 * (1.0 + lax.erf(pre * np.float32(0.5**0.5)))
            slope = cdf + pre * jnp.exp(-0.5 * pre * pre) * np.float32((2 * np.pi) ** -0.5)
            act_ref[place, lanes] = (pre * cdf).astype(BF)
            slope_ref[place, lanes] = slope.astype(BF)

    _tiles(meta_ref, count_at, (act_ref, slope_ref), body)


def up_product(meta, count_at, low, weight, bias):
    shape = jax.ShapeDtypeStruct((low.shape[0], weight.shape[1]), BF)
    return pl.pallas_call(
        functools.partial(_up_kernel, count_at),
        out_shape=(shape, shape),
        in_specs=[SMEM_SPEC] + [VMEM_SPEC] * 3,
        out_specs=(VMEM_SPEC, VMEM_SPEC),
        compiler_params=pltpu.CompilerParams(vmem_limit_bytes=12 << 20),
        cost_estimate=LIGHT,
        name="up_product",
    )(meta, low, weight, bias)


def _rows_kernel(count_at, turned, terms, scaled, meta_ref, *refs):
    lefts, rights = refs[:terms], refs[terms : 2 * terms]
    out_ref = refs[2 * terms + scaled]
    width = out_ref.shape[1]
    step = min(512, width)

    def body(place):
        @pl.loop(0, width // step)
        def _(turn):
            lanes = pl.ds(pl.multiple_of(turn * step, step), step)
            total = None
            for left_ref, right_ref in zip(lefts, rights):
                left = left_ref[place, :]
                if turned:
                    term = mm_cols(left, right_ref[lanes, :])
                else:
                    term = mm(left, right_ref[:, lanes])
                total = term if total is None else total + term
            if scaled:
                total = total * refs[2 * terms][place, lanes].astype(F32)
            out_ref[place, lanes] = total.astype(out_ref.dtype)

    _tiles(meta_ref, count_at, (out_ref,), body)


def rows_product(meta, count_at, lefts, rights, turned, kind, scale=None):
    width = rights[0].shape[0] if turned else rights[0].shape[1]
    args = [*lefts, *rights] + ([] if scale is None else [scale])
    return pl.pallas_call(
        functools.partial(_rows_kernel, count_at, turned, len(lefts), int(scale is not None)),
        out_shape=jax.ShapeDtypeStruct((lefts[0].shape[0], width), kind),
        in_specs=[SMEM_SPEC] + [VMEM_SPEC] * len(args),
        out_specs=VMEM_SPEC,
        compiler_params=pltpu.CompilerParams(vmem_limit_bytes=12 << 20),
        cost_estimate=LIGHT,
        name="rows_product",
    )(meta, *args)


def _grad_kernel(terms, meta_ref, at_ref, *refs):
    lefts, rights = refs[:terms], refs[terms : 2 * terms]
    out_ref, turned_ref = refs[2 * terms :]
    count, width = out_ref.shape
    first = 0
    for left_ref in lefts:
        rows = left_ref.shape[0]
        piece = left_ref[:, pl.ds(pl.multiple_of(at_ref[0], 128), count)]
        turned_ref[:, first : first + rows] = piece.astype(F32).T.astype(BF)
        first += rows
    step = 256

    @pl.loop(0, width // step)
    def _(turn):
        lanes = pl.ds(pl.multiple_of(turn * step, step), step)
        total, start = None, 0
        for right_ref in rights:
            rows = right_ref.shape[0]
            term = mm(turned_ref[:, start : start + rows], right_ref[:, lanes])
            total = term if total is None else total + term
            start += rows
        out_ref[:, lanes] = total.astype(out_ref.dtype)


def grad_product(meta, lefts, rights, start, count, kind):
    rows = sum(left.shape[0] for left in lefts)
    args = [*lefts, *rights]
    return pl.pallas_call(
        functools.partial(_grad_kernel, len(lefts)),
        out_shape=jax.ShapeDtypeStruct((count, rights[0].shape[1]), kind),
        in_specs=[SMEM_SPEC, SMEM_SPEC] + [VMEM_SPEC] * len(args),
        out_specs=VMEM_SPEC,
        scratch_shapes=[pltpu.VMEM((count, rows), BF)],
        compiler_params=pltpu.CompilerParams(vmem_limit_bytes=12 << 20),
        cost_estimate=LIGHT,
        name="grad_product",
    )(meta, jnp.asarray(start, jnp.int32)[None], *args)


def normed(inputs):
    average = jnp.mean(inputs, axis=-1, keepdims=True)
    centered = inputs - average
    variance = jnp.mean(centered * centered, axis=-1, keepdims=True)
    rstd = lax.rsqrt(variance + EPS)
    return centered * rstd, rstd


def norm_back(unit, rstd, grad, gain):
    scaled = grad * gain
    return (
        scaled
        - jnp.mean(scaled, axis=-1, keepdims=True)
        - unit * jnp.mean(scaled * unit, axis=-1, keepdims=True)
    ) * rstd


SWAP_X = [(i, i ^ 2) for i in range(4)]
SWAP_Y = [(i, i ^ 1) for i in range(8)]
SWAP_Z1 = [(i, i ^ 2) for i in range(8)]
SWAP_Z2 = [(i, i ^ 4) for i in range(8)]
AT_Y, AT_Z1, AT_Z2 = 14, 16, 17
MINE, OTHER = 19, 20


def moved(name, value, axis, pairs):
    with jax.named_scope(name):
        return lax.ppermute(value, axis, pairs)


class SeqSum:
    def __init__(self, name, meta, group_count):
        self.name, self.meta, self.whole = name, meta, group_count == 8
        index = lax.axis_index("seq")
        self.bits = {AT_Y: index % 2, AT_Z1: index // 2 % 2, AT_Z2: index // 4 % 2}

    def send(self, step, value, axis, pairs):
        self.token = value
        self.arrived = moved(f"{self.name}_{step}", value, axis, pairs)

    def start_x(self, far, own):
        self.kept = own[None]
        self.send("x", far.astype(BF), "head", SWAP_X)

    def start_y(self, far, kept):
        self.kept = kept
        self.send("y", far.astype(BF), "seq", SWAP_Y)

    def added(self, gates):
        arrived = after(self.arrived, *gates).astype(F32)
        self.kept = self.kept + arrived.reshape(self.kept.shape)

    def split(self, step, place, pairs):
        blocks, rows, columns = self.kept.shape
        halves = self.kept.reshape(blocks, 2, rows // 2, columns)
        bit = self.bits[place]
        self.kept = lax.dynamic_index_in_dim(halves, bit, 1, keepdims=False)
        sent = lax.dynamic_index_in_dim(halves, 1 - bit, 1, keepdims=False)
        self.send(step, sent.astype(BF).reshape(-1, columns), "seq", pairs)

    def step_y(self, *gates):
        self.added(gates)
        if self.whole:
            self.split("y", AT_Y, SWAP_Y)
            return
        count = self.kept.shape[1] // 2
        halves = lax.psum(self.kept[0], "seq").astype(BF).reshape(2, count, -1)
        bit = self.bits[AT_Y]
        self.mine = self.token = lax.dynamic_index_in_dim(halves, bit, 0, keepdims=False)
        self.arrived = lax.dynamic_index_in_dim(halves, 1 - bit, 0, keepdims=False)

    def step_z1(self, *gates):
        if self.whole:
            self.added(gates)
            self.split("z1", AT_Z1, SWAP_Z1)

    def step_z2(self, *gates):
        if self.whole:
            self.added(gates)
            self.split("z2", AT_Z2, SWAP_Z2)

    def step_x(self, *gates):
        if self.whole:
            self.added(gates)
            far = self.kept[1]
            self.kept = self.kept[:1]
            self.send("x", far.astype(BF), "head", SWAP_X)

    def back_z2(self, *gates):
        if self.whole:
            self.added(gates)
            self.mine = self.kept[0].astype(BF)
            self.send("back_z2", self.mine, "seq", SWAP_Z2)

    def joined(self, place, gates):
        arrived = after(self.arrived, *gates)
        self.mine = stack_rows(self.meta, place, self.mine, arrived, BF)

    def back_z1(self, *gates):
        if self.whole:
            self.joined(AT_Z2, gates)
            self.send("back_z1", self.mine, "seq", SWAP_Z1)

    def back_y(self, *gates):
        if self.whole:
            self.joined(AT_Z1, gates)
            self.send("back_y", self.mine, "seq", SWAP_Y)

    def halves(self, *gates):
        return self.mine, after(self.arrived, *gates)


def on_device(
    tokens,
    cotangent,
    lengths,
    seq_order,
    w_qkv,
    w_out,
    w_up,
    w_down,
    bias_q,
    bias_v,
    bias_out,
    bias_up,
    bias_down,
    gain_attn,
    shift_attn,
    gain_mlp,
    shift_mlp,
):
    group_count = lax.axis_size("seq")
    group_id = lax.axis_index("seq")
    here = lax.axis_index("head").astype(jnp.int32)
    core, chip = here % 2, here // 2
    slots, span_rows, width = tokens.shape
    part = width // 4
    ff_part = w_up.shape[1] // 4
    offsets = [k * group_count // slots for k in range(slots)]
    offsets[1], offsets[-1] = 1, group_count - 1
    swap_x = [(i, i ^ 2) for i in range(4)]
    swap_core = [(i, i ^ 1) for i in range(4)]

    def over_x(value, name="x"):
        with jax.named_scope(name):
            return lax.ppermute(value, "head", swap_x)

    def over_core(value, name="core"):
        with jax.named_scope(name):
            return lax.ppermute(value, "head", swap_core)

    slot_ids = jnp.arange(slots, dtype=jnp.int32)
    local_ids = group_id * slots + slot_ids
    given_slot = lax.dynamic_slice_in_dim(seq_order, group_id * slots, slots) % slots
    given_of_slot = jnp.sum(
        jnp.where(given_slot[None, :] == slot_ids[:, None], slot_ids[None, :], 0), axis=1
    )
    matches = seq_order[None, :] == local_ids[:, None]
    slot_lens = jnp.sum(jnp.where(matches, lengths[None, :], 0), axis=1)
    aligned = (slot_lens + 15) // 16 * 16
    choices = np.zeros((35, slots), np.int32)
    for row, picks in enumerate(itertools.combinations(range(1, slots), 3)):
        choices[row, [0, *picks]] = 1
    sides = jnp.sum(choices * aligned[None, :], axis=1)
    larger = jnp.maximum(sides, jnp.sum(aligned) - sides)
    squares = jnp.sum(choices * (slot_lens * slot_lens)[None, :], axis=1)
    heavier = jnp.maximum(squares, jnp.sum(slot_lens * slot_lens) - squares)
    score = larger * 1024 + heavier // 4096
    best = jnp.min(score)
    chosen = jnp.argmax(score == best)
    in_first = jnp.sum(
        jnp.where(jnp.arange(35)[:, None] == chosen, choices, 0), axis=0, dtype=jnp.int32
    )
    is_own = jnp.where(chip == 0, in_first, 1 - in_first)
    before = np.tril(np.ones((slots, slots), np.int32), -1)
    rank_own = jnp.sum(before * is_own[None, :], axis=1)
    rank_far = jnp.sum(before * (1 - is_own)[None, :], axis=1)
    list_pos = jnp.where(is_own == 1, rank_own, 4 + rank_far).astype(jnp.int32)
    at_place = list_pos[None, :] == slot_ids[:, None]
    slot_at = jnp.sum(jnp.where(at_place, slot_ids[None, :], 0), axis=1)
    own_lens = jnp.sum(jnp.where(at_place, slot_lens[None, :], 0), axis=1)[:4]
    own_aligned = (own_lens + 15) // 16 * 16
    own_offsets = jnp.sum(np.tril(np.ones((4, 4), np.int32), -1) * own_aligned[None, :], axis=1)
    total_rows = jnp.sum(own_aligned)
    meta = jnp.concatenate(
        [
            own_offsets,
            own_lens,
            (own_lens + 127) // 128,
            here[None],
            core[None],
            (group_id % 2)[None],
            (group_id // 2)[None],
            (group_id // 2 % 2)[None],
            (group_id // 4 % 2)[None],
            chip[None],
            jnp.clip(total_rows - core * HALF, 0, HALF)[None],
            jnp.clip(total_rows - (1 - core) * HALF, 0, HALF)[None],
            jnp.zeros((3,), jnp.int32),
        ]
    ).astype(jnp.int32)
    row_ids = core * HALF + jnp.arange(HALF, dtype=jnp.int32)
    row_keep = jnp.any(
        (row_ids[:, None] >= own_offsets[None, :])
        & (row_ids[:, None] < (own_offsets + own_lens)[None, :]),
        axis=1,
        keepdims=True,
    )

    def swapped(own, far):
        return own, far, over_core(own), over_core(far)

    if group_count == slots:
        spots = (group_id - given_slot) % slots
        sent_tokens = route(tokens, spots)
    else:
        sent_tokens = route(tokens, given_slot.astype(jnp.int32))
    small_here = jnp.concatenate(
        [
            bias_q,
            bias_v,
            bias_out,
            bias_down,
            gain_attn,
            shift_attn,
            gain_mlp,
            shift_mlp,
            bias_up,
        ]
    )[None, :]
    small_here = after(small_here, sent_tokens)
    small_core = over_core(small_here)

    def ordered(first, second, is_low):
        return jnp.concatenate(
            [jnp.where(is_low, first, second), jnp.where(is_low, second, first)], axis=0
        )

    small_pair = ordered(small_here, small_core, core == 0)
    small = ordered(small_pair, over_x(small_pair), chip == 0).astype(F32)

    def vector(place):
        return small[:, place * part : (place + 1) * part].reshape(1, width)

    def local_columns(rows):
        return jnp.concatenate(
            [
                lax.dynamic_index_in_dim(rows, core, 0, keepdims=False),
                lax.dynamic_index_in_dim(rows, core + 2, 0, keepdims=False),
            ]
        )

    query_bias = local_columns(small[:, 0:part])
    value_bias = local_columns(small[:, part : 2 * part])
    up_bias = local_columns(small[:, 8 * part :])[None, :]
    out_bias, down_bias = vector(2), vector(3)
    attn_gain, attn_shift, mlp_gain, mlp_shift = vector(4), vector(5), vector(6), vector(7)
    no_bias = jnp.zeros((part,), F32)
    joint_bias = jnp.concatenate(
        [query_bias[:part], no_bias, value_bias[:part], query_bias[part:], no_bias, value_bias[part:]]
    )[None, :]


    first_weights = over_x(
        after(jnp.concatenate([w_qkv, w_out], axis=1), sent_tokens), "x_first_weights"
    )
    if group_count == 8:
        share = w_down.shape[0] // 8
        turn = (group_id % 2) * 4 + group_id // 4 + 2 * (group_id // 2 % 2)
        lines = w_up.shape[0] // 16
        up_lines = lax.dynamic_slice_in_dim(w_up, turn * lines, lines, axis=0)
        mixed = jnp.concatenate(
            [lax.dynamic_slice_in_dim(w_down, turn * share, share, axis=0)]
            + jnp.split(up_lines, 4, axis=1),
            axis=0,
        )
        mixed = over_x(after(mixed, sent_tokens), "x_shares")
    else:
        mixed = small
    if group_count == slots:
        got = lax.all_to_all(sent_tokens, "seq", split_axis=0, concat_axis=0, tiled=True)
        came = (slot_ids - group_id) % slots
        placed = jnp.sum(
            jnp.where(came[:, None] == slot_ids[None, :], list_pos[None, :], 0), axis=1
        )
        lists = route(got, placed.astype(jnp.int32))
    else:
        arrived = [sent_tokens[0]]
        for k in range(1, slots):
            arrived.append(
                lax.ppermute(
                    sent_tokens[k],
                    "seq",
                    [(i, (i - offsets[k]) % group_count) for i in range(group_count)],
                )
            )
        lists = route(arrived, list_pos)

    def by_chip(own, far):
        return jnp.concatenate(
            [jnp.where(chip == 0, own, far), jnp.where(chip == 0, far, own)], axis=0
        )

    far_qkv, far_out = first_weights[:, : 3 * width], first_weights[:, 3 * width :]
    full_qkv = assemble(meta, 3, *swapped(w_qkv, far_qkv))
    full_out = by_chip(w_out, far_out)

    cot_lists = route(cotangent, list_pos)
    far_tokens = over_x(lists[4:], "x_tokens")
    if group_count == 8:
        pair = stack_rows(meta, AT_Z2, mixed, moved("share_z2", mixed, "seq", SWAP_Z2), BF)
        gate = four = stack_rows(meta, AT_Z1, pair, moved("share_z1", pair, "seq", SWAP_Z1), BF)
    else:
        gate = far_tokens
    rows_in = pack(meta, *swapped(lists[:4], after(far_tokens, gate, cot_lists)))
    w_up_later, _ = lax.optimization_barrier((w_up, far_tokens))
    if group_count == 8:
        far_up_high = over_x(w_up_later[part // 2 :], "x_up_weight")
        other_four = moved("share_y", four, "seq", SWAP_Y)
    else:
        far_up = over_x(w_up_later, "x_up_weight")
        full_down = by_chip(w_down, over_x(w_down))
        cot_far_in = cot_lists[4:]
    def halves(value):
        return (
            lax.dynamic_slice_in_dim(value, core * HALF, HALF, axis=0),
            lax.dynamic_slice_in_dim(value, (1 - core) * HALF, HALF, axis=0),
        )

    def in_order(mine, other):
        lower = jnp.where(core == 0, mine, other)
        upper = jnp.where(core == 0, other, mine)
        return jnp.concatenate([lower, upper], axis=0)

    def core_sum(lefts_mine, lefts_other, rights, turned):
        arriving = over_core(rows_product(meta, OTHER, lefts_other, rights, turned, BF))
        return rows_product(meta, MINE, lefts_mine, rights, turned, F32) + arriving.astype(F32)

    qkv = (mm(rows_in, full_qkv) + joint_bias).astype(BF)
    context, lse = attend(meta, qkv)
    if group_count == 8:
        context, other_four, far_up_high = lax.optimization_barrier(
            (context, other_four, far_up_high)
        )
        cot_far_in = after(cot_lists[4:], far_up_high)
        full_down, far_up = merge_shares(meta, w_down, far_up_high, four, other_four)
    full_up = assemble(meta, 1, *swapped(w_up, far_up))
    cot_arrived = over_x(cot_far_in, "x_cotangent")
    ctx_mine, ctx_other = halves(context)
    rows_mine, _ = halves(rows_in)
    resid_attn = (
        core_sum([ctx_mine], [ctx_other], [full_out], False) + rows_mine.astype(F32) + out_bias
    )
    unit_attn, rstd_attn = normed(resid_attn)
    hidden = unit_attn * attn_gain + attn_shift
    low_mine = hidden.astype(BF)
    low_other = over_core(low_mine)

    act_mine, slope_mine = up_product(meta, MINE, low_mine, full_up, up_bias)
    act_other, slope_other = up_product(meta, OTHER, low_other, full_up, up_bias)
    cot_rows = pack(meta, *swapped(cot_lists[:4], after(cot_arrived, act_mine)))
    resid_mlp = core_sum([act_mine], [act_other], [full_down], False) + hidden + down_bias
    unit_mlp, rstd_mlp = normed(resid_mlp)
    final_mine = (unit_mlp * mlp_gain + mlp_shift).astype(BF)

    cot_mine, _ = halves(cot_rows)
    grad_y = jnp.where(row_keep, cot_mine.astype(F32), 0.0)
    grad_mlp2 = norm_back(unit_mlp, rstd_mlp, grad_y, mlp_gain)
    sum_gain_mlp = jnp.sum(grad_y * unit_mlp, axis=0)
    sum_shift_mlp = jnp.sum(grad_y, axis=0)
    branch_mine = grad_mlp2.astype(BF)
    branch_other = over_core(branch_mine)
    sum_bias_down = jnp.sum(branch_mine, axis=0, dtype=F32)
    def grads(lefts, rights, start, count, kind=F32):
        return grad_product(meta, lefts, rights, start, count, kind)

    down_sum = SeqSum("down", meta, group_count)
    acts, branches = [act_mine, act_other], [branch_mine, branch_other]
    if group_count == 8:
        here_y = group_id % 2
        count = ff_part // 2

        def down_term(half, kind):
            return jnp.stack(
                [
                    grads(acts, branches, side * ff_part + half * count, count, kind)
                    for side in (chip, 1 - chip)
                ]
            )

        down_sum.start_y(down_term(1 - here_y, BF).reshape(-1, width), down_term(here_y, F32))
    else:
        down_sum.start_x(
            *(grads(acts, branches, side * ff_part, ff_part) for side in (1 - chip, chip))
        )
    branch_mine, branch_other, _ = lax.optimization_barrier(
        (branch_mine, branch_other, down_sum.token)
    )
    pre_mine = rows_product(meta, MINE, [branch_mine], [full_down], True, BF, slope_mine)
    pre_other = rows_product(meta, OTHER, [branch_other], [full_down], True, BF, slope_other)
    sum_bias_up = jnp.sum(pre_mine, axis=0, dtype=F32) + jnp.sum(pre_other, axis=0, dtype=F32)

    lows, pres = [low_mine, low_other], [pre_mine, pre_other]
    up_far, up_own = (
        grads(lows, pres, side * 2 * part, 2 * part, kind)
        for side, kind in ((1 - chip, BF), (chip, F32))
    )
    up_sum = SeqSum("up", meta, group_count)
    up_sum.start_x(up_far, up_own)
    pre_mine, pre_other, _ = lax.optimization_barrier((pre_mine, pre_other, up_sum.token))
    gh_other = rows_product(meta, OTHER, [pre_other], [full_up], True, BF)
    gh_arrived = over_core(gh_other)
    if group_count == 8:
        down_sum.step_z1(gh_other)
    else:
        down_sum.step_y(gh_other)
    pre_mine = after(pre_mine, down_sum.token)
    grad_hidden = rows_product(meta, MINE, [pre_mine], [full_up], True, F32)
    grad_hidden = grad_hidden + gh_arrived.astype(F32) + grad_mlp2

    grad_attn2 = norm_back(unit_attn, rstd_attn, grad_hidden, attn_gain)
    sum_gain_attn = jnp.sum(grad_hidden * unit_attn, axis=0)
    sum_shift_attn = jnp.sum(grad_hidden, axis=0)
    attn_mine = grad_attn2.astype(BF)
    attn_other = over_core(attn_mine)
    sum_bias_out = jnp.sum(attn_mine, axis=0, dtype=F32)
    half_width = width // 2

    def out_term(side, kind):
        term = grads([ctx_mine, ctx_other], [attn_mine, attn_other], side * part, part, kind)
        return jnp.concatenate([term[:, :half_width], term[:, half_width:]], axis=0)

    out_far, out_own = out_term(1 - chip, BF), out_term(chip, F32)
    down_sum.step_z2(out_own, out_far)
    up_sum.step_y(down_sum.token)
    attn_mine, attn_other, _ = lax.optimization_barrier((attn_mine, attn_other, up_sum.token))
    grad_ctx = in_order(
        rows_product(meta, MINE, [attn_mine], [full_out], True, BF),
        rows_product(meta, OTHER, [attn_other], [full_out], True, BF),
    )
    y_own, y_far = unpack(meta, final_mine, over_core(after(final_mine, gh_other)))
    y_arrived = over_x(y_far, "x_activations")
    grad_first = attend_back(meta, qkv, lse, after(grad_ctx, y_far), 0)
    down_sum.step_x(grad_first)
    up_sum.step_z1(down_sum.token)
    grad_first = after(grad_first, up_sum.token)

    first_far, first_own = (
        jnp.concatenate(
            [grads([rows_in], [grad_first], side * 2 * part, 2 * part, out.dtype), out], axis=1
        )
        for side, out in ((1 - chip, out_far), (chip, out_own))
    )
    first_sum = SeqSum("first", meta, group_count)
    first_sum.start_x(first_far, first_own)
    down_sum.back_z2(first_sum.token, first_own)
    grad_last = attend_back(meta, qkv, lse, after(grad_ctx, down_sum.token), 1)
    grad_last = after(grad_last, y_arrived)
    down_sum.back_z1(grad_last)
    up_sum.step_z2(down_sum.token)
    grad_last = after(grad_last, up_sum.token)

    qkv_blocks = [full_qkv[:, : 3 * part], full_qkv[:, 3 * part :]]
    first_mine, first_other = halves(grad_first)
    last_mine, last_other = halves(grad_last)
    gx_other = rows_product(meta, OTHER, [first_other, last_other], qkv_blocks, True, BF)
    gx_arrived = over_core(gx_other)
    gx_mine = rows_product(meta, MINE, [first_mine, last_mine], qkv_blocks, True, F32)
    gx_mine = (gx_mine + gx_arrived.astype(F32) + grad_attn2).astype(BF)
    gx_other = over_core(gx_mine)
    first_sum.step_y(gx_mine)
    down_sum.back_y(first_sum.token)
    up_sum.back_z2(down_sum.token)
    gx_mine = after(gx_mine, up_sum.token)
    gx_own, gx_far = unpack(meta, gx_mine, gx_other)
    gx_arrived = over_x(gx_far, "x_grad")
    up_sum.back_z1(gx_far)
    grad_last = after(grad_last, up_sum.token)
    last_far, last_own = (
        grads([rows_in], [grad_last], side * 2 * part, 2 * part, kind)
        for side, kind in ((1 - chip, BF), (chip, F32))
    )
    first_sums = jnp.sum(grad_first, axis=0, dtype=F32)
    last_sums = jnp.sum(grad_last, axis=0, dtype=F32)
    sum_bias_q = jnp.concatenate([first_sums[:part], last_sums[:part]])
    sum_bias_v = jnp.concatenate([first_sums[2 * part :], last_sums[2 * part :]])

    def whole_row(value):
        return value.reshape(4, part)

    def spread(value, size):
        result = jnp.zeros((4, size), F32)
        result = lax.dynamic_update_slice(result, value[None, :size], (core, 0))
        return lax.dynamic_update_slice(result, value[None, size:], (core + 2, 0))

    terms = jnp.concatenate(
        [
            spread(sum_bias_q, part),
            spread(sum_bias_v, part),
            whole_row(sum_bias_out),
            whole_row(sum_bias_down),
            whole_row(sum_gain_attn),
            whole_row(sum_shift_attn),
            whole_row(sum_gain_mlp),
            whole_row(sum_shift_mlp),
            spread(sum_bias_up, ff_part),
        ],
        axis=1,
    )

    def shard(value, flip):
        return lax.dynamic_index_in_dim(value, here ^ flip, 0, keepdims=True)

    from_core = over_core(jnp.concatenate([shard(terms, 1), shard(terms, 3)]).astype(BF))
    near_term = shard(terms, 0)[0] + from_core[0].astype(F32)
    far_term = shard(terms, 2)[0] + from_core[1].astype(F32)
    lanes = near_term.shape[0] // (2 * part)

    def as_columns(term):
        return jnp.pad(term.reshape(lanes, 2 * part).T, ((0, 0), (0, 128 - lanes)))

    last_far = jnp.concatenate([last_far, as_columns(far_term).astype(BF)], axis=1)
    last_own = jnp.concatenate([last_own, as_columns(near_term)], axis=1)
    last_sum = SeqSum("last", meta, group_count)
    last_sum.start_x(last_far, last_own)

    def my_block(mine, other):
        aligned_here = (group_id % 2) == core
        return jnp.where(aligned_here, mine, other), jnp.where(aligned_here, other, mine)

    def listed(own, arriving):
        parts = [own[k] for k in range(4)] + [arriving[k] for k in range(4)]
        return route(parts, slot_at.astype(jnp.int32))

    first_sum.step_z1(last_sum.token)
    grad_down = stack_rows(meta, AT_Y, *down_sum.halves(first_sum.token))
    back = listed(gx_own, after(gx_arrived, grad_down))
    returned = [back[0]]

    def send_back(count, *gates):
        for _ in range(count):
            k = len(returned)
            pairs = [(i, (i + offsets[k]) % group_count) for i in range(group_count)]
            returned.append(moved("return", after(back[k], *gates), "seq", pairs))

    send_back(2, grad_down)
    last_sum.step_y(back)
    up_sum.back_y(last_sum.token)
    first_sum.step_z2(up_sum.token, returned[1])
    send_back(1, first_sum.token)
    last_sum.step_z1(first_sum.token, returned[2])
    first_sum.back_z2(last_sum.token)
    send_back(1, last_sum.token)
    last_sum.step_z2(first_sum.token, returned[3])
    first_sum.back_z1(last_sum.token)
    send_back(1, last_sum.token)
    last_sum.back_z2(first_sum.token, returned[4])
    kept, sent = my_block(*up_sum.halves(last_sum.token))
    grad_w_up = spread_columns(meta, 1, 4 * ff_part, kept, over_core(sent))
    first_sum.back_y(kept)
    send_back(1, last_sum.token)
    last_sum.back_z1(first_sum.token, returned[5])
    send_back(1, first_sum.token)
    last_sum.back_y(last_sum.token, returned[6])
    first_halves = first_sum.halves(last_sum.token)
    last_halves = last_sum.halves(returned[7])
    activations = listed(y_own, after(y_arrived, last_sum.token))
    input_grad = route(returned, given_of_slot.astype(jnp.int32))

    blocks = []
    for mine, other in (first_halves, last_halves):
        kept, sent = my_block(mine[:, : 3 * part], other[:, : 3 * part])
        blocks += [kept, over_core(sent)]
    grad_w_qkv = spread_columns(meta, 3, 3 * width, *blocks)

    def by_y(mine, other, axis):
        lower = jnp.where(group_id % 2 == 0, mine, other)
        upper = jnp.where(group_id % 2 == 0, other, mine)
        return jnp.concatenate([lower, upper], axis=axis).astype(F32)

    grad_w_out = by_y(*(half[:, 3 * part :] for half in first_halves), 1)
    sums = by_y(*(half[:, 3 * part :] for half in last_halves), 0)[:, :lanes].T.reshape(-1)

    def piece(place):
        return sums[place * part : (place + 1) * part]

    return (
        activations,
        input_grad,
        grad_w_qkv,
        grad_w_out,
        grad_w_up,
        grad_down,
        piece(0),
        piece(1),
        piece(2),
        sums[8 * part :],
        piece(3),
        piece(4),
        piece(5),
        piece(6),
        piece(7),
    )


def solution(mesh):
    rows = P("seq", "head", None)
    weight, vector = P("head", None), P("head")
    in_specs = (rows, rows, P(), P()) + (weight,) * 4 + (vector,) * 9
    out_specs = (rows, rows) + (weight,) * 4 + (vector,) * 9
    return jax.shard_map(
        on_device, mesh=mesh, in_specs=in_specs, out_specs=out_specs, check_vma=False
    )
```

```python
import functools
import itertools

import jax
import jax.numpy as jnp
import numpy as np
from jax import lax
from jax.experimental import pallas as pl
from jax.experimental.pallas import tpu as pltpu
from jax.sharding import PartitionSpec as P

HEAD_SIZE = 64
CAP = 1536
HALF = CAP // 2
STEP = 512
EPS = 1e-12
BF = jnp.bfloat16
F32 = jnp.float32
VMEM_SPEC = pl.BlockSpec(memory_space=pltpu.VMEM)
SMEM_SPEC = pl.BlockSpec(memory_space=pltpu.SMEM)
ANY_SPEC = pl.BlockSpec(memory_space=pl.ANY)
LIGHT = pl.CostEstimate(flops=0, bytes_accessed=1024, transcendentals=0)


def after(value, *others):
    return lax.optimization_barrier((value, *others))[0]


def mm(left, right):
    return jnp.dot(left, right, preferred_element_type=F32)


def mm_rows(left, right):
    return lax.dot_general(left, right, (((0,), (0,)), ((), ())), preferred_element_type=F32)


def mm_cols(left, right):
    return lax.dot_general(left, right, (((1,), (1,)), ((), ())), preferred_element_type=F32)


def _route_kernel(count, single, dst_ref, *refs):
    out_ref = refs[-1]
    for k in range(count):
        out_ref[dst_ref[k]] = refs[0][k] if single else refs[k][...]


def route(blocks, dst):
    single = not isinstance(blocks, (list, tuple))
    args = [blocks] if single else list(blocks)
    count = args[0].shape[0] if single else len(args)
    shape = args[0].shape[1:] if single else args[0].shape
    return pl.pallas_call(
        functools.partial(_route_kernel, count, single),
        out_shape=jax.ShapeDtypeStruct((count,) + shape, args[0].dtype),
        in_specs=[SMEM_SPEC] + [VMEM_SPEC] * len(args),
        out_specs=VMEM_SPEC,
        compiler_params=pltpu.CompilerParams(vmem_limit_bytes=12 << 20),
        cost_estimate=LIGHT,
        name="route",
    )(dst, *args)


def _pack_kernel(meta_ref, a0, a1, a2, a3, out_ref):
    here = meta_ref[12]
    out_ref[...] = jnp.zeros_like(out_ref)
    for slot in range(4):
        offset, length = meta_ref[slot], meta_ref[4 + slot]
        for src, flip in ((a0, 0), (a1, 2), (a2, 1), (a3, 3)):
            start = (here ^ flip) * 128
            pieces = jnp.clip((length - start + 15) // 16, 0, 8)

            @pl.loop(0, pieces)
            def _(i):
                row = pl.multiple_of(offset + start + i * 16, 16)
                out_ref[pl.ds(row, 16), :] = src[slot, pl.ds(pl.multiple_of(i * 16, 16), 16), :]


def pack(meta, own, from_x, from_core, from_both):
    return pl.pallas_call(
        _pack_kernel,
        out_shape=jax.ShapeDtypeStruct((CAP, own.shape[-1]), own.dtype),
        in_specs=[SMEM_SPEC] + [VMEM_SPEC] * 4,
        out_specs=VMEM_SPEC,
        compiler_params=pltpu.CompilerParams(vmem_limit_bytes=12 << 20),
        cost_estimate=LIGHT,
        name="pack",
    )(meta, own, from_x, from_core, from_both)


def _unpack_kernel(meta_ref, mine_ref, other_ref, own_ref, far_ref, rows_ref, sems):
    here, core = meta_ref[12], meta_ref[13]
    first = pltpu.make_async_copy(
        mine_ref, rows_ref.at[pl.ds(pl.multiple_of(core * HALF, 16), HALF)], sems.at[0]
    )
    second = pltpu.make_async_copy(
        other_ref, rows_ref.at[pl.ds(pl.multiple_of((1 - core) * HALF, 16), HALF)], sems.at[1]
    )
    first.start()
    second.start()
    first.wait()
    second.wait()
    width = rows_ref.shape[1]
    for slot in range(4):
        offset, length = meta_ref[slot], meta_ref[4 + slot]
        for dst, flip in ((own_ref, 0), (far_ref, 2)):
            start = (here ^ flip) * 128

            @pl.loop(0, 8)
            def _(i):
                position = start + i * 16
                row = pl.multiple_of(jnp.minimum(offset + position, CAP - 16), 16)
                keep = lax.broadcasted_iota(jnp.int32, (16, width), 0) + position < length
                part = rows_ref[pl.ds(row, 16), :].astype(F32)
                dst[slot, pl.ds(pl.multiple_of(i * 16, 16), 16), :] = jnp.where(
                    keep, part, 0.0
                ).astype(BF)


def unpack(meta, mine, other):
    width = mine.shape[1]
    shape = jax.ShapeDtypeStruct((4, 128, width), BF)
    return pl.pallas_call(
        _unpack_kernel,
        out_shape=(shape, shape),
        in_specs=[SMEM_SPEC, ANY_SPEC, ANY_SPEC],
        out_specs=(VMEM_SPEC, VMEM_SPEC),
        scratch_shapes=[pltpu.VMEM((CAP, width), BF), pltpu.SemaphoreType.DMA((2,))],
        compiler_params=pltpu.CompilerParams(vmem_limit_bytes=12 << 20),
        cost_estimate=LIGHT,
        name="unpack",
    )(meta, mine, other)


def masked(scores, key_bias):
    first = scores.shape[0] - 128
    if first == 0:
        return scores + key_bias
    return jnp.concatenate([scores[:first], scores[first:] + key_bias], axis=0)


def _attend_kernel(meta_ref, qkv_ref, ctx_ref, lse_ref):
    ctx_ref[...] = jnp.zeros_like(ctx_ref)
    width = ctx_ref.shape[1]
    part = width // 2

    def one(slot, blocks):
        span = blocks * 128
        offset = pl.multiple_of(meta_ref[slot], 16)
        length = meta_ref[4 + slot]
        rows = pl.ds(offset, span)
        key_id = lax.broadcasted_iota(jnp.int32, (128, 1), 0) + (span - 128)
        key_bias = jnp.where(key_id < length, 0.0, -1e30)

        @pl.loop(0, width // 128, unroll=2)
        def _(pair):
            lane0 = pl.multiple_of((pair // 2) * (3 * part) + (pair % 2) * 128, 128)
            keys = qkv_ref[rows, pl.ds(pl.multiple_of(part + lane0, 128), 128)]
            values = qkv_ref[rows, pl.ds(pl.multiple_of(2 * part + lane0, 128), 128)]
            values_t = values.astype(F32).T.astype(BF)
            for first in range(0, span, STEP):
                step = min(span - first, STEP)
                queries = qkv_ref[
                    pl.ds(pl.multiple_of(offset + first, 16), step), pl.ds(lane0, 128)
                ]
                queries = queries * jnp.asarray(HEAD_SIZE**-0.5, BF)
                lane = lax.broadcasted_iota(jnp.int32, (step, 128), 1)
                parts = []
                for half in range(2):
                    picked = jnp.where((lane >= 64) == (half == 1), queries, jnp.zeros_like(queries))
                    scores = mm_cols(keys, picked)
                    scores = masked(scores, key_bias)
                    highest = jnp.max(scores, axis=0, keepdims=True)
                    expo = jnp.exp(scores - highest)
                    total = jnp.sum(expo, axis=0, keepdims=True)
                    weighted = mm(values_t[64 * half : 64 * half + 64], expo.astype(BF))
                    parts.append(weighted * (1.0 / total))
                    lse_ref[slot, pair * 2 + half, :, first : first + step] = highest + jnp.log(total)
                mixed = jnp.concatenate(parts, axis=0).T
                out_lane = pl.multiple_of(pair * 128, 128)
                ctx_ref[pl.ds(pl.multiple_of(offset + first, 16), step), pl.ds(out_lane, 128)] = (
                    mixed.astype(BF)
                )

    @pl.loop(0, 4)
    def _(slot):
        for blocks in range(1, 5):
            pl.when(meta_ref[8 + slot] == blocks)(functools.partial(one, slot, blocks))


def attend(meta, qkv):
    width = qkv.shape[1] // 3
    return pl.pallas_call(
        _attend_kernel,
        out_shape=(
            jax.ShapeDtypeStruct((CAP, width), BF),
            jax.ShapeDtypeStruct((4, width // HEAD_SIZE, 1, 512), F32),
        ),
        in_specs=[SMEM_SPEC, VMEM_SPEC],
        out_specs=(VMEM_SPEC, VMEM_SPEC),
        compiler_params=pltpu.CompilerParams(vmem_limit_bytes=12 << 20),
        cost_estimate=LIGHT,
        name="attend",
    )(meta, qkv)


def _attend_back_kernel(block, meta_ref, qkv_ref, lse_ref, gctx_ref, out_ref):
    out_ref[...] = jnp.zeros_like(out_ref)
    part = out_ref.shape[1] // 3

    def one(slot, blocks):
        span = blocks * 128
        offset = pl.multiple_of(meta_ref[slot], 16)
        length = meta_ref[4 + slot]
        rows = pl.ds(offset, span)
        key_id = lax.broadcasted_iota(jnp.int32, (128, 1), 0) + (span - 128)
        key_bias = jnp.where(key_id < length, 0.0, -1e30)

        @pl.loop(0, part // 128, unroll=2)
        def _(turn):
            pair = block * (part // 128) + turn
            out_lane = pl.multiple_of(turn * 128, 128)
            base = block * 3 * part
            lane0 = pl.multiple_of(base + turn * 128, 128)
            ctx_lane = pl.multiple_of(block * part + turn * 128, 128)
            keys = qkv_ref[rows, pl.ds(pl.multiple_of(part + lane0, 128), 128)]
            values = qkv_ref[rows, pl.ds(pl.multiple_of(2 * part + lane0, 128), 128)]
            keys_t = keys.astype(F32).T.astype(BF)
            grad_keys = jnp.zeros((span, 128), F32)
            grad_values = jnp.zeros((span, 128), F32)
            for first in range(0, span, STEP):
                step = min(span - first, STEP)
                here = pl.ds(pl.multiple_of(offset + first, 16), step)
                queries = qkv_ref[here, pl.ds(lane0, 128)] * jnp.asarray(HEAD_SIZE**-0.5, BF)
                grad_ctx = gctx_ref[here, pl.ds(ctx_lane, 128)]
                lane = lax.broadcasted_iota(jnp.int32, (step, 128), 1)
                row = lax.broadcasted_iota(jnp.int32, (step, 128), 0) + first
                grad_ctx = jnp.where(row < length, grad_ctx, jnp.zeros_like(grad_ctx))
                parts = []
                for half in range(2):
                    side = (lane >= 64) == (half == 1)
                    picked = jnp.where(side, queries, jnp.zeros_like(queries))
                    picked_grad = jnp.where(side, grad_ctx, jnp.zeros_like(grad_ctx))
                    scores = mm_cols(keys, picked)
                    log_total = lse_ref[slot, pair * 2 + half, :, first : first + step]
                    scores = scores - log_total
                    scores = masked(scores, key_bias)
                    probs = jnp.exp(scores)
                    grad_values = grad_values + mm(probs.astype(BF), picked_grad)
                    grad_probs = mm_cols(values, picked_grad)
                    inner = jnp.sum(probs * grad_probs, axis=0, keepdims=True)
                    grad_scores = (probs * (grad_probs - inner)).astype(BF)
                    grad_keys = grad_keys + mm(grad_scores, picked)
                    parts.append(mm(keys_t[64 * half : 64 * half + 64], grad_scores))
                grad_queries = jnp.concatenate(parts, axis=0).T * HEAD_SIZE**-0.5
                out_ref[here, pl.ds(out_lane, 128)] = grad_queries.astype(BF)
            key_lane = pl.multiple_of(part + out_lane, 128)
            value_lane = pl.multiple_of(2 * part + out_lane, 128)
            out_ref[rows, pl.ds(key_lane, 128)] = grad_keys.astype(BF)
            out_ref[rows, pl.ds(value_lane, 128)] = grad_values.astype(BF)

    @pl.loop(0, 4)
    def _(slot):
        for blocks in range(1, 5):
            pl.when(meta_ref[8 + slot] == blocks)(functools.partial(one, slot, blocks))


def attend_back(meta, qkv, lse, grad_ctx, block):
    return pl.pallas_call(
        functools.partial(_attend_back_kernel, block),
        out_shape=jax.ShapeDtypeStruct((qkv.shape[0], qkv.shape[1] // 2), BF),
        in_specs=[SMEM_SPEC] + [VMEM_SPEC] * 3,
        out_specs=VMEM_SPEC,
        compiler_params=pltpu.CompilerParams(vmem_limit_bytes=12 << 20),
        cost_estimate=LIGHT,
        name="attend_back",
    )(meta, qkv, lse, grad_ctx)


def _assemble_kernel(kinds, meta_ref, *refs):
    out_ref = refs[-1]
    here, core = meta_ref[12], meta_ref[13]
    rows, columns = refs[0].shape
    block = columns // (4 * kinds)
    for flip, src in zip((0, 2, 1, 3), refs[:4]):
        place = pl.ds(pl.multiple_of((here ^ flip) * rows, 16), rows)
        for kind in range(kinds):
            for side in range(2):
                lane = pl.multiple_of((kind * 4 + core + 2 * side) * block, 128)
                spot = (side * kinds + kind) * block
                out_ref[place, spot : spot + block] = src[:, pl.ds(lane, block)]


def assemble(meta, kinds, own, from_x, from_core, from_both):
    rows, columns = own.shape
    return pl.pallas_call(
        functools.partial(_assemble_kernel, kinds),
        out_shape=jax.ShapeDtypeStruct((4 * rows, columns // 2), BF),
        in_specs=[SMEM_SPEC] + [VMEM_SPEC] * 4,
        out_specs=VMEM_SPEC,
        compiler_params=pltpu.CompilerParams(vmem_limit_bytes=12 << 20),
        cost_estimate=LIGHT,
        name="assemble",
    )(meta, own, from_x, from_core, from_both)


def _spread_kernel(kinds, sides, meta_ref, *refs):
    out_ref = refs[-1]
    core = meta_ref[13]
    block = out_ref.shape[1] // (4 * kinds)
    for flip in range(2):
        for kind in range(kinds):
            for side in range(2):
                lane = pl.multiple_of((kind * 4 + (core ^ flip) + 2 * side) * block, 128)
                if sides:
                    src, spot = refs[2 * side + flip], kind * block
                else:
                    src, spot = refs[flip], (side * kinds + kind) * block
                out_ref[:, pl.ds(lane, block)] = src[:, spot : spot + block].astype(F32)


def spread_columns(meta, kinds, columns, *blocks):
    return pl.pallas_call(
        functools.partial(_spread_kernel, kinds, len(blocks) == 4),
        out_shape=jax.ShapeDtypeStruct((blocks[0].shape[0], columns), F32),
        in_specs=[SMEM_SPEC] + [VMEM_SPEC] * len(blocks),
        out_specs=VMEM_SPEC,
        compiler_params=pltpu.CompilerParams(vmem_limit_bytes=12 << 20),
        cost_estimate=LIGHT,
        name="spread_columns",
    )(meta, *blocks)


def _stack_kernel(place, meta_ref, mine_ref, other_ref, out_ref):
    spot = meta_ref[place]
    rows = mine_ref.shape[0]
    mine_at = pl.multiple_of(spot * rows, 16)
    other_at = pl.multiple_of((1 - spot) * rows, 16)
    out_ref[pl.ds(mine_at, rows), :] = mine_ref[...].astype(out_ref.dtype)
    out_ref[pl.ds(other_at, rows), :] = other_ref[...].astype(out_ref.dtype)


def stack_rows(meta, place, mine, other, kind=F32):
    return pl.pallas_call(
        functools.partial(_stack_kernel, place),
        out_shape=jax.ShapeDtypeStruct((2 * mine.shape[0], mine.shape[1]), kind),
        in_specs=[SMEM_SPEC] + [VMEM_SPEC] * 2,
        out_specs=VMEM_SPEC,
        compiler_params=pltpu.CompilerParams(vmem_limit_bytes=12 << 20),
        cost_estimate=LIGHT,
        name="stack_rows",
    )(meta, mine, other)


def _merge_kernel(meta_ref, down_ref, out_weight_ref, mine_ref, other_ref, down_out, out_out):
    here_y, chip = meta_ref[14], meta_ref[18]
    size = mine_ref.shape[0] // 4
    first = 0
    for own_ref, out_ref in ((down_ref, down_out), (out_weight_ref, out_out)):
        rows, share = own_ref.shape[0], own_ref.shape[0] // 8
        out_ref[pl.ds(pl.multiple_of(chip * rows, 16), rows), :] = own_ref[...]
        for src, y in ((mine_ref, here_y), (other_ref, 1 - here_y)):
            for turn in range(4):
                at = (1 - chip) * rows + (y * 4 + turn) * share
                out_ref[pl.ds(pl.multiple_of(at, 16), share), :] = src[
                    turn * size + first : turn * size + first + share, :
                ]
        first += share


def merge_shares(meta, w_down, w_out, mine, other):
    return pl.pallas_call(
        _merge_kernel,
        out_shape=tuple(
            jax.ShapeDtypeStruct((2 * weight.shape[0], weight.shape[1]), BF)
            for weight in (w_down, w_out)
        ),
        in_specs=[SMEM_SPEC] + [VMEM_SPEC] * 4,
        out_specs=(VMEM_SPEC, VMEM_SPEC),
        compiler_params=pltpu.CompilerParams(vmem_limit_bytes=12 << 20),
        cost_estimate=LIGHT,
        name="merge_shares",
    )(meta, w_down, w_out, mine, other)


TILE = 256


def _tiles(meta_ref, count_at, out_refs, body):
    rows = out_refs[0].shape[0]
    used = jnp.minimum((meta_ref[count_at] + TILE - 1) // TILE, rows // TILE)

    @pl.loop(0, used)
    def _(tile):
        body(pl.ds(pl.multiple_of(tile * TILE, TILE), TILE))

    @pl.loop(used, rows // TILE)
    def _(tile):
        for out_ref in out_refs:
            place = pl.ds(pl.multiple_of(tile * TILE, TILE), TILE)
            out_ref[place, :] = jnp.zeros((TILE, out_ref.shape[1]), out_ref.dtype)


def _up_kernel(count_at, meta_ref, low_ref, weight_ref, bias_ref, act_ref, slope_ref):
    width = act_ref.shape[1]
    step = 512

    def body(place):
        @pl.loop(0, width // step)
        def _(turn):
            lanes = pl.ds(pl.multiple_of(turn * step, step), step)
            pre = mm(low_ref[place, :], weight_ref[:, lanes]) + bias_ref[:, lanes]
            cdf = 0.5 * (1.0 + lax.erf(pre * np.float32(0.5**0.5)))
            slope = cdf + pre * jnp.exp(-0.5 * pre * pre) * np.float32((2 * np.pi) ** -0.5)
            act_ref[place, lanes] = (pre * cdf).astype(BF)
            slope_ref[place, lanes] = slope.astype(BF)

    _tiles(meta_ref, count_at, (act_ref, slope_ref), body)


def up_product(meta, count_at, low, weight, bias):
    shape = jax.ShapeDtypeStruct((low.shape[0], weight.shape[1]), BF)
    return pl.pallas_call(
        functools.partial(_up_kernel, count_at),
        out_shape=(shape, shape),
        in_specs=[SMEM_SPEC] + [VMEM_SPEC] * 3,
        out_specs=(VMEM_SPEC, VMEM_SPEC),
        compiler_params=pltpu.CompilerParams(vmem_limit_bytes=8 << 20),
        cost_estimate=LIGHT,
        name="up_product",
    )(meta, low, weight, bias)


def _qkv_kernel(meta_ref, rows_ref, weight_ref, bias_ref, out_ref):
    step = out_ref.shape[1] // 2

    def body(place):
        for first in (0, step):
            lanes = slice(first, first + step)
            product = mm(rows_ref[place, :], weight_ref[:, lanes]) + bias_ref[:, lanes]
            out_ref[place, lanes] = product.astype(BF)

    _tiles(meta_ref, ALL, (out_ref,), body)


def qkv_product(meta, rows, weight, bias):
    return pl.pallas_call(
        _qkv_kernel,
        out_shape=jax.ShapeDtypeStruct((rows.shape[0], weight.shape[1]), BF),
        in_specs=[SMEM_SPEC] + [VMEM_SPEC] * 3,
        out_specs=VMEM_SPEC,
        compiler_params=pltpu.CompilerParams(vmem_limit_bytes=8 << 20),
        cost_estimate=LIGHT,
        name="qkv_product",
    )(meta, rows, weight, bias)


def _rows_kernel(count_at, turned, terms, scaled, meta_ref, *refs):
    lefts, rights = refs[:terms], refs[terms : 2 * terms]
    out_ref = refs[2 * terms + scaled]
    width = out_ref.shape[1]
    step = min(512, width)

    def body(place):
        @pl.loop(0, width // step)
        def _(turn):
            lanes = pl.ds(pl.multiple_of(turn * step, step), step)
            total = None
            for left_ref, right_ref in zip(lefts, rights):
                left = left_ref[place, :]
                if turned:
                    term = mm_cols(left, right_ref[lanes, :])
                else:
                    term = mm(left, right_ref[:, lanes])
                total = term if total is None else total + term
            if scaled:
                total = total * refs[2 * terms][place, lanes].astype(F32)
            out_ref[place, lanes] = total.astype(out_ref.dtype)

    _tiles(meta_ref, count_at, (out_ref,), body)


def rows_product(meta, count_at, lefts, rights, turned, kind, scale=None):
    width = rights[0].shape[0] if turned else rights[0].shape[1]
    args = [*lefts, *rights] + ([] if scale is None else [scale])
    return pl.pallas_call(
        functools.partial(_rows_kernel, count_at, turned, len(lefts), int(scale is not None)),
        out_shape=jax.ShapeDtypeStruct((lefts[0].shape[0], width), kind),
        in_specs=[SMEM_SPEC] + [VMEM_SPEC] * len(args),
        out_specs=VMEM_SPEC,
        compiler_params=pltpu.CompilerParams(vmem_limit_bytes=8 << 20),
        cost_estimate=LIGHT,
        name="rows_product",
    )(meta, *args)


def _grad_kernel(terms, meta_ref, at_ref, *refs):
    lefts, rights = refs[:terms], refs[terms : 2 * terms]
    out_ref, turned_ref = refs[2 * terms :]
    count, width = out_ref.shape
    first = 0
    for left_ref in lefts:
        rows = left_ref.shape[0]
        piece = left_ref[:, pl.ds(pl.multiple_of(at_ref[0], 128), count)]
        turned_ref[:, first : first + rows] = piece.astype(F32).T.astype(BF)
        first += rows
    step = 256

    @pl.loop(0, width // step)
    def _(turn):
        lanes = pl.ds(pl.multiple_of(turn * step, step), step)
        total, start = None, 0
        for right_ref in rights:
            rows = right_ref.shape[0]
            term = mm(turned_ref[:, start : start + rows], right_ref[:, lanes])
            total = term if total is None else total + term
            start += rows
        out_ref[:, lanes] = total.astype(out_ref.dtype)


def grad_product(meta, lefts, rights, start, count, kind):
    rows = sum(left.shape[0] for left in lefts)
    args = [*lefts, *rights]
    return pl.pallas_call(
        functools.partial(_grad_kernel, len(lefts)),
        out_shape=jax.ShapeDtypeStruct((count, rights[0].shape[1]), kind),
        in_specs=[SMEM_SPEC, SMEM_SPEC] + [VMEM_SPEC] * len(args),
        out_specs=VMEM_SPEC,
        scratch_shapes=[pltpu.VMEM((count, rows), BF)],
        compiler_params=pltpu.CompilerParams(vmem_limit_bytes=12 << 20),
        cost_estimate=LIGHT,
        name="grad_product",
    )(meta, jnp.asarray(start, jnp.int32)[None], *args)


def normed(inputs):
    average = jnp.mean(inputs, axis=-1, keepdims=True)
    centered = inputs - average
    variance = jnp.mean(centered * centered, axis=-1, keepdims=True)
    rstd = lax.rsqrt(variance + EPS)
    return centered * rstd, rstd


def norm_back(unit, rstd, grad, gain):
    scaled = grad * gain
    return (
        scaled
        - jnp.mean(scaled, axis=-1, keepdims=True)
        - unit * jnp.mean(scaled * unit, axis=-1, keepdims=True)
    ) * rstd


SWAP_X = [(i, i ^ 2) for i in range(4)]
SWAP_Y = [(i, i ^ 1) for i in range(8)]
SWAP_Z1 = [(i, i ^ 2) for i in range(8)]
SWAP_Z2 = [(i, i ^ 4) for i in range(8)]
AT_Y, AT_Z1, AT_Z2 = 14, 16, 17
MINE, OTHER, ALL = 19, 20, 21


def moved(name, value, axis, pairs):
    with jax.named_scope(name):
        return lax.ppermute(value, axis, pairs)


class SeqSum:
    def __init__(self, name, meta, group_count):
        self.name, self.meta, self.whole = name, meta, group_count == 8
        index = lax.axis_index("seq")
        self.bits = {AT_Y: index % 2, AT_Z1: index // 2 % 2, AT_Z2: index // 4 % 2}

    def send(self, step, value, axis, pairs):
        self.token = value
        self.arrived = moved(f"{self.name}_{step}", value, axis, pairs)

    def start_x(self, far, own):
        self.kept = own[None]
        self.send("x", far.astype(BF), "head", SWAP_X)

    def start_y(self, far, kept):
        self.kept = kept
        self.send("y", far.astype(BF), "seq", SWAP_Y)

    def added(self, gates):
        arrived = after(self.arrived, *gates).astype(F32)
        self.kept = self.kept + arrived.reshape(self.kept.shape)

    def split(self, step, place, pairs):
        blocks, rows, columns = self.kept.shape
        halves = self.kept.reshape(blocks, 2, rows // 2, columns)
        bit = self.bits[place]
        self.kept = lax.dynamic_index_in_dim(halves, bit, 1, keepdims=False)
        sent = lax.dynamic_index_in_dim(halves, 1 - bit, 1, keepdims=False)
        self.send(step, sent.astype(BF).reshape(-1, columns), "seq", pairs)

    def step_y(self, *gates):
        self.added(gates)
        if self.whole:
            self.split("y", AT_Y, SWAP_Y)
            return
        count = self.kept.shape[1] // 2
        halves = lax.psum(self.kept[0], "seq").astype(BF).reshape(2, count, -1)
        bit = self.bits[AT_Y]
        self.mine = self.token = lax.dynamic_index_in_dim(halves, bit, 0, keepdims=False)
        self.arrived = lax.dynamic_index_in_dim(halves, 1 - bit, 0, keepdims=False)

    def step_z1(self, *gates):
        if self.whole:
            self.added(gates)
            self.split("z1", AT_Z1, SWAP_Z1)

    def step_z2(self, *gates):
        if self.whole:
            self.added(gates)
            self.split("z2", AT_Z2, SWAP_Z2)

    def step_x(self, *gates):
        if self.whole:
            self.added(gates)
            far = self.kept[1]
            self.kept = self.kept[:1]
            self.send("x", far.astype(BF), "head", SWAP_X)

    def back_z2(self, *gates):
        if self.whole:
            self.added(gates)
            self.mine = self.kept[0].astype(BF)
            self.send("back_z2", self.mine, "seq", SWAP_Z2)

    def joined(self, place, gates):
        arrived = after(self.arrived, *gates)
        self.mine = stack_rows(self.meta, place, self.mine, arrived, BF)

    def back_z1(self, *gates):
        if self.whole:
            self.joined(AT_Z2, gates)
            self.send("back_z1", self.mine, "seq", SWAP_Z1)

    def back_y(self, *gates):
        if self.whole:
            self.joined(AT_Z1, gates)
            self.send("back_y", self.mine, "seq", SWAP_Y)

    def halves(self, *gates):
        return self.mine, after(self.arrived, *gates)


def on_device(
    tokens,
    cotangent,
    lengths,
    seq_order,
    w_qkv,
    w_out,
    w_up,
    w_down,
    bias_q,
    bias_v,
    bias_out,
    bias_up,
    bias_down,
    gain_attn,
    shift_attn,
    gain_mlp,
    shift_mlp,
):
    group_count = lax.axis_size("seq")
    group_id = lax.axis_index("seq")
    here = lax.axis_index("head").astype(jnp.int32)
    core, chip = here % 2, here // 2
    slots, span_rows, width = tokens.shape
    part = width // 4
    ff_part = w_up.shape[1] // 4
    offsets = [k * group_count // slots for k in range(slots)]
    offsets[1], offsets[-1] = 1, group_count - 1
    swap_x = [(i, i ^ 2) for i in range(4)]
    swap_core = [(i, i ^ 1) for i in range(4)]

    def over_x(value, name="x"):
        with jax.named_scope(name):
            return lax.ppermute(value, "head", swap_x)

    def over_core(value, name="core"):
        with jax.named_scope(name):
            return lax.ppermute(value, "head", swap_core)

    slot_ids = jnp.arange(slots, dtype=jnp.int32)
    local_ids = group_id * slots + slot_ids
    given_slot = lax.dynamic_slice_in_dim(seq_order, group_id * slots, slots) % slots
    given_of_slot = jnp.sum(
        jnp.where(given_slot[None, :] == slot_ids[:, None], slot_ids[None, :], 0), axis=1
    )
    matches = seq_order[None, :] == local_ids[:, None]
    slot_lens = jnp.sum(jnp.where(matches, lengths[None, :], 0), axis=1)
    aligned = (slot_lens + 15) // 16 * 16
    choices = np.zeros((35, slots), np.int32)
    for row, picks in enumerate(itertools.combinations(range(1, slots), 3)):
        choices[row, [0, *picks]] = 1
    sides = jnp.sum(choices * aligned[None, :], axis=1)
    larger = jnp.maximum(sides, jnp.sum(aligned) - sides)
    squares = jnp.sum(choices * (slot_lens * slot_lens)[None, :], axis=1)
    heavier = jnp.maximum(squares, jnp.sum(slot_lens * slot_lens) - squares)
    score = larger * 1024 + heavier // 4096
    best = jnp.min(score)
    chosen = jnp.argmax(score == best)
    in_first = jnp.sum(
        jnp.where(jnp.arange(35)[:, None] == chosen, choices, 0), axis=0, dtype=jnp.int32
    )
    is_own = jnp.where(chip == 0, in_first, 1 - in_first)
    before = np.tril(np.ones((slots, slots), np.int32), -1)
    rank_own = jnp.sum(before * is_own[None, :], axis=1)
    rank_far = jnp.sum(before * (1 - is_own)[None, :], axis=1)
    list_pos = jnp.where(is_own == 1, rank_own, 4 + rank_far).astype(jnp.int32)
    at_place = list_pos[None, :] == slot_ids[:, None]
    slot_at = jnp.sum(jnp.where(at_place, slot_ids[None, :], 0), axis=1)
    own_lens = jnp.sum(jnp.where(at_place, slot_lens[None, :], 0), axis=1)[:4]
    own_aligned = (own_lens + 15) // 16 * 16
    own_offsets = jnp.sum(np.tril(np.ones((4, 4), np.int32), -1) * own_aligned[None, :], axis=1)
    total_rows = jnp.sum(own_aligned)
    meta = jnp.concatenate(
        [
            own_offsets,
            own_lens,
            (own_lens + 127) // 128,
            here[None],
            core[None],
            (group_id % 2)[None],
            (group_id // 2)[None],
            (group_id // 2 % 2)[None],
            (group_id // 4 % 2)[None],
            chip[None],
            jnp.clip(total_rows - core * HALF, 0, HALF)[None],
            jnp.clip(total_rows - (1 - core) * HALF, 0, HALF)[None],
            total_rows[None],
            jnp.zeros((2,), jnp.int32),
        ]
    ).astype(jnp.int32)
    row_ids = core * HALF + jnp.arange(HALF, dtype=jnp.int32)
    row_keep = jnp.any(
        (row_ids[:, None] >= own_offsets[None, :])
        & (row_ids[:, None] < (own_offsets + own_lens)[None, :]),
        axis=1,
        keepdims=True,
    )

    def swapped(own, far):
        return own, far, over_core(own), over_core(far)

    if group_count == slots:
        spots = (group_id - given_slot) % slots
        sent_tokens = route(tokens, spots)
    else:
        sent_tokens = route(tokens, given_slot.astype(jnp.int32))
    small_here = jnp.concatenate(
        [
            bias_q,
            bias_v,
            bias_out,
            bias_down,
            gain_attn,
            shift_attn,
            gain_mlp,
            shift_mlp,
            bias_up,
        ]
    )[None, :]
    small_here = after(small_here, sent_tokens)
    small_core = over_core(small_here)

    def ordered(first, second, is_low):
        return jnp.concatenate(
            [jnp.where(is_low, first, second), jnp.where(is_low, second, first)], axis=0
        )

    small_pair = ordered(small_here, small_core, core == 0)
    small = ordered(small_pair, over_x(small_pair), chip == 0).astype(F32)

    def vector(place):
        return small[:, place * part : (place + 1) * part].reshape(1, width)

    def local_columns(rows):
        return jnp.concatenate(
            [
                lax.dynamic_index_in_dim(rows, core, 0, keepdims=False),
                lax.dynamic_index_in_dim(rows, core + 2, 0, keepdims=False),
            ]
        )

    query_bias = local_columns(small[:, 0:part])
    value_bias = local_columns(small[:, part : 2 * part])
    up_bias = local_columns(small[:, 8 * part :])[None, :]
    out_bias, down_bias = vector(2), vector(3)
    attn_gain, attn_shift, mlp_gain, mlp_shift = vector(4), vector(5), vector(6), vector(7)
    no_bias = jnp.zeros((part,), F32)
    joint_bias = jnp.concatenate(
        [query_bias[:part], no_bias, value_bias[:part], query_bias[part:], no_bias, value_bias[part:]]
    )[None, :]


    far_qkv = over_x(after(w_qkv, sent_tokens), "x_first_weights")
    if group_count == 8:
        turn = (group_id % 2) * 4 + group_id // 4 + 2 * (group_id // 2 % 2)
        mixed = jnp.concatenate(
            [
                lax.dynamic_slice_in_dim(
                    weight, turn * (weight.shape[0] // 8), weight.shape[0] // 8, axis=0
                )
                for weight in (w_down, w_out)
            ],
            axis=0,
        )
        mixed = over_x(after(mixed, sent_tokens), "x_shares")
    else:
        mixed = small
    if group_count == slots:
        got = lax.all_to_all(sent_tokens, "seq", split_axis=0, concat_axis=0, tiled=True)
        came = (slot_ids - group_id) % slots
        placed = jnp.sum(
            jnp.where(came[:, None] == slot_ids[None, :], list_pos[None, :], 0), axis=1
        )
        lists = route(got, placed.astype(jnp.int32))
    else:
        arrived = [sent_tokens[0]]
        for k in range(1, slots):
            arrived.append(
                lax.ppermute(
                    sent_tokens[k],
                    "seq",
                    [(i, (i - offsets[k]) % group_count) for i in range(group_count)],
                )
            )
        lists = route(arrived, list_pos)

    def by_chip(own, far):
        return jnp.concatenate(
            [jnp.where(chip == 0, own, far), jnp.where(chip == 0, far, own)], axis=0
        )

    full_qkv = assemble(meta, 3, *swapped(w_qkv, far_qkv))

    cot_lists = route(cotangent, list_pos)
    far_tokens = over_x(lists[4:], "x_tokens")
    if group_count == 8:
        mixed = after(mixed, lists)
        pair = stack_rows(meta, AT_Z2, mixed, moved("share_z2", mixed, "seq", SWAP_Z2), BF)
        gate = pair
        four = stack_rows(meta, AT_Z1, pair, moved("share_z1", pair, "seq", SWAP_Z1), BF)
    else:
        gate = far_tokens
    here_blocks = swapped(lists[:4], after(far_tokens, gate, cot_lists))
    if group_count == 8:
        here_blocks = (*here_blocks[:3], after(here_blocks[3], four))
    rows_in = pack(meta, *here_blocks)
    w_up_later, _ = lax.optimization_barrier((w_up, far_tokens))
    far_up = over_x(w_up_later, "x_up_weight")
    if group_count == 8:
        other_four = moved("share_y", four, "seq", SWAP_Y)
    else:
        full_down, full_out = by_chip(w_down, over_x(w_down)), by_chip(w_out, over_x(w_out))

    def halves(value):
        return (
            lax.dynamic_slice_in_dim(value, core * HALF, HALF, axis=0),
            lax.dynamic_slice_in_dim(value, (1 - core) * HALF, HALF, axis=0),
        )

    def in_order(mine, other):
        lower = jnp.where(core == 0, mine, other)
        upper = jnp.where(core == 0, other, mine)
        return jnp.concatenate([lower, upper], axis=0)

    def core_sum(lefts_mine, lefts_other, rights, turned):
        arriving = over_core(rows_product(meta, OTHER, lefts_other, rights, turned, BF))
        return rows_product(meta, MINE, lefts_mine, rights, turned, F32) + arriving.astype(F32)

    qkv = qkv_product(meta, rows_in, full_qkv, joint_bias)
    context, lse = attend(meta, qkv)
    if group_count == 8:
        context, other_four = lax.optimization_barrier((context, other_four))
        full_down, full_out = merge_shares(meta, w_down, w_out, four, other_four)
    cot_far_in = after(cot_lists[4:], far_up)
    full_up = assemble(meta, 1, *swapped(w_up, far_up))
    cot_arrived = over_x(cot_far_in, "x_cotangent")
    ctx_mine, ctx_other = halves(context)
    rows_mine, _ = halves(rows_in)
    resid_attn = (
        core_sum([ctx_mine], [ctx_other], [full_out], False) + rows_mine.astype(F32) + out_bias
    )
    unit_attn, rstd_attn = normed(resid_attn)
    hidden = unit_attn * attn_gain + attn_shift
    low_mine = hidden.astype(BF)
    low_other = over_core(low_mine)

    act_mine, slope_mine = up_product(meta, MINE, low_mine, full_up, up_bias)
    act_other, slope_other = up_product(meta, OTHER, low_other, full_up, up_bias)
    cot_rows = pack(meta, *swapped(cot_lists[:4], after(cot_arrived, act_mine)))
    resid_mlp = core_sum([act_mine], [act_other], [full_down], False) + hidden + down_bias
    unit_mlp, rstd_mlp = normed(resid_mlp)
    final_mine = (unit_mlp * mlp_gain + mlp_shift).astype(BF)

    cot_mine, _ = halves(cot_rows)
    grad_y = jnp.where(row_keep, cot_mine.astype(F32), 0.0)
    grad_mlp2 = norm_back(unit_mlp, rstd_mlp, grad_y, mlp_gain)
    sum_gain_mlp = jnp.sum(grad_y * unit_mlp, axis=0)
    sum_shift_mlp = jnp.sum(grad_y, axis=0)
    branch_mine = grad_mlp2.astype(BF)
    branch_other = over_core(branch_mine)
    sum_bias_down = jnp.sum(branch_mine, axis=0, dtype=F32)
    def grads(lefts, rights, start, count, kind=F32):
        return grad_product(meta, lefts, rights, start, count, kind)

    down_sum = SeqSum("down", meta, group_count)
    acts, branches = [act_mine, act_other], [branch_mine, branch_other]
    if group_count == 8:
        here_y = group_id % 2
        count = ff_part // 2

        def down_term(half, kind):
            return jnp.stack(
                [
                    grads(acts, branches, side * ff_part + half * count, count, kind)
                    for side in (chip, 1 - chip)
                ]
            )

        down_sum.start_y(down_term(1 - here_y, BF).reshape(-1, width), down_term(here_y, F32))
    else:
        down_sum.start_x(
            *(grads(acts, branches, side * ff_part, ff_part) for side in (1 - chip, chip))
        )
    branch_mine, branch_other, _ = lax.optimization_barrier(
        (branch_mine, branch_other, down_sum.token)
    )
    pre_mine = rows_product(meta, MINE, [branch_mine], [full_down], True, BF, slope_mine)
    pre_other = rows_product(meta, OTHER, [branch_other], [full_down], True, BF, slope_other)
    sum_bias_up = jnp.sum(pre_mine, axis=0, dtype=F32) + jnp.sum(pre_other, axis=0, dtype=F32)

    lows, pres = [low_mine, low_other], [pre_mine, pre_other]
    up_far, up_own = (
        grads(lows, pres, side * 2 * part, 2 * part, kind)
        for side, kind in ((1 - chip, BF), (chip, F32))
    )
    up_sum = SeqSum("up", meta, group_count)
    up_sum.start_x(up_far, up_own)
    pre_mine, pre_other, _ = lax.optimization_barrier((pre_mine, pre_other, up_sum.token))
    gh_other = rows_product(meta, OTHER, [pre_other], [full_up], True, BF)
    gh_arrived = over_core(gh_other)
    if group_count == 8:
        down_sum.step_z1(gh_other)
    else:
        down_sum.step_y(gh_other)
    pre_mine = after(pre_mine, down_sum.token)
    grad_hidden = rows_product(meta, MINE, [pre_mine], [full_up], True, F32)
    grad_hidden = grad_hidden + gh_arrived.astype(F32) + grad_mlp2

    grad_attn2 = norm_back(unit_attn, rstd_attn, grad_hidden, attn_gain)
    sum_gain_attn = jnp.sum(grad_hidden * unit_attn, axis=0)
    sum_shift_attn = jnp.sum(grad_hidden, axis=0)
    attn_mine = grad_attn2.astype(BF)
    attn_other = over_core(attn_mine)
    sum_bias_out = jnp.sum(attn_mine, axis=0, dtype=F32)
    half_width = width // 2

    def out_term(side, kind):
        term = grads([ctx_mine, ctx_other], [attn_mine, attn_other], side * part, part, kind)
        return jnp.concatenate([term[:, :half_width], term[:, half_width:]], axis=0)

    out_far, out_own = out_term(1 - chip, BF), out_term(chip, F32)
    down_sum.step_z2(out_own, out_far)
    up_sum.step_y(down_sum.token)
    attn_mine, attn_other, _ = lax.optimization_barrier((attn_mine, attn_other, up_sum.token))
    grad_ctx = in_order(
        rows_product(meta, MINE, [attn_mine], [full_out], True, BF),
        rows_product(meta, OTHER, [attn_other], [full_out], True, BF),
    )
    y_own, y_far = unpack(meta, final_mine, over_core(after(final_mine, gh_other)))
    y_arrived = over_x(y_far, "x_activations")
    grad_first = attend_back(meta, qkv, lse, after(grad_ctx, y_far), 0)
    down_sum.step_x(grad_first)
    up_sum.step_z1(down_sum.token)
    grad_first = after(grad_first, up_sum.token)

    first_far, first_own = (
        jnp.concatenate(
            [grads([rows_in], [grad_first], side * 2 * part, 2 * part, out.dtype), out], axis=1
        )
        for side, out in ((1 - chip, out_far), (chip, out_own))
    )
    first_sum = SeqSum("first", meta, group_count)
    first_sum.start_x(first_far, first_own)
    down_sum.back_z2(first_sum.token, first_own)
    grad_last = attend_back(meta, qkv, lse, after(grad_ctx, down_sum.token), 1)
    grad_last = after(grad_last, y_arrived)
    down_sum.back_z1(grad_last)
    up_sum.step_z2(down_sum.token)
    grad_last = after(grad_last, up_sum.token)

    qkv_blocks = [full_qkv[:, : 3 * part], full_qkv[:, 3 * part :]]
    first_mine, first_other = halves(grad_first)
    last_mine, last_other = halves(grad_last)
    gx_other = rows_product(meta, OTHER, [first_other, last_other], qkv_blocks, True, BF)
    gx_arrived = over_core(gx_other)
    gx_mine = rows_product(meta, MINE, [first_mine, last_mine], qkv_blocks, True, F32)
    gx_mine = (gx_mine + gx_arrived.astype(F32) + grad_attn2).astype(BF)
    gx_other = over_core(gx_mine)
    first_sum.step_y(gx_mine)
    down_sum.back_y(first_sum.token)
    up_sum.back_z2(down_sum.token)
    gx_mine = after(gx_mine, up_sum.token)
    gx_own, gx_far = unpack(meta, gx_mine, gx_other)
    gx_arrived = over_x(gx_far, "x_grad")
    up_sum.back_z1(gx_far)
    grad_last = after(grad_last, up_sum.token)
    last_far, last_own = (
        grads([rows_in], [grad_last], side * 2 * part, 2 * part, kind)
        for side, kind in ((1 - chip, BF), (chip, F32))
    )
    first_sums = jnp.sum(grad_first, axis=0, dtype=F32)
    last_sums = jnp.sum(grad_last, axis=0, dtype=F32)
    sum_bias_q = jnp.concatenate([first_sums[:part], last_sums[:part]])
    sum_bias_v = jnp.concatenate([first_sums[2 * part :], last_sums[2 * part :]])

    def whole_row(value):
        return value.reshape(4, part)

    def spread(value, size):
        result = jnp.zeros((4, size), F32)
        result = lax.dynamic_update_slice(result, value[None, :size], (core, 0))
        return lax.dynamic_update_slice(result, value[None, size:], (core + 2, 0))

    terms = jnp.concatenate(
        [
            spread(sum_bias_q, part),
            spread(sum_bias_v, part),
            whole_row(sum_bias_out),
            whole_row(sum_bias_down),
            whole_row(sum_gain_attn),
            whole_row(sum_shift_attn),
            whole_row(sum_gain_mlp),
            whole_row(sum_shift_mlp),
            spread(sum_bias_up, ff_part),
        ],
        axis=1,
    )

    def shard(value, flip):
        return lax.dynamic_index_in_dim(value, here ^ flip, 0, keepdims=True)

    from_core = over_core(jnp.concatenate([shard(terms, 1), shard(terms, 3)]).astype(BF))
    near_term = shard(terms, 0)[0] + from_core[0].astype(F32)
    far_term = shard(terms, 2)[0] + from_core[1].astype(F32)
    lanes = near_term.shape[0] // (2 * part)

    def as_columns(term):
        return jnp.pad(term.reshape(lanes, 2 * part).T, ((0, 0), (0, 128 - lanes)))

    last_far = jnp.concatenate([last_far, as_columns(far_term).astype(BF)], axis=1)
    last_own = jnp.concatenate([last_own, as_columns(near_term)], axis=1)
    last_sum = SeqSum("last", meta, group_count)
    last_sum.start_x(last_far, last_own)

    def my_block(mine, other):
        aligned_here = (group_id % 2) == core
        return jnp.where(aligned_here, mine, other), jnp.where(aligned_here, other, mine)

    def listed(own, arriving):
        parts = [own[k] for k in range(4)] + [arriving[k] for k in range(4)]
        return route(parts, slot_at.astype(jnp.int32))

    first_sum.step_z1(last_sum.token)
    grad_down = stack_rows(meta, AT_Y, *down_sum.halves(first_sum.token))
    back = listed(gx_own, after(gx_arrived, grad_down))
    returned = [back[0]]

    def send_back(count, *gates):
        for _ in range(count):
            k = len(returned)
            pairs = [(i, (i + offsets[k]) % group_count) for i in range(group_count)]
            returned.append(moved("return", after(back[k], *gates), "seq", pairs))

    send_back(2, grad_down)
    last_sum.step_y(back)
    up_sum.back_y(last_sum.token)
    first_sum.step_z2(up_sum.token, returned[1])
    send_back(1, first_sum.token)
    last_sum.step_z1(first_sum.token, returned[2])
    first_sum.back_z2(last_sum.token)
    send_back(1, last_sum.token)
    last_sum.step_z2(first_sum.token, returned[3])
    first_sum.back_z1(last_sum.token)
    send_back(1, last_sum.token)
    last_sum.back_z2(first_sum.token, returned[4])
    kept, sent = my_block(*up_sum.halves(last_sum.token))
    grad_w_up = spread_columns(meta, 1, 4 * ff_part, kept, over_core(sent))
    first_sum.back_y(kept)
    send_back(1, last_sum.token)
    last_sum.back_z1(first_sum.token, returned[5])
    send_back(1, first_sum.token)
    last_sum.back_y(last_sum.token, returned[6])
    first_halves = first_sum.halves(last_sum.token)
    last_halves = last_sum.halves(returned[7])
    activations = listed(y_own, after(y_arrived, last_sum.token))
    input_grad = route(returned, given_of_slot.astype(jnp.int32))

    blocks = []
    for mine, other in (first_halves, last_halves):
        kept, sent = my_block(mine[:, : 3 * part], other[:, : 3 * part])
        blocks += [kept, over_core(sent)]
    grad_w_qkv = spread_columns(meta, 3, 3 * width, *blocks)

    def by_y(mine, other, axis):
        lower = jnp.where(group_id % 2 == 0, mine, other)
        upper = jnp.where(group_id % 2 == 0, other, mine)
        return jnp.concatenate([lower, upper], axis=axis).astype(F32)

    grad_w_out = by_y(*(half[:, 3 * part :] for half in first_halves), 1)
    sums = by_y(*(half[:, 3 * part :] for half in last_halves), 0)[:, :lanes].T.reshape(-1)

    def piece(place):
        return sums[place * part : (place + 1) * part]

    return (
        activations,
        input_grad,
        grad_w_qkv,
        grad_w_out,
        grad_w_up,
        grad_down,
        piece(0),
        piece(1),
        piece(2),
        sums[8 * part :],
        piece(3),
        piece(4),
        piece(5),
        piece(6),
        piece(7),
    )


def solution(mesh):
    rows = P("seq", "head", None)
    weight, vector = P("head", None), P("head")
    in_specs = (rows, rows, P(), P()) + (weight,) * 4 + (vector,) * 9
    out_specs = (rows, rows) + (weight,) * 4 + (vector,) * 9
    return jax.shard_map(
        on_device, mesh=mesh, in_specs=in_specs, out_specs=out_specs, check_vma=False
    )
```

```python
import functools
import itertools

import jax
import jax.numpy as jnp
import numpy as np
from jax import lax
from jax.experimental import pallas as pl
from jax.experimental.pallas import tpu as pltpu
from jax.sharding import PartitionSpec as P

HEAD_SIZE = 64
CAP = 1536
HALF = CAP // 2
STEP = 512
EPS = 1e-12
BF = jnp.bfloat16
F32 = jnp.float32
VMEM_SPEC = pl.BlockSpec(memory_space=pltpu.VMEM)
SMEM_SPEC = pl.BlockSpec(memory_space=pltpu.SMEM)
ANY_SPEC = pl.BlockSpec(memory_space=pl.ANY)
LIGHT = pl.CostEstimate(flops=0, bytes_accessed=1024, transcendentals=0)


def after(value, *others):
    return lax.optimization_barrier((value, *others))[0]


def mm(left, right):
    return jnp.dot(left, right, preferred_element_type=F32)


def mm_rows(left, right):
    return lax.dot_general(left, right, (((0,), (0,)), ((), ())), preferred_element_type=F32)


def mm_cols(left, right):
    return lax.dot_general(left, right, (((1,), (1,)), ((), ())), preferred_element_type=F32)


def _route_kernel(count, single, dst_ref, *refs):
    out_ref = refs[-1]
    for k in range(count):
        out_ref[dst_ref[k]] = refs[0][k] if single else refs[k][...]


def route(blocks, dst):
    single = not isinstance(blocks, (list, tuple))
    args = [blocks] if single else list(blocks)
    count = args[0].shape[0] if single else len(args)
    shape = args[0].shape[1:] if single else args[0].shape
    return pl.pallas_call(
        functools.partial(_route_kernel, count, single),
        out_shape=jax.ShapeDtypeStruct((count,) + shape, args[0].dtype),
        in_specs=[SMEM_SPEC] + [VMEM_SPEC] * len(args),
        out_specs=VMEM_SPEC,
        compiler_params=pltpu.CompilerParams(vmem_limit_bytes=12 << 20),
        cost_estimate=LIGHT,
        name="route",
    )(dst, *args)


def _pack_kernel(meta_ref, a0, a1, a2, a3, out_ref):
    here = meta_ref[12]
    out_ref[...] = jnp.zeros_like(out_ref)
    for slot in range(4):
        offset, length = meta_ref[slot], meta_ref[4 + slot]
        for src, flip in ((a0, 0), (a1, 2), (a2, 1), (a3, 3)):
            start = (here ^ flip) * 128
            pieces = jnp.clip((length - start + 15) // 16, 0, 8)

            @pl.loop(0, pieces)
            def _(i):
                row = pl.multiple_of(offset + start + i * 16, 16)
                out_ref[pl.ds(row, 16), :] = src[slot, pl.ds(pl.multiple_of(i * 16, 16), 16), :]


def pack(meta, own, from_x, from_core, from_both):
    return pl.pallas_call(
        _pack_kernel,
        out_shape=jax.ShapeDtypeStruct((CAP, own.shape[-1]), own.dtype),
        in_specs=[SMEM_SPEC] + [VMEM_SPEC] * 4,
        out_specs=VMEM_SPEC,
        compiler_params=pltpu.CompilerParams(vmem_limit_bytes=12 << 20),
        cost_estimate=LIGHT,
        name="pack",
    )(meta, own, from_x, from_core, from_both)


def _unpack_kernel(meta_ref, mine_ref, other_ref, own_ref, far_ref, rows_ref, sems):
    here, core = meta_ref[12], meta_ref[13]
    first = pltpu.make_async_copy(
        mine_ref, rows_ref.at[pl.ds(pl.multiple_of(core * HALF, 16), HALF)], sems.at[0]
    )
    second = pltpu.make_async_copy(
        other_ref, rows_ref.at[pl.ds(pl.multiple_of((1 - core) * HALF, 16), HALF)], sems.at[1]
    )
    first.start()
    second.start()
    first.wait()
    second.wait()
    width = rows_ref.shape[1]
    for slot in range(4):
        offset, length = meta_ref[slot], meta_ref[4 + slot]
        for dst, flip in ((own_ref, 0), (far_ref, 2)):
            start = (here ^ flip) * 128

            whole = jnp.clip((length - start) // 16, 0, 8)
            some = jnp.clip((length - start + 15) // 16, 0, 8)

            def piece(i):
                row = pl.multiple_of(jnp.minimum(offset + start + i * 16, CAP - 16), 16)
                return rows_ref[pl.ds(row, 16), :]

            def put(i, value):
                dst[slot, pl.ds(pl.multiple_of(i * 16, 16), 16), :] = value

            @pl.loop(0, whole)
            def _(i):
                put(i, piece(i))

            @pl.loop(whole, some)
            def _(i):
                keep = lax.broadcasted_iota(jnp.int32, (16, width), 0) + (start + i * 16) < length
                put(i, jnp.where(keep, piece(i).astype(F32), 0.0).astype(BF))

            @pl.loop(some, 8)
            def _(i):
                put(i, jnp.zeros((16, width), BF))


def unpack(meta, mine, other):
    width = mine.shape[1]
    shape = jax.ShapeDtypeStruct((4, 128, width), BF)
    return pl.pallas_call(
        _unpack_kernel,
        out_shape=(shape, shape),
        in_specs=[SMEM_SPEC, ANY_SPEC, ANY_SPEC],
        out_specs=(VMEM_SPEC, VMEM_SPEC),
        scratch_shapes=[pltpu.VMEM((CAP, width), BF), pltpu.SemaphoreType.DMA((2,))],
        compiler_params=pltpu.CompilerParams(vmem_limit_bytes=12 << 20),
        cost_estimate=LIGHT,
        name="unpack",
    )(meta, mine, other)


def masked(scores, key_bias):
    first = scores.shape[0] - 128
    if first == 0:
        return scores + key_bias
    return jnp.concatenate([scores[:first], scores[first:] + key_bias], axis=0)


def _attend_kernel(meta_ref, qkv_ref, ctx_ref, lse_ref):
    ctx_ref[...] = jnp.zeros_like(ctx_ref)
    width = ctx_ref.shape[1]
    part = width // 2

    def one(slot, blocks):
        span = blocks * 128
        offset = pl.multiple_of(meta_ref[slot], 16)
        length = meta_ref[4 + slot]
        rows = pl.ds(offset, span)
        key_id = lax.broadcasted_iota(jnp.int32, (128, 1), 0) + (span - 128)
        key_bias = jnp.where(key_id < length, 0.0, -1e30)

        @pl.loop(0, width // 128, unroll=2)
        def _(pair):
            lane0 = pl.multiple_of((pair // 2) * (3 * part) + (pair % 2) * 128, 128)
            keys = qkv_ref[rows, pl.ds(pl.multiple_of(part + lane0, 128), 128)]
            values = qkv_ref[rows, pl.ds(pl.multiple_of(2 * part + lane0, 128), 128)]
            values_t = values.astype(F32).T.astype(BF)
            for first in range(0, span, STEP):
                step = min(span - first, STEP)
                queries = qkv_ref[
                    pl.ds(pl.multiple_of(offset + first, 16), step), pl.ds(lane0, 128)
                ]
                queries = queries * jnp.asarray(HEAD_SIZE**-0.5, BF)
                lane = lax.broadcasted_iota(jnp.int32, (step, 128), 1)
                parts = []
                for half in range(2):
                    picked = jnp.where((lane >= 64) == (half == 1), queries, jnp.zeros_like(queries))
                    scores = mm_cols(keys, picked)
                    scores = masked(scores, key_bias)
                    highest = jnp.max(scores, axis=0, keepdims=True)
                    expo = jnp.exp(scores - highest)
                    total = jnp.sum(expo, axis=0, keepdims=True)
                    weighted = mm(values_t[64 * half : 64 * half + 64], expo.astype(BF))
                    parts.append(weighted * (1.0 / total))
                    lse_ref[slot, pair * 2 + half, :, first : first + step] = highest + jnp.log(total)
                mixed = jnp.concatenate(parts, axis=0).T
                out_lane = pl.multiple_of(pair * 128, 128)
                ctx_ref[pl.ds(pl.multiple_of(offset + first, 16), step), pl.ds(out_lane, 128)] = (
                    mixed.astype(BF)
                )

    @pl.loop(0, 4)
    def _(slot):
        for blocks in range(1, 5):
            pl.when(meta_ref[8 + slot] == blocks)(functools.partial(one, slot, blocks))


def attend(meta, qkv):
    width = qkv.shape[1] // 3
    return pl.pallas_call(
        _attend_kernel,
        out_shape=(
            jax.ShapeDtypeStruct((CAP, width), BF),
            jax.ShapeDtypeStruct((4, width // HEAD_SIZE, 1, 512), F32),
        ),
        in_specs=[SMEM_SPEC, VMEM_SPEC],
        out_specs=(VMEM_SPEC, VMEM_SPEC),
        compiler_params=pltpu.CompilerParams(vmem_limit_bytes=12 << 20),
        cost_estimate=LIGHT,
        name="attend",
    )(meta, qkv)


def _attend_back_kernel(block, meta_ref, qkv_ref, lse_ref, gctx_ref, out_ref):
    out_ref[...] = jnp.zeros_like(out_ref)
    part = out_ref.shape[1] // 3

    def one(slot, blocks):
        span = blocks * 128
        offset = pl.multiple_of(meta_ref[slot], 16)
        length = meta_ref[4 + slot]
        rows = pl.ds(offset, span)
        key_id = lax.broadcasted_iota(jnp.int32, (128, 1), 0) + (span - 128)
        key_bias = jnp.where(key_id < length, 0.0, -1e30)

        @pl.loop(0, part // 128, unroll=2)
        def _(turn):
            pair = block * (part // 128) + turn
            out_lane = pl.multiple_of(turn * 128, 128)
            base = block * 3 * part
            lane0 = pl.multiple_of(base + turn * 128, 128)
            ctx_lane = pl.multiple_of(block * part + turn * 128, 128)
            keys = qkv_ref[rows, pl.ds(pl.multiple_of(part + lane0, 128), 128)]
            values = qkv_ref[rows, pl.ds(pl.multiple_of(2 * part + lane0, 128), 128)]
            keys_t = keys.astype(F32).T.astype(BF)
            grad_keys = jnp.zeros((span, 128), F32)
            grad_values = jnp.zeros((span, 128), F32)
            for first in range(0, span, STEP):
                step = min(span - first, STEP)
                here = pl.ds(pl.multiple_of(offset + first, 16), step)
                queries = qkv_ref[here, pl.ds(lane0, 128)] * jnp.asarray(HEAD_SIZE**-0.5, BF)
                grad_ctx = gctx_ref[here, pl.ds(ctx_lane, 128)]
                lane = lax.broadcasted_iota(jnp.int32, (step, 128), 1)
                row = lax.broadcasted_iota(jnp.int32, (step, 128), 0) + first
                grad_ctx = jnp.where(row < length, grad_ctx, jnp.zeros_like(grad_ctx))
                parts = []
                for half in range(2):
                    side = (lane >= 64) == (half == 1)
                    picked = jnp.where(side, queries, jnp.zeros_like(queries))
                    picked_grad = jnp.where(side, grad_ctx, jnp.zeros_like(grad_ctx))
                    scores = mm_cols(keys, picked)
                    log_total = lse_ref[slot, pair * 2 + half, :, first : first + step]
                    scores = scores - log_total
                    scores = masked(scores, key_bias)
                    probs = jnp.exp(scores)
                    grad_values = grad_values + mm(probs.astype(BF), picked_grad)
                    grad_probs = mm_cols(values, picked_grad)
                    inner = jnp.sum(probs * grad_probs, axis=0, keepdims=True)
                    grad_scores = (probs * (grad_probs - inner)).astype(BF)
                    grad_keys = grad_keys + mm(grad_scores, picked)
                    parts.append(mm(keys_t[64 * half : 64 * half + 64], grad_scores))
                grad_queries = jnp.concatenate(parts, axis=0).T * HEAD_SIZE**-0.5
                out_ref[here, pl.ds(out_lane, 128)] = grad_queries.astype(BF)
            key_lane = pl.multiple_of(part + out_lane, 128)
            value_lane = pl.multiple_of(2 * part + out_lane, 128)
            out_ref[rows, pl.ds(key_lane, 128)] = grad_keys.astype(BF)
            out_ref[rows, pl.ds(value_lane, 128)] = grad_values.astype(BF)

    @pl.loop(0, 4)
    def _(slot):
        for blocks in range(1, 5):
            pl.when(meta_ref[8 + slot] == blocks)(functools.partial(one, slot, blocks))


def attend_back(meta, qkv, lse, grad_ctx, block):
    return pl.pallas_call(
        functools.partial(_attend_back_kernel, block),
        out_shape=jax.ShapeDtypeStruct((qkv.shape[0], qkv.shape[1] // 2), BF),
        in_specs=[SMEM_SPEC] + [VMEM_SPEC] * 3,
        out_specs=VMEM_SPEC,
        compiler_params=pltpu.CompilerParams(vmem_limit_bytes=12 << 20),
        cost_estimate=LIGHT,
        name="attend_back",
    )(meta, qkv, lse, grad_ctx)


def _assemble_kernel(kinds, meta_ref, *refs):
    out_ref = refs[-1]
    here, core = meta_ref[12], meta_ref[13]
    rows, columns = refs[0].shape
    block = columns // (4 * kinds)
    for flip, src in zip((0, 2, 1, 3), refs[:4]):
        place = pl.ds(pl.multiple_of((here ^ flip) * rows, 16), rows)
        for kind in range(kinds):
            for side in range(2):
                lane = pl.multiple_of((kind * 4 + core + 2 * side) * block, 128)
                spot = (side * kinds + kind) * block
                out_ref[place, spot : spot + block] = src[:, pl.ds(lane, block)]


def assemble(meta, kinds, own, from_x, from_core, from_both):
    rows, columns = own.shape
    return pl.pallas_call(
        functools.partial(_assemble_kernel, kinds),
        out_shape=jax.ShapeDtypeStruct((4 * rows, columns // 2), BF),
        in_specs=[SMEM_SPEC] + [VMEM_SPEC] * 4,
        out_specs=VMEM_SPEC,
        compiler_params=pltpu.CompilerParams(vmem_limit_bytes=12 << 20),
        cost_estimate=LIGHT,
        name="assemble",
    )(meta, own, from_x, from_core, from_both)


def _spread_kernel(kinds, sides, meta_ref, *refs):
    out_ref = refs[-1]
    core = meta_ref[13]
    block = out_ref.shape[1] // (4 * kinds)
    for flip in range(2):
        for kind in range(kinds):
            for side in range(2):
                lane = pl.multiple_of((kind * 4 + (core ^ flip) + 2 * side) * block, 128)
                if sides:
                    src, spot = refs[2 * side + flip], kind * block
                else:
                    src, spot = refs[flip], (side * kinds + kind) * block
                out_ref[:, pl.ds(lane, block)] = src[:, spot : spot + block].astype(F32)


def spread_columns(meta, kinds, columns, *blocks):
    return pl.pallas_call(
        functools.partial(_spread_kernel, kinds, len(blocks) == 4),
        out_shape=jax.ShapeDtypeStruct((blocks[0].shape[0], columns), F32),
        in_specs=[SMEM_SPEC] + [VMEM_SPEC] * len(blocks),
        out_specs=VMEM_SPEC,
        compiler_params=pltpu.CompilerParams(vmem_limit_bytes=12 << 20),
        cost_estimate=LIGHT,
        name="spread_columns",
    )(meta, *blocks)


def _stack_kernel(place, meta_ref, mine_ref, other_ref, out_ref):
    spot = meta_ref[place]
    rows = mine_ref.shape[0]
    mine_at = pl.multiple_of(spot * rows, 16)
    other_at = pl.multiple_of((1 - spot) * rows, 16)
    out_ref[pl.ds(mine_at, rows), :] = mine_ref[...].astype(out_ref.dtype)
    out_ref[pl.ds(other_at, rows), :] = other_ref[...].astype(out_ref.dtype)


def stack_rows(meta, place, mine, other, kind=F32):
    return pl.pallas_call(
        functools.partial(_stack_kernel, place),
        out_shape=jax.ShapeDtypeStruct((2 * mine.shape[0], mine.shape[1]), kind),
        in_specs=[SMEM_SPEC] + [VMEM_SPEC] * 2,
        out_specs=VMEM_SPEC,
        compiler_params=pltpu.CompilerParams(vmem_limit_bytes=12 << 20),
        cost_estimate=LIGHT,
        name="stack_rows",
    )(meta, mine, other)


def _merge_kernel(meta_ref, down_ref, out_weight_ref, mine_ref, other_ref, down_out, out_out):
    here_y, chip = meta_ref[14], meta_ref[18]
    size = mine_ref.shape[0] // 4
    first = 0
    for own_ref, out_ref in ((down_ref, down_out), (out_weight_ref, out_out)):
        rows, share = own_ref.shape[0], own_ref.shape[0] // 8
        out_ref[pl.ds(pl.multiple_of(chip * rows, 16), rows), :] = own_ref[...]
        for src, y in ((mine_ref, here_y), (other_ref, 1 - here_y)):
            for turn in range(4):
                at = (1 - chip) * rows + (y * 4 + turn) * share
                out_ref[pl.ds(pl.multiple_of(at, 16), share), :] = src[
                    turn * size + first : turn * size + first + share, :
                ]
        first += share


def merge_shares(meta, w_down, w_out, mine, other):
    return pl.pallas_call(
        _merge_kernel,
        out_shape=tuple(
            jax.ShapeDtypeStruct((2 * weight.shape[0], weight.shape[1]), BF)
            for weight in (w_down, w_out)
        ),
        in_specs=[SMEM_SPEC] + [VMEM_SPEC] * 4,
        out_specs=(VMEM_SPEC, VMEM_SPEC),
        compiler_params=pltpu.CompilerParams(vmem_limit_bytes=12 << 20),
        cost_estimate=LIGHT,
        name="merge_shares",
    )(meta, w_down, w_out, mine, other)


TILE = 256


def _tiles(meta_ref, count_at, out_refs, body):
    rows = out_refs[0].shape[0]
    used = jnp.minimum((meta_ref[count_at] + TILE - 1) // TILE, rows // TILE)

    @pl.loop(0, used)
    def _(tile):
        body(pl.ds(pl.multiple_of(tile * TILE, TILE), TILE))

    @pl.loop(used, rows // TILE)
    def _(tile):
        for out_ref in out_refs:
            place = pl.ds(pl.multiple_of(tile * TILE, TILE), TILE)
            out_ref[place, :] = jnp.zeros((TILE, out_ref.shape[1]), out_ref.dtype)


def _up_kernel(count_at, meta_ref, low_ref, weight_ref, bias_ref, act_ref, slope_ref):
    width = act_ref.shape[1]
    step = 512

    def body(place):
        @pl.loop(0, width // step)
        def _(turn):
            lanes = pl.ds(pl.multiple_of(turn * step, step), step)
            pre = mm(low_ref[place, :], weight_ref[:, lanes]) + bias_ref[:, lanes]
            cdf = 0.5 * (1.0 + lax.erf(pre * np.float32(0.5**0.5)))
            slope = cdf + pre * jnp.exp(-0.5 * pre * pre) * np.float32((2 * np.pi) ** -0.5)
            act_ref[place, lanes] = (pre * cdf).astype(BF)
            slope_ref[place, lanes] = slope.astype(BF)

    _tiles(meta_ref, count_at, (act_ref, slope_ref), body)


def up_product(meta, count_at, low, weight, bias):
    shape = jax.ShapeDtypeStruct((low.shape[0], weight.shape[1]), BF)
    return pl.pallas_call(
        functools.partial(_up_kernel, count_at),
        out_shape=(shape, shape),
        in_specs=[SMEM_SPEC] + [VMEM_SPEC] * 3,
        out_specs=(VMEM_SPEC, VMEM_SPEC),
        compiler_params=pltpu.CompilerParams(vmem_limit_bytes=8 << 20),
        cost_estimate=LIGHT,
        name="up_product",
    )(meta, low, weight, bias)


def _qkv_kernel(meta_ref, rows_ref, weight_ref, bias_ref, out_ref):
    step = out_ref.shape[1] // 2

    def body(place):
        for first in (0, step):
            lanes = slice(first, first + step)
            product = mm(rows_ref[place, :], weight_ref[:, lanes]) + bias_ref[:, lanes]
            out_ref[place, lanes] = product.astype(BF)

    _tiles(meta_ref, ALL, (out_ref,), body)


def qkv_product(meta, rows, weight, bias):
    return pl.pallas_call(
        _qkv_kernel,
        out_shape=jax.ShapeDtypeStruct((rows.shape[0], weight.shape[1]), BF),
        in_specs=[SMEM_SPEC] + [VMEM_SPEC] * 3,
        out_specs=VMEM_SPEC,
        compiler_params=pltpu.CompilerParams(vmem_limit_bytes=8 << 20),
        cost_estimate=LIGHT,
        name="qkv_product",
    )(meta, rows, weight, bias)


def _rows_kernel(count_at, turned, terms, scaled, meta_ref, *refs):
    lefts, rights = refs[:terms], refs[terms : 2 * terms]
    out_ref = refs[2 * terms + scaled]
    width = out_ref.shape[1]
    step = min(512, width)

    def body(place):
        @pl.loop(0, width // step)
        def _(turn):
            lanes = pl.ds(pl.multiple_of(turn * step, step), step)
            total = None
            for left_ref, right_ref in zip(lefts, rights):
                left = left_ref[place, :]
                if turned:
                    term = mm_cols(left, right_ref[lanes, :])
                else:
                    term = mm(left, right_ref[:, lanes])
                total = term if total is None else total + term
            if scaled:
                total = total * refs[2 * terms][place, lanes].astype(F32)
            out_ref[place, lanes] = total.astype(out_ref.dtype)

    _tiles(meta_ref, count_at, (out_ref,), body)


def rows_product(meta, count_at, lefts, rights, turned, kind, scale=None):
    width = rights[0].shape[0] if turned else rights[0].shape[1]
    args = [*lefts, *rights] + ([] if scale is None else [scale])
    return pl.pallas_call(
        functools.partial(_rows_kernel, count_at, turned, len(lefts), int(scale is not None)),
        out_shape=jax.ShapeDtypeStruct((lefts[0].shape[0], width), kind),
        in_specs=[SMEM_SPEC] + [VMEM_SPEC] * len(args),
        out_specs=VMEM_SPEC,
        compiler_params=pltpu.CompilerParams(vmem_limit_bytes=8 << 20),
        cost_estimate=LIGHT,
        name="rows_product",
    )(meta, *args)


def _grad_kernel(terms, meta_ref, at_ref, *refs):
    lefts, rights = refs[:terms], refs[terms : 2 * terms]
    out_ref, turned_ref = refs[2 * terms :]
    count, width = out_ref.shape
    first = 0
    for left_ref in lefts:
        rows = left_ref.shape[0]
        piece = left_ref[:, pl.ds(pl.multiple_of(at_ref[0], 128), count)]
        turned_ref[:, first : first + rows] = piece.astype(F32).T.astype(BF)
        first += rows
    step = 256

    @pl.loop(0, width // step)
    def _(turn):
        lanes = pl.ds(pl.multiple_of(turn * step, step), step)
        total, start = None, 0
        for right_ref in rights:
            rows = right_ref.shape[0]
            term = mm(turned_ref[:, start : start + rows], right_ref[:, lanes])
            total = term if total is None else total + term
            start += rows
        out_ref[:, lanes] = total.astype(out_ref.dtype)


def grad_product(meta, lefts, rights, start, count, kind):
    rows = sum(left.shape[0] for left in lefts)
    args = [*lefts, *rights]
    return pl.pallas_call(
        functools.partial(_grad_kernel, len(lefts)),
        out_shape=jax.ShapeDtypeStruct((count, rights[0].shape[1]), kind),
        in_specs=[SMEM_SPEC, SMEM_SPEC] + [VMEM_SPEC] * len(args),
        out_specs=VMEM_SPEC,
        scratch_shapes=[pltpu.VMEM((count, rows), BF)],
        compiler_params=pltpu.CompilerParams(vmem_limit_bytes=12 << 20),
        cost_estimate=LIGHT,
        name="grad_product",
    )(meta, jnp.asarray(start, jnp.int32)[None], *args)


def normed(inputs):
    average = jnp.mean(inputs, axis=-1, keepdims=True)
    centered = inputs - average
    variance = jnp.mean(centered * centered, axis=-1, keepdims=True)
    rstd = lax.rsqrt(variance + EPS)
    return centered * rstd, rstd


def norm_back(unit, rstd, grad, gain):
    scaled = grad * gain
    return (
        scaled
        - jnp.mean(scaled, axis=-1, keepdims=True)
        - unit * jnp.mean(scaled * unit, axis=-1, keepdims=True)
    ) * rstd


SWAP_X = [(i, i ^ 2) for i in range(4)]
SWAP_Y = [(i, i ^ 1) for i in range(8)]
SWAP_Z1 = [(i, i ^ 2) for i in range(8)]
SWAP_Z2 = [(i, i ^ 4) for i in range(8)]
AT_Y, AT_Z1, AT_Z2 = 14, 16, 17
MINE, OTHER, ALL = 19, 20, 21


def moved(name, value, axis, pairs):
    with jax.named_scope(name):
        return lax.ppermute(value, axis, pairs)


class SeqSum:
    def __init__(self, name, meta, group_count):
        self.name, self.meta, self.whole = name, meta, group_count == 8
        index = lax.axis_index("seq")
        self.bits = {AT_Y: index % 2, AT_Z1: index // 2 % 2, AT_Z2: index // 4 % 2}

    def send(self, step, value, axis, pairs):
        self.token = value
        self.arrived = moved(f"{self.name}_{step}", value, axis, pairs)

    def start_x(self, far, own):
        self.kept = own[None]
        self.send("x", far.astype(BF), "head", SWAP_X)

    def start_y(self, far, kept):
        self.kept = kept
        self.send("y", far.astype(BF), "seq", SWAP_Y)

    def added(self, gates):
        arrived = after(self.arrived, *gates).astype(F32)
        self.kept = self.kept + arrived.reshape(self.kept.shape)

    def split(self, step, place, pairs):
        blocks, rows, columns = self.kept.shape
        halves = self.kept.reshape(blocks, 2, rows // 2, columns)
        bit = self.bits[place]
        self.kept = lax.dynamic_index_in_dim(halves, bit, 1, keepdims=False)
        sent = lax.dynamic_index_in_dim(halves, 1 - bit, 1, keepdims=False)
        self.send(step, sent.astype(BF).reshape(-1, columns), "seq", pairs)

    def step_y(self, *gates):
        self.added(gates)
        if self.whole:
            self.split("y", AT_Y, SWAP_Y)
            return
        count = self.kept.shape[1] // 2
        halves = lax.psum(self.kept[0], "seq").astype(BF).reshape(2, count, -1)
        bit = self.bits[AT_Y]
        self.mine = self.token = lax.dynamic_index_in_dim(halves, bit, 0, keepdims=False)
        self.arrived = lax.dynamic_index_in_dim(halves, 1 - bit, 0, keepdims=False)

    def step_z1(self, *gates):
        if self.whole:
            self.added(gates)
            self.split("z1", AT_Z1, SWAP_Z1)

    def step_z2(self, *gates):
        if self.whole:
            self.added(gates)
            self.split("z2", AT_Z2, SWAP_Z2)

    def step_x(self, *gates):
        if self.whole:
            self.added(gates)
            far = self.kept[1]
            self.kept = self.kept[:1]
            self.send("x", far.astype(BF), "head", SWAP_X)

    def back_z2(self, *gates):
        if self.whole:
            self.added(gates)
            self.mine = self.kept[0].astype(BF)
            self.send("back_z2", self.mine, "seq", SWAP_Z2)

    def joined(self, place, gates):
        arrived = after(self.arrived, *gates)
        self.mine = stack_rows(self.meta, place, self.mine, arrived, BF)

    def back_z1(self, *gates):
        if self.whole:
            self.joined(AT_Z2, gates)
            self.send("back_z1", self.mine, "seq", SWAP_Z1)

    def back_y(self, *gates):
        if self.whole:
            self.joined(AT_Z1, gates)
            self.send("back_y", self.mine, "seq", SWAP_Y)

    def halves(self, *gates):
        return self.mine, after(self.arrived, *gates)


def on_device(
    tokens,
    cotangent,
    lengths,
    seq_order,
    w_qkv,
    w_out,
    w_up,
    w_down,
    bias_q,
    bias_v,
    bias_out,
    bias_up,
    bias_down,
    gain_attn,
    shift_attn,
    gain_mlp,
    shift_mlp,
):
    group_count = lax.axis_size("seq")
    group_id = lax.axis_index("seq")
    here = lax.axis_index("head").astype(jnp.int32)
    core, chip = here % 2, here // 2
    slots, span_rows, width = tokens.shape
    part = width // 4
    ff_part = w_up.shape[1] // 4
    offsets = [k * group_count // slots for k in range(slots)]
    offsets[1], offsets[-1] = 1, group_count - 1
    swap_x = [(i, i ^ 2) for i in range(4)]
    swap_core = [(i, i ^ 1) for i in range(4)]

    def over_x(value, name="x"):
        with jax.named_scope(name):
            return lax.ppermute(value, "head", swap_x)

    def over_core(value, name="core"):
        with jax.named_scope(name):
            return lax.ppermute(value, "head", swap_core)

    slot_ids = jnp.arange(slots, dtype=jnp.int32)
    local_ids = group_id * slots + slot_ids
    given_slot = lax.dynamic_slice_in_dim(seq_order, group_id * slots, slots) % slots
    given_of_slot = jnp.sum(
        jnp.where(given_slot[None, :] == slot_ids[:, None], slot_ids[None, :], 0), axis=1
    )
    matches = seq_order[None, :] == local_ids[:, None]
    slot_lens = jnp.sum(jnp.where(matches, lengths[None, :], 0), axis=1)
    aligned = (slot_lens + 15) // 16 * 16
    choices = np.zeros((35, slots), np.int32)
    for row, picks in enumerate(itertools.combinations(range(1, slots), 3)):
        choices[row, [0, *picks]] = 1
    sides = jnp.sum(choices * aligned[None, :], axis=1)
    larger = jnp.maximum(sides, jnp.sum(aligned) - sides)
    squares = jnp.sum(choices * (slot_lens * slot_lens)[None, :], axis=1)
    heavier = jnp.maximum(squares, jnp.sum(slot_lens * slot_lens) - squares)
    score = larger * 1024 + heavier // 4096
    best = jnp.min(score)
    chosen = jnp.argmax(score == best)
    in_first = jnp.sum(
        jnp.where(jnp.arange(35)[:, None] == chosen, choices, 0), axis=0, dtype=jnp.int32
    )
    is_own = jnp.where(chip == 0, in_first, 1 - in_first)
    before = np.tril(np.ones((slots, slots), np.int32), -1)
    rank_own = jnp.sum(before * is_own[None, :], axis=1)
    rank_far = jnp.sum(before * (1 - is_own)[None, :], axis=1)
    list_pos = jnp.where(is_own == 1, rank_own, 4 + rank_far).astype(jnp.int32)
    at_place = list_pos[None, :] == slot_ids[:, None]
    slot_at = jnp.sum(jnp.where(at_place, slot_ids[None, :], 0), axis=1)
    own_lens = jnp.sum(jnp.where(at_place, slot_lens[None, :], 0), axis=1)[:4]
    own_aligned = (own_lens + 15) // 16 * 16
    own_offsets = jnp.sum(np.tril(np.ones((4, 4), np.int32), -1) * own_aligned[None, :], axis=1)
    total_rows = jnp.sum(own_aligned)
    meta = jnp.concatenate(
        [
            own_offsets,
            own_lens,
            (own_lens + 127) // 128,
            here[None],
            core[None],
            (group_id % 2)[None],
            (group_id // 2)[None],
            (group_id // 2 % 2)[None],
            (group_id // 4 % 2)[None],
            chip[None],
            jnp.clip(total_rows - core * HALF, 0, HALF)[None],
            jnp.clip(total_rows - (1 - core) * HALF, 0, HALF)[None],
            total_rows[None],
            jnp.zeros((2,), jnp.int32),
        ]
    ).astype(jnp.int32)
    row_ids = core * HALF + jnp.arange(HALF, dtype=jnp.int32)
    row_keep = jnp.any(
        (row_ids[:, None] >= own_offsets[None, :])
        & (row_ids[:, None] < (own_offsets + own_lens)[None, :]),
        axis=1,
        keepdims=True,
    )

    def swapped(own, far):
        return own, far, over_core(own), over_core(far)

    if group_count == slots:
        spots = (group_id - given_slot) % slots
        sent_tokens = route(tokens, spots)
    else:
        sent_tokens = route(tokens, given_slot.astype(jnp.int32))
    small_here = jnp.concatenate(
        [
            bias_q,
            bias_v,
            bias_out,
            bias_down,
            gain_attn,
            shift_attn,
            gain_mlp,
            shift_mlp,
            bias_up,
        ]
    )[None, :]
    small_here = after(small_here, sent_tokens)
    small_core = over_core(small_here)

    def ordered(first, second, is_low):
        return jnp.concatenate(
            [jnp.where(is_low, first, second), jnp.where(is_low, second, first)], axis=0
        )

    small_pair = ordered(small_here, small_core, core == 0)
    small = ordered(small_pair, over_x(small_pair), chip == 0).astype(F32)

    def vector(place):
        return small[:, place * part : (place + 1) * part].reshape(1, width)

    def local_columns(rows):
        return jnp.concatenate(
            [
                lax.dynamic_index_in_dim(rows, core, 0, keepdims=False),
                lax.dynamic_index_in_dim(rows, core + 2, 0, keepdims=False),
            ]
        )

    query_bias = local_columns(small[:, 0:part])
    value_bias = local_columns(small[:, part : 2 * part])
    up_bias = local_columns(small[:, 8 * part :])[None, :]
    out_bias, down_bias = vector(2), vector(3)
    attn_gain, attn_shift, mlp_gain, mlp_shift = vector(4), vector(5), vector(6), vector(7)
    no_bias = jnp.zeros((part,), F32)
    joint_bias = jnp.concatenate(
        [query_bias[:part], no_bias, value_bias[:part], query_bias[part:], no_bias, value_bias[part:]]
    )[None, :]


    far_qkv = over_x(after(w_qkv, sent_tokens), "x_first_weights")
    if group_count == 8:
        turn = (group_id % 2) * 4 + group_id // 4 + 2 * (group_id // 2 % 2)
        mixed = jnp.concatenate(
            [
                lax.dynamic_slice_in_dim(
                    weight, turn * (weight.shape[0] // 8), weight.shape[0] // 8, axis=0
                )
                for weight in (w_down, w_out)
            ],
            axis=0,
        )
        mixed = over_x(after(mixed, sent_tokens), "x_shares")
    else:
        mixed = small
    if group_count == slots:
        got = lax.all_to_all(sent_tokens, "seq", split_axis=0, concat_axis=0, tiled=True)
        came = (slot_ids - group_id) % slots
        placed = jnp.sum(
            jnp.where(came[:, None] == slot_ids[None, :], list_pos[None, :], 0), axis=1
        )
        lists = route(got, placed.astype(jnp.int32))
    else:
        arrived = [sent_tokens[0]]
        for k in range(1, slots):
            arrived.append(
                lax.ppermute(
                    sent_tokens[k],
                    "seq",
                    [(i, (i - offsets[k]) % group_count) for i in range(group_count)],
                )
            )
        lists = route(arrived, list_pos)

    def by_chip(own, far):
        return jnp.concatenate(
            [jnp.where(chip == 0, own, far), jnp.where(chip == 0, far, own)], axis=0
        )

    full_qkv = assemble(meta, 3, *swapped(w_qkv, far_qkv))

    cot_lists = route(cotangent, list_pos)
    far_tokens = over_x(lists[4:], "x_tokens")
    if group_count == 8:
        mixed = after(mixed, lists)
        pair = stack_rows(meta, AT_Z2, mixed, moved("share_z2", mixed, "seq", SWAP_Z2), BF)
        gate = pair
        four = stack_rows(meta, AT_Z1, pair, moved("share_z1", pair, "seq", SWAP_Z1), BF)
    else:
        gate = far_tokens
    here_blocks = swapped(lists[:4], after(far_tokens, gate, cot_lists))
    if group_count == 8:
        here_blocks = (*here_blocks[:3], after(here_blocks[3], four))
    rows_in = pack(meta, *here_blocks)
    w_up_later, _ = lax.optimization_barrier((w_up, far_tokens))
    far_up = over_x(w_up_later, "x_up_weight")
    if group_count == 8:
        other_four = moved("share_y", four, "seq", SWAP_Y)
    else:
        full_down, full_out = by_chip(w_down, over_x(w_down)), by_chip(w_out, over_x(w_out))

    def halves(value):
        return (
            lax.dynamic_slice_in_dim(value, core * HALF, HALF, axis=0),
            lax.dynamic_slice_in_dim(value, (1 - core) * HALF, HALF, axis=0),
        )

    def in_order(mine, other):
        lower = jnp.where(core == 0, mine, other)
        upper = jnp.where(core == 0, other, mine)
        return jnp.concatenate([lower, upper], axis=0)

    def core_sum(lefts_mine, lefts_other, rights, turned):
        arriving = over_core(rows_product(meta, OTHER, lefts_other, rights, turned, BF))
        return rows_product(meta, MINE, lefts_mine, rights, turned, F32) + arriving.astype(F32)

    qkv = qkv_product(meta, rows_in, full_qkv, joint_bias)
    context, lse = attend(meta, qkv)
    if group_count == 8:
        context, other_four = lax.optimization_barrier((context, other_four))
        full_down, full_out = merge_shares(meta, w_down, w_out, four, other_four)
    cot_far_in = after(cot_lists[4:], far_up)
    full_up = assemble(meta, 1, *swapped(w_up, far_up))
    cot_arrived = over_x(cot_far_in, "x_cotangent")
    ctx_mine, ctx_other = halves(context)
    rows_mine, _ = halves(rows_in)
    resid_attn = (
        core_sum([ctx_mine], [ctx_other], [full_out], False) + rows_mine.astype(F32) + out_bias
    )
    unit_attn, rstd_attn = normed(resid_attn)
    hidden = unit_attn * attn_gain + attn_shift
    low_mine = hidden.astype(BF)
    low_other = over_core(low_mine)

    act_mine, slope_mine = up_product(meta, MINE, low_mine, full_up, up_bias)
    act_other, slope_other = up_product(meta, OTHER, low_other, full_up, up_bias)
    cot_rows = pack(meta, *swapped(cot_lists[:4], after(cot_arrived, act_mine)))
    resid_mlp = core_sum([act_mine], [act_other], [full_down], False) + hidden + down_bias
    unit_mlp, rstd_mlp = normed(resid_mlp)
    final_mine = (unit_mlp * mlp_gain + mlp_shift).astype(BF)

    cot_mine, _ = halves(cot_rows)
    grad_y = jnp.where(row_keep, cot_mine.astype(F32), 0.0)
    grad_mlp2 = norm_back(unit_mlp, rstd_mlp, grad_y, mlp_gain)
    sum_gain_mlp = jnp.sum(grad_y * unit_mlp, axis=0)
    sum_shift_mlp = jnp.sum(grad_y, axis=0)
    branch_mine = grad_mlp2.astype(BF)
    branch_other = over_core(branch_mine)
    sum_bias_down = jnp.sum(branch_mine, axis=0, dtype=F32)
    def grads(lefts, rights, start, count, kind=F32):
        return grad_product(meta, lefts, rights, start, count, kind)

    down_sum = SeqSum("down", meta, group_count)
    acts, branches = [act_mine, act_other], [branch_mine, branch_other]
    if group_count == 8:
        here_y = group_id % 2
        count = ff_part // 2

        def down_term(half, kind):
            return jnp.stack(
                [
                    grads(acts, branches, side * ff_part + half * count, count, kind)
                    for side in (chip, 1 - chip)
                ]
            )

        down_sum.start_y(down_term(1 - here_y, BF).reshape(-1, width), down_term(here_y, F32))
    else:
        down_sum.start_x(
            *(grads(acts, branches, side * ff_part, ff_part) for side in (1 - chip, chip))
        )
    branch_mine, branch_other, _ = lax.optimization_barrier(
        (branch_mine, branch_other, down_sum.token)
    )
    pre_mine = rows_product(meta, MINE, [branch_mine], [full_down], True, BF, slope_mine)
    pre_other = rows_product(meta, OTHER, [branch_other], [full_down], True, BF, slope_other)
    sum_bias_up = jnp.sum(pre_mine, axis=0, dtype=F32) + jnp.sum(pre_other, axis=0, dtype=F32)

    lows, pres = [low_mine, low_other], [pre_mine, pre_other]
    up_far, up_own = (
        grads(lows, pres, side * 2 * part, 2 * part, kind)
        for side, kind in ((1 - chip, BF), (chip, F32))
    )
    up_sum = SeqSum("up", meta, group_count)
    up_sum.start_x(up_far, up_own)
    pre_mine, pre_other, _ = lax.optimization_barrier((pre_mine, pre_other, up_sum.token))
    gh_other = rows_product(meta, OTHER, [pre_other], [full_up], True, BF)
    gh_arrived = over_core(gh_other)
    if group_count == 8:
        down_sum.step_z1(gh_other)
    else:
        down_sum.step_y(gh_other)
    pre_mine = after(pre_mine, down_sum.token)
    grad_hidden = rows_product(meta, MINE, [pre_mine], [full_up], True, F32)
    grad_hidden = grad_hidden + gh_arrived.astype(F32) + grad_mlp2

    grad_attn2 = norm_back(unit_attn, rstd_attn, grad_hidden, attn_gain)
    sum_gain_attn = jnp.sum(grad_hidden * unit_attn, axis=0)
    sum_shift_attn = jnp.sum(grad_hidden, axis=0)
    attn_mine = grad_attn2.astype(BF)
    attn_other = over_core(attn_mine)
    sum_bias_out = jnp.sum(attn_mine, axis=0, dtype=F32)
    half_width = width // 2

    def out_term(side, kind):
        term = grads([ctx_mine, ctx_other], [attn_mine, attn_other], side * part, part, kind)
        return jnp.concatenate([term[:, :half_width], term[:, half_width:]], axis=0)

    out_far, out_own = out_term(1 - chip, BF), out_term(chip, F32)
    down_sum.step_z2(out_own, out_far)
    up_sum.step_y(down_sum.token)
    attn_mine, attn_other, _ = lax.optimization_barrier((attn_mine, attn_other, up_sum.token))
    grad_ctx = in_order(
        rows_product(meta, MINE, [attn_mine], [full_out], True, BF),
        rows_product(meta, OTHER, [attn_other], [full_out], True, BF),
    )
    y_own, y_far = unpack(meta, final_mine, over_core(after(final_mine, gh_other)))
    y_arrived = over_x(y_far, "x_activations")
    grad_first = attend_back(meta, qkv, lse, after(grad_ctx, y_far), 0)
    down_sum.step_x(grad_first)
    up_sum.step_z1(down_sum.token)
    grad_first = after(grad_first, up_sum.token)

    first_far, first_own = (
        jnp.concatenate(
            [grads([rows_in], [grad_first], side * 2 * part, 2 * part, out.dtype), out], axis=1
        )
        for side, out in ((1 - chip, out_far), (chip, out_own))
    )
    first_sum = SeqSum("first", meta, group_count)
    first_sum.start_x(first_far, first_own)
    down_sum.back_z2(first_sum.token, first_own)
    grad_last = attend_back(meta, qkv, lse, after(grad_ctx, down_sum.token), 1)
    grad_last = after(grad_last, y_arrived)
    down_sum.back_z1(grad_last)
    up_sum.step_z2(down_sum.token)
    grad_last = after(grad_last, up_sum.token)

    qkv_blocks = [full_qkv[:, : 3 * part], full_qkv[:, 3 * part :]]
    first_mine, first_other = halves(grad_first)
    last_mine, last_other = halves(grad_last)
    gx_other = rows_product(meta, OTHER, [first_other, last_other], qkv_blocks, True, BF)
    gx_arrived = over_core(gx_other)
    gx_mine = rows_product(meta, MINE, [first_mine, last_mine], qkv_blocks, True, F32)
    gx_mine = (gx_mine + gx_arrived.astype(F32) + grad_attn2).astype(BF)
    gx_other = over_core(gx_mine)
    first_sum.step_y(gx_mine)
    down_sum.back_y(first_sum.token)
    up_sum.back_z2(down_sum.token)
    gx_mine = after(gx_mine, up_sum.token)
    gx_own, gx_far = unpack(meta, gx_mine, gx_other)
    gx_arrived = over_x(gx_far, "x_grad")
    up_sum.back_z1(gx_far)
    grad_last = after(grad_last, up_sum.token)
    last_far, last_own = (
        grads([rows_in], [grad_last], side * 2 * part, 2 * part, kind)
        for side, kind in ((1 - chip, BF), (chip, F32))
    )
    first_sums = jnp.sum(grad_first, axis=0, dtype=F32)
    last_sums = jnp.sum(grad_last, axis=0, dtype=F32)
    sum_bias_q = jnp.concatenate([first_sums[:part], last_sums[:part]])
    sum_bias_v = jnp.concatenate([first_sums[2 * part :], last_sums[2 * part :]])

    def whole_row(value):
        return value.reshape(4, part)

    def spread(value, size):
        result = jnp.zeros((4, size), F32)
        result = lax.dynamic_update_slice(result, value[None, :size], (core, 0))
        return lax.dynamic_update_slice(result, value[None, size:], (core + 2, 0))

    terms = jnp.concatenate(
        [
            spread(sum_bias_q, part),
            spread(sum_bias_v, part),
            whole_row(sum_bias_out),
            whole_row(sum_bias_down),
            whole_row(sum_gain_attn),
            whole_row(sum_shift_attn),
            whole_row(sum_gain_mlp),
            whole_row(sum_shift_mlp),
            spread(sum_bias_up, ff_part),
        ],
        axis=1,
    )

    def shard(value, flip):
        return lax.dynamic_index_in_dim(value, here ^ flip, 0, keepdims=True)

    from_core = over_core(jnp.concatenate([shard(terms, 1), shard(terms, 3)]).astype(BF))
    near_term = shard(terms, 0)[0] + from_core[0].astype(F32)
    far_term = shard(terms, 2)[0] + from_core[1].astype(F32)
    lanes = near_term.shape[0] // (2 * part)

    def as_columns(term):
        return jnp.pad(term.reshape(lanes, 2 * part).T, ((0, 0), (0, 128 - lanes)))

    last_far = jnp.concatenate([last_far, as_columns(far_term).astype(BF)], axis=1)
    last_own = jnp.concatenate([last_own, as_columns(near_term)], axis=1)
    last_sum = SeqSum("last", meta, group_count)
    last_sum.start_x(last_far, last_own)

    def my_block(mine, other):
        aligned_here = (group_id % 2) == core
        return jnp.where(aligned_here, mine, other), jnp.where(aligned_here, other, mine)

    def listed(own, arriving):
        parts = [own[k] for k in range(4)] + [arriving[k] for k in range(4)]
        return route(parts, slot_at.astype(jnp.int32))

    first_sum.step_z1(last_sum.token)
    grad_down = stack_rows(meta, AT_Y, *down_sum.halves(first_sum.token))
    back = listed(gx_own, after(gx_arrived, grad_down))
    returned = [back[0]]

    def send_back(count, *gates):
        for _ in range(count):
            k = len(returned)
            pairs = [(i, (i + offsets[k]) % group_count) for i in range(group_count)]
            returned.append(moved("return", after(back[k], *gates), "seq", pairs))

    send_back(2, grad_down)
    last_sum.step_y(back)
    up_sum.back_y(last_sum.token)
    first_sum.step_z2(up_sum.token, returned[1])
    send_back(1, first_sum.token)
    last_sum.step_z1(first_sum.token, returned[2])
    first_sum.back_z2(last_sum.token)
    send_back(1, last_sum.token)
    last_sum.step_z2(first_sum.token, returned[3])
    first_sum.back_z1(last_sum.token)
    send_back(1, last_sum.token)
    last_sum.back_z2(first_sum.token, returned[4])
    kept, sent = my_block(*up_sum.halves(last_sum.token))
    grad_w_up = spread_columns(meta, 1, 4 * ff_part, kept, over_core(sent))
    first_sum.back_y(kept)
    send_back(1, last_sum.token)
    last_sum.back_z1(first_sum.token, returned[5])
    send_back(1, first_sum.token)
    last_sum.back_y(last_sum.token, returned[6])
    first_halves = first_sum.halves(last_sum.token)
    last_halves = last_sum.halves(returned[7])
    activations = listed(y_own, after(y_arrived, last_sum.token))
    input_grad = route(returned, given_of_slot.astype(jnp.int32))

    blocks = []
    for mine, other in (first_halves, last_halves):
        kept, sent = my_block(mine[:, : 3 * part], other[:, : 3 * part])
        blocks += [kept, over_core(sent)]
    grad_w_qkv = spread_columns(meta, 3, 3 * width, *blocks)

    def by_y(mine, other, axis):
        lower = jnp.where(group_id % 2 == 0, mine, other)
        upper = jnp.where(group_id % 2 == 0, other, mine)
        return jnp.concatenate([lower, upper], axis=axis).astype(F32)

    grad_w_out = by_y(*(half[:, 3 * part :] for half in first_halves), 1)
    sums = by_y(*(half[:, 3 * part :] for half in last_halves), 0)[:, :lanes].T.reshape(-1)

    def piece(place):
        return sums[place * part : (place + 1) * part]

    return (
        activations,
        input_grad,
        grad_w_qkv,
        grad_w_out,
        grad_w_up,
        grad_down,
        piece(0),
        piece(1),
        piece(2),
        sums[8 * part :],
        piece(3),
        piece(4),
        piece(5),
        piece(6),
        piece(7),
    )


def solution(mesh):
    rows = P("seq", "head", None)
    weight, vector = P("head", None), P("head")
    in_specs = (rows, rows, P(), P()) + (weight,) * 4 + (vector,) * 9
    out_specs = (rows, rows) + (weight,) * 4 + (vector,) * 9
    return jax.shard_map(
        on_device, mesh=mesh, in_specs=in_specs, out_specs=out_specs, check_vma=False
    )
```
